32 devices in a mesh: branch: 2 (over x), head: 4 (over y, core), tokens: 4 (over z).
Axes of the slice: x: 2, y: 2, z: 4, core: 2. Of those that a mesh axis runs over, the one named last changes fastest.
Arguments:
- queries: bfloat16 [2, 4608, 1536], P('branch', 'tokens', 'head'), may hold values from -128 to 128
- keys: bfloat16 [2, 4608, 1536], P('branch', 'tokens', 'head'), may hold values from -4 to 4
- values: bfloat16 [2, 4608, 1536], P('branch', 'tokens', 'head'), may hold values from -96 to 96
- residual: bfloat16 [2, 4608, 2, 1536], P('branch', 'tokens', None, 'head'), may hold values from -3 to 3
- gate: bfloat16 [2, 2, 1536], replicated, may hold values from 0.099609375 to 1.8984375
- out_weight: bfloat16 [1536, 3072], P('head'), may hold values from -0.15625 to 0.15625
- time_offsets: int32 [3, 4], replicated, may hold values from 0 to 1
- guidance_index: int32 [18], replicated, may hold values from 0 to 7
Outputs:
- guided: bfloat16 [4608, 3072], P('tokens', ('branch', 'head'))
The draws below stay inside these ranges and needn't reach their ends.
All inputs are finite; a program needn't handle non-finite values.
Results may differ from the reference program's by a relative error of at most 0.0051.
Values may be sent and summed in bfloat16 or wider, within the bound.
No kernel may reach another device: no remote copies, remote signals or barrier semaphores. Data moves between devices by JAX's collectives and lax.ppermute only.
A program may use at most 128 MiB of HBM per device.

```python
import math
import jax
import jax.numpy as jnp
from jax import lax

D = 3072
HEADS = 12
HD = 128
ATT = 1536
TH = 8
TW = 8
TILES_T = 3
TILE = 384
TILES_W = 4
FRAMES = 18
TOKENS = 4608


def shared_keys(key):
    base_keys = jax.random.normal(key, (2, TOKENS, ATT), jnp.float32)
    return jnp.clip(base_keys, -4.0, 4.0)


def draw_keys(key, part):
    base_keys = shared_keys(key)
    return base_keys.astype(jnp.bfloat16)


def draw_queries(key, part):
    key = jax.random.fold_in(key, 2)
    fresh_rows = jnp.clip(jax.random.normal(key, (2, TOKENS, ATT), jnp.float32), -4.0, 4.0)
    return fresh_rows.astype(jnp.bfloat16)


def touch_ends(array, key, low, high):
    longest = array.shape.index(max(array.shape))
    spots = []
    for shift in (0, 1):
        where = [jax.random.randint(jax.random.fold_in(key, axis), (), 0, length) for axis, length in enumerate(array.shape)]
        where[longest] = (where[longest] + shift) % array.shape[longest]
        spots.append(tuple(where))
    return array.at[spots[0]].set(low).at[spots[1]].set(high)


def block_scale(key, dims, split, low, largest):
    level = 1.0
    for dim, parts in split:
        heights = jax.random.uniform(jax.random.fold_in(jax.random.fold_in(key, 6), dim), (parts,), jnp.float32, low / len(split), largest / len(split))
        level = level * jnp.repeat(jnp.exp(heights), dims[dim] // parts).reshape((-1,) + (1,) * (len(dims) - 1 - dim))
    return level


def bell_draw(rng, extent, spread, most, split=(), held_as=jnp.bfloat16):
    array = spread * jax.random.normal(rng, extent, jnp.float32)
    if split:
        array = array * block_scale(rng, extent, split, -0.22, 0.18)
    return jnp.clip(array, -most, most).astype(held_as)


def setup_inputs(seed: int = 0) -> dict:
    splits = jax.random.split(jax.random.key(seed), 9)
    queries = draw_queries(jax.random.fold_in(splits[8], 71), 0)
    keys = draw_keys(jax.random.fold_in(splits[8], 71), 0)
    values = bell_draw(splits[2], (2, TOKENS, ATT), 16.0, 96.0, ((0, 2), (1, 4), (2, 4)))
    residual = bell_draw(splits[3], (2, TOKENS, 2, D // 2), 0.5, 3.0, ((0, 2), (1, 4), (3, 4)))
    gate = jnp.clip(1.0 + 0.18 * jax.random.normal(splits[4], (2, 2, D // 2), jnp.float32), 0.099609375, 1.8984375).astype(jnp.bfloat16)
    out_weight = bell_draw(splits[5], (ATT, D), ATT ** -0.5, 0.15625, ((0, 4),))
    time_offsets = touch_ends(jax.random.randint(splits[6], (TILES_T, TILES_W), 0, 2), jax.random.fold_in(splits[6], 1), 0, 1).astype(jnp.int32)
    guidance_index = touch_ends(jax.random.randint(splits[7], (FRAMES,), 0, 8), jax.random.fold_in(splits[7], 1), 0, 7).astype(jnp.int32)
    return dict(queries=queries, keys=keys, values=values, residual=residual, gate=gate, out_weight=out_weight, time_offsets=time_offsets, guidance_index=guidance_index)


def reference(queries, keys, values, residual, gate, out_weight, time_offsets, guidance_index):
    tile_shape = (2, TILES_W, TILES_T, TILE, HEADS, HD)
    query_tiles = queries.reshape(tile_shape)
    key_tiles = keys.reshape(tile_shape)
    value_tiles = values.reshape(tile_shape)
    tile_count = TILES_W * TILES_T
    score_scale = 1.0 / math.sqrt(HD)
    near_steps = jnp.arange(3, dtype=jnp.int32) - 1
    time_range = jnp.arange(TILES_T, dtype=jnp.int32)

    def one_tile(tile_index):
        branch = tile_index // tile_count
        tile_rest = tile_index % tile_count
        width_tile = tile_rest // TILES_T
        time_tile = tile_rest % TILES_T
        query_tile = query_tiles[branch, width_tile, time_tile].astype(jnp.float32)
        width_near = width_tile + near_steps
        width_safe = jnp.clip(width_near, 0, TILES_W - 1).astype(jnp.int32)
        key_block = jnp.take(key_tiles[branch], width_safe, axis=0)
        value_block = jnp.take(value_tiles[branch], width_safe, axis=0)
        offset = time_offsets[time_tile, width_tile]
        time_ok = (time_range >= time_tile - offset) & (time_range <= time_tile - offset + 1)
        width_ok = (width_near >= 0) & (width_near < TILES_W)
        allowed = width_ok[:, None, None] & time_ok[None, :, None]
        allowed = jnp.broadcast_to(allowed, (3, TILES_T, TILE)).reshape(-1)
        key_flat = key_block.reshape(-1, HEADS, HD).astype(jnp.float32)
        value_flat = value_block.reshape(-1, HEADS, HD).astype(jnp.float32)
        scores = jnp.einsum('qhd,khd->hqk', query_tile, key_flat) * score_scale
        masked = jnp.where(allowed[None, None, :], scores, -1e+30)
        row_max = lax.optimization_barrier(jnp.max(masked, axis=2, keepdims=True))
        weights = jnp.where(allowed[None, None, :], jnp.exp(masked - row_max), 0.0)
        norm_total = lax.optimization_barrier(jnp.sum(weights, axis=2, keepdims=True))
        rounded = lax.optimization_barrier(weights.astype(jnp.bfloat16)).astype(jnp.float32)
        blended = jnp.einsum('hqk,khd->qhd', rounded, value_flat)
        return (blended / jnp.transpose(norm_total, (1, 0, 2))).reshape(TILE, ATT).astype(jnp.bfloat16)
    attention = lax.map(one_tile, jnp.arange(2 * tile_count, dtype=jnp.int32)).reshape(2, TOKENS, ATT)
    projected = jnp.stack([jnp.dot(attention[0], out_weight, preferred_element_type=jnp.float32), jnp.dot(attention[1], out_weight, preferred_element_type=jnp.float32)])
    residual_flat = residual.reshape(2, TOKENS, D).astype(jnp.float32)
    gate_flat = gate.reshape(2, D).astype(jnp.float32)
    hidden = residual_flat + gate_flat[:, None, :] * projected
    guide_scale = 1.0 + 0.5 * guidance_index.astype(jnp.float32)
    token_scale = jnp.broadcast_to(guide_scale.reshape(1, FRAMES, 1), (TILES_W, FRAMES, TH * TW)).reshape(TOKENS)
    guided = hidden[1] + token_scale[:, None] * (hidden[0] - hidden[1])
    return guided.astype(jnp.bfloat16)
```

```python
import functools
import math

import jax
import jax.numpy as jnp
from jax import lax
from jax.experimental import pallas as pl
from jax.experimental.pallas import tpu as pltpu
from jax.sharding import PartitionSpec as P

HD = 128
FRAME = 64
FAR = 1e30
EXP2_SCALE = math.log2(math.e) / math.sqrt(HD)
VMEM_LIMIT = 40 * 1024 * 1024


def attention_kernel(info_ref, q_ref, k_ref, v_ref, low_ref, high_ref, out_ref):
    tiles_time = pl.num_programs(0)
    tile = q_ref.shape[0]
    time_tile = pl.program_id(0)
    first = time_tile - info_ref[time_tile]
    query = q_ref[...]
    ones = jnp.ones((tile, HD), jnp.bfloat16)
    sides = (
        (lambda rows: k_ref[rows, :], lambda rows: v_ref[rows, :], None),
        (lambda rows: low_ref[0, rows, :], lambda rows: low_ref[1, rows, :], info_ref[tiles_time]),
        (lambda rows: high_ref[0, rows, :], lambda rows: high_ref[1, rows, :], info_ref[tiles_time + 1]),
    )
    blocks = []
    row_max = None
    for step in range(2):
        key_tile = first + step
        inside = (key_tile >= 0) & (key_tile < tiles_time)
        start = jnp.clip(key_tile, 0, tiles_time - 1) * tile
        rows = pl.ds(pl.multiple_of(start, tile), tile)
        for keys_of, values_of, width_ok in sides:
            allowed = inside if width_ok is None else inside & (width_ok == 1)
            scores = lax.dot_general(
                query, keys_of(rows), (((1,), (1,)), ((), ())), preferred_element_type=jnp.float32
            )
            block_max = jnp.where(allowed, jnp.max(scores, axis=1, keepdims=True), -FAR)
            row_max = block_max if row_max is None else jnp.maximum(row_max, block_max)
            blocks.append((scores, values_of, rows, allowed))
    shift = row_max * EXP2_SCALE
    total = jnp.zeros((tile, 2 * HD), jnp.float32)
    for scores, values_of, rows, allowed in blocks:
        weights = jnp.exp2(scores * EXP2_SCALE - jnp.where(allowed, shift, FAR))
        total += jnp.dot(
            weights.astype(jnp.bfloat16),
            jnp.concatenate([values_of(rows), ones], axis=1),
            preferred_element_type=jnp.float32,
        )
    out_ref[...] = (total[:, :HD] / total[:, HD:]).astype(jnp.bfloat16)


def attention(info, queries, keys, values, low, high, head, tile):
    count = queries.shape[0]
    side = pl.BlockSpec((2, count, HD), lambda t, info: (0, 0, 0))
    whole = pl.BlockSpec((count, HD), lambda t, info: (0, head))
    pairs = count * 6 * tile
    return pl.pallas_call(
        attention_kernel,
        out_shape=jax.ShapeDtypeStruct((count, HD), jnp.bfloat16),
        grid_spec=pltpu.PrefetchScalarGridSpec(
            num_scalar_prefetch=1,
            grid=(count // tile,),
            in_specs=[pl.BlockSpec((tile, HD), lambda t, info: (t, head)), whole, whole, side, side],
            out_specs=pl.BlockSpec((tile, HD), lambda t, info: (t, 0)),
        ),
        compiler_params=pltpu.CompilerParams(vmem_limit_bytes=VMEM_LIMIT),
        cost_estimate=pl.CostEstimate(
            flops=4 * pairs * HD, bytes_accessed=8 * count * HD * 2, transcendentals=pairs
        ),
        name="attention",
    )(info, queries, keys, values, low, high)


def projection_kernel(head_count, info_ref, *refs):
    *pieces, w_ref, gate_ref, mine_ref, other_ref, out_ref = refs
    tile = out_ref.shape[0]
    frames = tile // FRAME
    time_tile = pl.program_id(0)
    branch = info_ref[0]
    weights = w_ref[...].reshape(-1, w_ref.shape[-1])
    hidden = []
    for which in range(2):
        rows = jnp.concatenate(
            [piece[which * head_count + h] for h in range(head_count) for piece in pieces], axis=1
        )
        projected = jnp.dot(rows, weights, preferred_element_type=jnp.float32)
        gate = jnp.where(branch == 0, gate_ref[which, 0:1, :], gate_ref[which, 1:2, :])
        base = jnp.where(branch == which, mine_ref[...], other_ref[...])
        hidden.append(base.astype(jnp.float32) + gate.astype(jnp.float32) * projected)
    for frame in range(frames):
        rows = slice(frame * FRAME, (frame + 1) * FRAME)
        step = info_ref[1 + time_tile * frames + frame].astype(jnp.float32)
        guide = 1.0 + 0.5 * step
        cond, uncond = hidden[0][rows], hidden[1][rows]
        out_ref[rows, :] = (uncond + guide * (cond - uncond)).astype(jnp.bfloat16)


def project(info, pieces, weights, gate, mine, other, tile, head_count):
    count, width = mine.shape
    rows = pl.BlockSpec((tile, width), lambda t, info: (t, 0))
    piece = pl.BlockSpec((2 * head_count, tile, HD), lambda t, info: (0, t, 0))
    return pl.pallas_call(
        functools.partial(projection_kernel, head_count),
        out_shape=jax.ShapeDtypeStruct((count, width), jnp.bfloat16),
        grid_spec=pltpu.PrefetchScalarGridSpec(
            num_scalar_prefetch=1,
            grid=(count // tile,),
            in_specs=[piece] * len(pieces)
            + [
                pl.BlockSpec(weights.shape, lambda t, info: (0, 0, 0)),
                pl.BlockSpec(gate.shape, lambda t, info: (0, 0, 0)),
                rows,
                rows,
            ],
            out_specs=rows,
        ),
        compiler_params=pltpu.CompilerParams(vmem_limit_bytes=VMEM_LIMIT),
        cost_estimate=pl.CostEstimate(
            flops=4 * count * width * len(pieces) * head_count * HD,
            bytes_accessed=2 * count * (3 * width + 2 * len(pieces) * head_count * HD),
            transcendentals=0,
        ),
        name="projection",
    )(info, *pieces, weights, gate, mine, other)


def local(queries, keys, values, residual, gate, out_weight, time_offsets, guidance_index):
    tiles_time, tiles_wide = time_offsets.shape
    count, features = queries.shape[1:]
    tile = count // tiles_time
    heads = features // HD
    head_count = lax.axis_size("head")
    columns = lax.axis_size("tokens")
    branch_pos = lax.axis_index("branch")
    head_pos = lax.axis_index("head")
    width_pos = lax.axis_index("tokens")
    width = gate.shape[2] // head_count

    up = [(i, i + 1) for i in range(columns - 1)]
    down = [(i + 1, i) for i in range(columns - 1)]
    swap = [(0, 1), (1, 0)]

    low, high = [], []
    for head in range(heads):
        cols = slice(head * HD, (head + 1) * HD)
        key_value = jnp.stack([keys[0, :, cols], values[0, :, cols]])
        low.append(lax.ppermute(key_value, "tokens", up))
        high.append(lax.ppermute(key_value, "tokens", down))

    half = lax.dynamic_index_in_dim(residual[0], branch_pos, 1, keepdims=False)
    other_half = lax.dynamic_index_in_dim(residual[0], 1 - branch_pos, 1, keepdims=False)
    partner_half = lax.ppermute(other_half, "branch", swap)
    gate_block = lax.dynamic_slice_in_dim(gate, head_pos * width, width, 2)

    branch_weight = lax.dynamic_slice_in_dim(out_weight, branch_pos * gate.shape[2], gate.shape[2], 1)
    branch_weight = branch_weight.reshape(features, head_count, width).transpose(1, 0, 2)
    weights = lax.all_to_all(branch_weight, "head", 0, 0)

    offsets = lax.dynamic_index_in_dim(time_offsets, width_pos, 1, keepdims=False)
    edges = jnp.stack([width_pos > 0, width_pos < tiles_wide - 1]).astype(jnp.int32)
    attention_info = jnp.concatenate([offsets, edges])
    projection_info = jnp.concatenate([branch_pos[None].astype(jnp.int32), guidance_index])

    pieces = []
    for head in range(heads):
        own = attention(
            attention_info, queries[0], keys[0], values[0], low[head], high[head], head, tile
        )
        pieces.append(lax.all_gather(own, ("branch", "head")))
    return project(
        projection_info, pieces, weights, gate_block, half, partner_half, tile, head_count
    )


def solution(mesh):
    return jax.shard_map(
        local,
        mesh=mesh,
        in_specs=(
            P("branch", "tokens", "head"),
            P("branch", "tokens", "head"),
            P("branch", "tokens", "head"),
            P("branch", "tokens", None, "head"),
            P(),
            P("head", None),
            P(),
            P(),
        ),
        out_specs=P("tokens", ("branch", "head")),
        check_vma=False,
    )
```

```python
import functools
import math

import jax
import jax.numpy as jnp
from jax import lax
from jax.experimental import pallas as pl
from jax.experimental.pallas import tpu as pltpu
from jax.sharding import PartitionSpec as P

HD = 128
FRAME = 64
FAR = 1e30
EXP2_SCALE = math.log2(math.e) / math.sqrt(HD)
VMEM_LIMIT = 40 * 1024 * 1024


def attention_kernel(info_ref, q_ref, k_ref, v_ref, low_ref, high_ref, out_ref):
    tiles_time = pl.num_programs(0)
    tile = q_ref.shape[0]
    first = pl.program_id(0) - info_ref[pl.program_id(0)]
    base = jnp.clip(first, 0, tiles_time - 2)
    rows = pl.ds(pl.multiple_of(base * tile, tile), 2 * tile)
    inside = [(base + step >= first) & (base + step <= first + 1) for step in range(2)]
    query = q_ref[...]
    sides = (
        (k_ref[rows, :], v_ref[rows, :], None),
        (low_ref[0, rows, :], low_ref[1, rows, :], info_ref[tiles_time] == 1),
        (high_ref[0, rows, :], high_ref[1, rows, :], info_ref[tiles_time + 1] == 1),
    )
    blocks = []
    row_max = None
    for keys, _, width_ok in sides:
        scores = lax.dot_general(
            query, keys, (((1,), (1,)), ((), ())), preferred_element_type=jnp.float32
        )
        for step in range(2):
            allowed = inside[step] if width_ok is None else inside[step] & width_ok
            block = scores[:, step * tile : (step + 1) * tile]
            block_max = jnp.where(allowed, jnp.max(block, axis=1, keepdims=True), -FAR)
            row_max = block_max if row_max is None else jnp.maximum(row_max, block_max)
            blocks.append((block, allowed))
    shift = row_max * EXP2_SCALE
    weights = [
        jnp.exp2(block * EXP2_SCALE - jnp.where(allowed, shift, FAR)).astype(jnp.bfloat16)
        for block, allowed in blocks
    ]
    values = jnp.concatenate([side[1] for side in sides], axis=0)
    total = jnp.dot(
        jnp.concatenate(weights, axis=1),
        jnp.concatenate([values, jnp.ones_like(values)], axis=1),
        preferred_element_type=jnp.float32,
    )
    out_ref[...] = (total[:, :HD] / total[:, HD:]).astype(jnp.bfloat16)


def attention(info, queries, keys, values, low, high, head, tile):
    count = queries.shape[0]
    side = pl.BlockSpec((2, count, HD), lambda t, info: (0, 0, 0))
    whole = pl.BlockSpec((count, HD), lambda t, info: (0, head))
    pairs = count * 6 * tile
    return pl.pallas_call(
        attention_kernel,
        out_shape=jax.ShapeDtypeStruct((count, HD), jnp.bfloat16),
        grid_spec=pltpu.PrefetchScalarGridSpec(
            num_scalar_prefetch=1,
            grid=(count // tile,),
            in_specs=[pl.BlockSpec((tile, HD), lambda t, info: (t, head)), whole, whole, side, side],
            out_specs=pl.BlockSpec((tile, HD), lambda t, info: (t, 0)),
        ),
        compiler_params=pltpu.CompilerParams(vmem_limit_bytes=VMEM_LIMIT),
        cost_estimate=pl.CostEstimate(
            flops=4 * pairs * HD, bytes_accessed=8 * count * HD * 2, transcendentals=pairs
        ),
        name="attention",
    )(info, queries, keys, values, low, high)


def projection_kernel(info_ref, *refs):
    *pieces, gate_ref, mine_ref, other_ref, out_ref = refs
    weight_count = info_weights(pieces)
    weight_refs, pieces = pieces[:weight_count], pieces[weight_count:]
    tile = out_ref.shape[0]
    frames = tile // FRAME
    time_tile = pl.program_id(0)
    own_first = info_ref[0] == 0
    weights = jnp.concatenate([ref[...] for ref in weight_refs], axis=0)
    half = len(pieces) // 2
    hidden = []
    for which, base_ref in enumerate((mine_ref, other_ref)):
        rows = jnp.concatenate(
            [piece[...] for piece in pieces[which * half : (which + 1) * half]], axis=1
        )
        projected = jnp.dot(rows, weights, preferred_element_type=jnp.float32)
        hidden.append(base_ref[...].astype(jnp.float32) + gate_ref[which] * projected)
    for frame in range(frames):
        rows = slice(frame * FRAME, (frame + 1) * FRAME)
        step = info_ref[1 + time_tile * frames + frame].astype(jnp.float32)
        guide = 1.0 + 0.5 * step
        cond = jnp.where(own_first, hidden[0][rows], hidden[1][rows])
        uncond = jnp.where(own_first, hidden[1][rows], hidden[0][rows])
        out_ref[rows, :] = (uncond + guide * (cond - uncond)).astype(jnp.bfloat16)


def info_weights(operands):
    return 4


def project(info, weights, pieces, gate, mine, other, tile):
    count, width = mine.shape
    rows = pl.BlockSpec((tile, width), lambda t, info: (t, 0))
    piece = pl.BlockSpec((tile, HD), lambda t, info: (t, 0))
    return pl.pallas_call(
        projection_kernel,
        out_shape=jax.ShapeDtypeStruct((count, width), jnp.bfloat16),
        grid_spec=pltpu.PrefetchScalarGridSpec(
            num_scalar_prefetch=1,
            grid=(count // tile,),
            in_specs=[pl.BlockSpec(w.shape, lambda t, info: (0, 0)) for w in weights]
            + [piece] * len(pieces)
            + [pl.BlockSpec(gate.shape, lambda t, info: (0, 0, 0)), rows, rows],
            out_specs=rows,
        ),
        compiler_params=pltpu.CompilerParams(vmem_limit_bytes=VMEM_LIMIT),
        cost_estimate=pl.CostEstimate(
            flops=2 * count * width * len(pieces) * HD,
            bytes_accessed=2 * count * (3 * width + len(pieces) * HD),
            transcendentals=0,
        ),
        name="projection",
    )(info, *weights, *pieces, gate, mine, other)


def pack_kernel(k_ref, v_ref, *out_refs):
    for head, out_ref in enumerate(out_refs):
        cols = slice(head * HD, (head + 1) * HD)
        out_ref[0] = k_ref[:, cols]
        out_ref[1] = v_ref[:, cols]


def pack_heads(keys, values, tile):
    count, features = keys.shape
    heads = features // HD
    rows = pl.BlockSpec((tile, features), lambda t: (t, 0))
    return pl.pallas_call(
        pack_kernel,
        out_shape=[jax.ShapeDtypeStruct((2, count, HD), jnp.bfloat16)] * heads,
        grid=(count // tile,),
        in_specs=[rows, rows],
        out_specs=[pl.BlockSpec((2, tile, HD), lambda t: (0, t, 0))] * heads,
        cost_estimate=pl.CostEstimate(
            flops=0, bytes_accessed=8 * count * features, transcendentals=0
        ),
        name="pack_heads",
    )(keys, values)


def split_kernel(info_ref, w_ref, *out_refs):
    for index, out_ref in enumerate(out_refs):

        @pl.when(pl.program_id(0) == index)
        def _():
            out_ref[...] = w_ref[...]


def split_weight(info, weight, width, head_count):
    rows = weight.shape[0]
    return pl.pallas_call(
        split_kernel,
        out_shape=[jax.ShapeDtypeStruct((rows, width), jnp.bfloat16)] * head_count,
        grid_spec=pltpu.PrefetchScalarGridSpec(
            num_scalar_prefetch=1,
            grid=(head_count,),
            in_specs=[pl.BlockSpec((rows, width), lambda i, info: (0, info[i]))],
            out_specs=[pl.BlockSpec((rows, width), lambda i, info: (0, 0))] * head_count,
        ),
        cost_estimate=pl.CostEstimate(
            flops=0, bytes_accessed=4 * rows * width * head_count, transcendentals=0
        ),
        name="split_weight",
    )(info, weight)


def local(queries, keys, values, residual, gate, out_weight, time_offsets, guidance_index):
    tiles_time, tiles_wide = time_offsets.shape
    count, features = queries.shape[1:]
    tile = count // tiles_time
    heads = features // HD
    head_count = lax.axis_size("head")
    columns = lax.axis_size("tokens")
    branch_pos = lax.axis_index("branch")
    head_pos = lax.axis_index("head")
    width_pos = lax.axis_index("tokens")
    width = gate.shape[2] // head_count

    up = [(i, i + 1) for i in range(columns - 1)]
    down = [(i + 1, i) for i in range(columns - 1)]

    def swap(value, branch_bit, head_bits):
        if not head_bits:
            return lax.ppermute(value, "branch", [(0, 1), (1, 0)])
        if not branch_bit:
            return lax.ppermute(value, "head", [(i, i ^ head_bits) for i in range(head_count)])
        flip = head_count + head_bits
        return lax.ppermute(
            value, ("branch", "head"), [(i, i ^ flip) for i in range(2 * head_count)]
        )

    packed = pack_heads(keys[0], values[0], tile)
    packed, residual, out_weight = lax.optimization_barrier((packed, residual, out_weight))
    low, high = [], []
    for key_value in packed:
        low.append(lax.ppermute(key_value, "tokens", up))
        high.append(lax.ppermute(key_value, "tokens", down))

    first_half, second_half = residual[0, :, 0], residual[0, :, 1]
    mine = jnp.where(branch_pos == 0, first_half, second_half)
    other = swap(jnp.where(branch_pos == 0, second_half, first_half), 1, 0)
    gate_block = lax.dynamic_slice(
        gate, (0, branch_pos, head_pos * width), (2, 1, width)
    ).astype(jnp.float32)
    gate_block = jnp.where(branch_pos == 0, gate_block, gate_block[::-1])

    distances = jnp.arange(head_count, dtype=jnp.int32)
    blocks = split_weight(
        branch_pos * head_count + (head_pos ^ distances), out_weight, width, head_count
    )
    weights = [blocks[0]] + [swap(blocks[bits], 0, bits) for bits in range(1, head_count)]

    offsets = lax.dynamic_index_in_dim(time_offsets, width_pos, 1, keepdims=False)
    edges = jnp.stack([width_pos > 0, width_pos < tiles_wide - 1]).astype(jnp.int32)
    attention_info = jnp.concatenate([offsets, edges])
    projection_info = jnp.concatenate([branch_pos[None].astype(jnp.int32), guidance_index])

    pieces = {}
    for head in range(heads):
        own = attention(
            attention_info, queries[0], keys[0], values[0], low[head], high[head], head, tile
        )
        pieces[0, 0, head] = own
        pieces[1, 0, head] = swap(own, 1, 0)
        pieces[0, 2, head] = swap(own, 0, 2)
        pieces[1, 2, head] = swap(own, 1, 2)
        for branch_bit in range(2):
            for bits in (0, 2):
                pieces[branch_bit, bits + 1, head] = swap(pieces[branch_bit, bits, head], 0, 1)
    ordered = [
        pieces[branch_bit, bits, head]
        for branch_bit in range(2)
        for bits in range(head_count)
        for head in range(heads)
    ]
    return project(projection_info, weights, ordered, gate_block, mine, other, tile)


def solution(mesh):
    return jax.shard_map(
        local,
        mesh=mesh,
        in_specs=(
            P("branch", "tokens", "head"),
            P("branch", "tokens", "head"),
            P("branch", "tokens", "head"),
            P("branch", "tokens", None, "head"),
            P(),
            P("head", None),
            P(),
            P(),
        ),
        out_specs=P("tokens", ("branch", "head")),
        check_vma=False,
    )
```

```python
import functools
import math

import jax
import jax.numpy as jnp
from jax import lax
from jax.experimental import pallas as pl
from jax.experimental.pallas import tpu as pltpu
from jax.sharding import PartitionSpec as P

HD = 128
FRAME = 64
FAR = 1e30
EXP2_SCALE = math.log2(math.e) / math.sqrt(HD)
VMEM_LIMIT = 24 * 1024 * 1024


def attention_kernel(info_ref, q_ref, k_ref, v_ref, low_ref, high_ref, out_ref):
    tiles_time = info_ref.shape[0] - 2
    tile = q_ref.shape[0] // tiles_time
    width_oks = (None, info_ref[tiles_time] == 1, info_ref[tiles_time + 1] == 1)

    def window(t):
        first = t - info_ref[t]
        base = jnp.clip(first, 0, tiles_time - 2)
        inside = [(base + step >= first) & (base + step <= first + 1) for step in range(2)]
        return pl.ds(pl.multiple_of(base * tile, tile), 2 * tile), inside

    def score(t):
        rows, inside = window(t)
        query = q_ref[t * tile : (t + 1) * tile, :]
        blocks = []
        row_max = None
        for keys, width_ok in zip(
            (k_ref[rows, :], low_ref[0, rows, :], high_ref[0, rows, :]), width_oks
        ):
            scores = lax.dot_general(
                query, keys, (((1,), (1,)), ((), ())), preferred_element_type=jnp.float32
            )
            for step in range(2):
                allowed = inside[step] if width_ok is None else inside[step] & width_ok
                block = scores[:, step * tile : (step + 1) * tile]
                lanes = block[:, :HD]
                for first in range(HD, tile, HD):
                    lanes = jnp.maximum(lanes, block[:, first : first + HD])
                lanes = jnp.where(allowed, lanes, -FAR)
                row_max = lanes if row_max is None else jnp.maximum(row_max, lanes)
                blocks.append((block, allowed))
        return blocks, jnp.max(row_max, axis=1, keepdims=True) * EXP2_SCALE

    def blend(t, blocks, shift):
        rows, _ = window(t)
        weights = [
            jnp.exp2(block * EXP2_SCALE - jnp.where(allowed, shift, FAR)).astype(jnp.bfloat16)
            for block, allowed in blocks
        ]
        values = jnp.concatenate([v_ref[rows, :], low_ref[1, rows, :], high_ref[1, rows, :]], axis=0)
        total = jnp.dot(
            jnp.concatenate(weights, axis=1),
            jnp.concatenate([values, jnp.ones_like(values)], axis=1),
            preferred_element_type=jnp.float32,
        )
        out_ref[t * tile : (t + 1) * tile, :] = (total[:, :HD] / total[:, HD:]).astype(jnp.bfloat16)

    ready = score(0)
    for t in range(tiles_time):
        later = score(t + 1) if t + 1 < tiles_time else None
        blend(t, *ready)
        ready = later


def attention(info, queries, keys, values, low, high, head, tile):
    count = queries.shape[0]
    side = pl.BlockSpec((2, count, HD), lambda i, info: (0, 0, 0))
    whole = pl.BlockSpec((count, HD), lambda i, info: (0, head))
    pairs = count * 6 * tile
    return pl.pallas_call(
        attention_kernel,
        out_shape=jax.ShapeDtypeStruct((count, HD), jnp.bfloat16),
        grid_spec=pltpu.PrefetchScalarGridSpec(
            num_scalar_prefetch=1,
            grid=(1,),
            in_specs=[whole, whole, whole, side, side],
            out_specs=pl.BlockSpec((count, HD), lambda i, info: (0, 0)),
        ),
        compiler_params=pltpu.CompilerParams(vmem_limit_bytes=VMEM_LIMIT),
        cost_estimate=pl.CostEstimate(
            flops=4 * pairs * HD, bytes_accessed=8 * count * HD * 2, transcendentals=pairs
        ),
        name="attention",
    )(info, queries, keys, values, low, high)


def partial_kernel(first, own_cols, info_ref, *refs):
    near_ref, far_ref, *pieces, gate_ref, base_own_ref, base_other_ref, own_ref, other_ref = refs
    tile = own_ref.shape[0]
    frames = tile // FRAME
    time_tile = pl.program_id(0)
    cond_first = info_ref[0] == 0
    weights = jnp.concatenate([near_ref[...], far_ref[...]], axis=0)
    half = len(pieces) // 2
    parts = []
    for which in range(2):
        rows = jnp.concatenate(
            [piece[...] for piece in pieces[which * half : (which + 1) * half]], axis=1
        )
        projected = jnp.dot(rows, weights, preferred_element_type=jnp.float32)
        parts.append(gate_ref[which] * projected)
    for frame in range(frames):
        rows = slice(frame * FRAME, (frame + 1) * FRAME)
        guide = 1.0 + 0.5 * info_ref[1 + time_tile * frames + frame].astype(jnp.float32)
        scales = (jnp.where(cond_first, guide, 1.0 - guide), jnp.where(cond_first, 1.0 - guide, guide))
        total = scales[0] * parts[0][rows] + scales[1] * parts[1][rows]
        own, other = total[:, :own_cols], total[:, own_cols:]
        if first:
            own += scales[0] * base_own_ref[rows, :].astype(jnp.float32)
            own += scales[1] * base_other_ref[rows, :].astype(jnp.float32)
        else:
            own += base_own_ref[rows, :]
            other += base_other_ref[rows, :]
        own_ref[rows, :] = own
        other_ref[rows, :] = other.astype(other_ref.dtype)


def partial_projection(info, weights, pieces, gate, base, tile, group):
    count, width = base[0].shape
    first = group.start == 0
    depth = len(group) * HD
    weight = pl.BlockSpec((depth, 2 * width), lambda t, info: (group.start // len(group), 0))
    rows = pl.BlockSpec((tile, width), lambda t, info: (t, 0))
    piece = pl.BlockSpec((tile, HD), lambda t, info: (t, 0))
    return pl.pallas_call(
        functools.partial(partial_kernel, first, width),
        out_shape=[
            jax.ShapeDtypeStruct((count, width), jnp.float32),
            jax.ShapeDtypeStruct((count, width), jnp.float32 if first else jnp.bfloat16),
        ],
        grid_spec=pltpu.PrefetchScalarGridSpec(
            num_scalar_prefetch=1,
            grid=(count // tile,),
            in_specs=[weight] * 2
            + [piece] * len(pieces)
            + [pl.BlockSpec(gate.shape, lambda t, info: (0, 0, 0)), rows, rows],
            out_specs=[rows, rows],
        ),
        compiler_params=pltpu.CompilerParams(vmem_limit_bytes=VMEM_LIMIT),
        cost_estimate=pl.CostEstimate(
            flops=4 * count * width * len(pieces) * HD,
            bytes_accessed=2 * count * (6 * width + len(pieces) * HD),
            transcendentals=0,
        ),
        name="partial_projection",
    )(info, *weights, *pieces, gate, *base)


def pack_kernel(k_ref, v_ref, *out_refs):
    for head, out_ref in enumerate(out_refs):
        cols = slice(head * HD, (head + 1) * HD)
        out_ref[0] = k_ref[:, cols]
        out_ref[1] = v_ref[:, cols]


def pack_heads(keys, values, first, heads, tile):
    count = keys.shape[0]
    rows = pl.BlockSpec((tile, heads * HD), lambda t: (t, first // heads))
    return pl.pallas_call(
        pack_kernel,
        out_shape=[jax.ShapeDtypeStruct((2, count, HD), jnp.bfloat16)] * heads,
        grid=(count // tile,),
        in_specs=[rows, rows],
        out_specs=[pl.BlockSpec((2, tile, HD), lambda t: (0, t, 0))] * heads,
        cost_estimate=pl.CostEstimate(
            flops=0, bytes_accessed=8 * count * heads * HD, transcendentals=0
        ),
        name="pack_heads",
    )(keys, values)


def split_kernel(info_ref, w_ref, near_ref, far_ref):
    cols = near_ref.shape[1]
    for index, out_ref in enumerate((near_ref, far_ref)):
        for side in range(2):

            @pl.when(pl.program_id(0) == 2 * index + side)
            def _():
                out_ref[:, side * (cols // 2) : (side + 1) * (cols // 2)] = w_ref[...]


def split_weight(info, weight, width):
    rows = weight.shape[0]
    whole = pl.BlockSpec((rows, 2 * width), lambda i, info: (0, 0))
    return pl.pallas_call(
        split_kernel,
        out_shape=[jax.ShapeDtypeStruct((rows, 2 * width), jnp.bfloat16)] * 2,
        grid_spec=pltpu.PrefetchScalarGridSpec(
            num_scalar_prefetch=1,
            grid=(4,),
            in_specs=[pl.BlockSpec((rows, width), lambda i, info: (0, info[i]))],
            out_specs=[whole, whole],
        ),
        cost_estimate=pl.CostEstimate(
            flops=0, bytes_accessed=16 * rows * width, transcendentals=0
        ),
        name="split_weight",
    )(info, weight)


def local(queries, keys, values, residual, gate, out_weight, time_offsets, guidance_index):
    tiles_time, tiles_wide = time_offsets.shape
    count, features = queries.shape[1:]
    tile = count // tiles_time
    heads = features // HD
    head_count = lax.axis_size("head")
    columns = lax.axis_size("tokens")
    branch_pos = lax.axis_index("branch")
    head_pos = lax.axis_index("head")
    width_pos = lax.axis_index("tokens")
    width = gate.shape[2] // head_count

    up = [(i, i + 1) for i in range(columns - 1)]
    down = [(i + 1, i) for i in range(columns - 1)]

    def swap(value, branch_bit, head_bits):
        if not branch_bit and not head_bits:
            return value
        if not head_bits:
            return lax.ppermute(value, "branch", [(0, 1), (1, 0)])
        if not branch_bit:
            return lax.ppermute(value, "head", [(i, i ^ head_bits) for i in range(head_count)])
        flip = head_count + head_bits
        return lax.ppermute(
            value, ("branch", "head"), [(i, i ^ flip) for i in range(2 * head_count)]
        )

    packed = pack_heads(keys[0], values[0], 0, 1, tile)
    (packed, late_keys, late_values, residual, out_weight) = lax.optimization_barrier(
        (packed, keys[0], values[0], residual, out_weight)
    )
    for head in range(1, heads):
        packed += pack_heads(late_keys, late_values, head, 1, tile)
    low = [lax.ppermute(key_value, "tokens", up) for key_value in packed]
    high = [lax.ppermute(key_value, "tokens", down) for key_value in packed]

    first_half, second_half = residual[0, :, 0], residual[0, :, 1]
    mine = jnp.where(branch_pos == 0, first_half, second_half)
    other = swap(jnp.where(branch_pos == 0, second_half, first_half), 1, 0)
    gate_block = jnp.concatenate(
        [
            lax.dynamic_slice(gate, (0, branch_pos, place * width), (2, 1, width))
            for place in (head_pos, head_pos ^ 1)
        ],
        axis=2,
    ).astype(jnp.float32)
    gate_block = jnp.where(branch_pos == 0, gate_block, gate_block[::-1])

    distances = jnp.arange(4, dtype=jnp.int32)
    near, far = split_weight(
        branch_pos * head_count + (head_pos ^ distances), out_weight, width
    )
    far = swap(far, 0, 2)

    offsets = lax.dynamic_index_in_dim(time_offsets, width_pos, 1, keepdims=False)
    edges = jnp.stack([width_pos > 0, width_pos < tiles_wide - 1]).astype(jnp.int32)
    attention_info = jnp.concatenate([offsets, edges])
    projection_info = jnp.concatenate([branch_pos[None].astype(jnp.int32), guidance_index])

    pieces = {}
    head_queries = queries[0]
    for head in range(heads):
        if head == 1:
            head_queries, other = lax.optimization_barrier((head_queries, other))
        own = attention(
            attention_info, head_queries, keys[0], values[0], low[head], high[head], head, tile
        )
        for branch_bit in range(2):
            for bits in (0, 2):
                pieces[branch_bit, bits, head] = swap(own, branch_bit, bits)

    base = (mine, other)
    for group in (range(heads - 1), range(heads - 1, heads)):
        ordered = [pieces[bit, bits, head] for bit in range(2) for bits in (0, 2) for head in group]
        base = partial_projection(
            projection_info, (near, far), ordered, gate_block, base, tile, group
        )
    return (base[0] + swap(base[1], 0, 1).astype(jnp.float32)).astype(jnp.bfloat16)


def solution(mesh):
    return jax.shard_map(
        local,
        mesh=mesh,
        in_specs=(
            P("branch", "tokens", "head"),
            P("branch", "tokens", "head"),
            P("branch", "tokens", "head"),
            P("branch", "tokens", None, "head"),
            P(),
            P("head", None),
            P(),
            P(),
        ),
        out_specs=P("tokens", ("branch", "head")),
        check_vma=False,
    )
```

```python
import functools
import math

import jax
import jax.numpy as jnp
from jax import lax
from jax.experimental import pallas as pl
from jax.experimental.pallas import tpu as pltpu
from jax.sharding import PartitionSpec as P

HD = 128
FRAME = 64
FAR = 1e30
EXP2_SCALE = math.log2(math.e) / math.sqrt(HD)
VMEM_LIMIT = 24 * 1024 * 1024
COPY_PARTS = 3


def attention_kernel(info_ref, q_ref, k_ref, v_ref, side_a_ref, side_b_ref, out_ref):
    tiles_time = info_ref.shape[0] - 2
    tile = q_ref.shape[0] // tiles_time
    width_oks = (None, info_ref[tiles_time] == 1, info_ref[tiles_time + 1] == 1)

    def window(t):
        first = t - info_ref[t]
        base = jnp.clip(first, 0, tiles_time - 2)
        inside = [(base + step >= first) & (base + step <= first + 1) for step in range(2)]
        return pl.ds(pl.multiple_of(base * tile, tile), 2 * tile), inside

    def score(t):
        rows, inside = window(t)
        query = q_ref[t * tile : (t + 1) * tile, :]
        blocks = []
        row_max = None
        for keys, width_ok in zip(
            (k_ref[rows, :], side_a_ref[0, rows, :], side_b_ref[0, rows, :]), width_oks
        ):
            scores = lax.dot_general(
                query, keys, (((1,), (1,)), ((), ())), preferred_element_type=jnp.float32
            )
            for step in range(2):
                allowed = inside[step] if width_ok is None else inside[step] & width_ok
                block = scores[:, step * tile : (step + 1) * tile]
                lanes = block[:, :HD]
                for first in range(HD, tile, HD):
                    lanes = jnp.maximum(lanes, block[:, first : first + HD])
                lanes = jnp.where(allowed, lanes, -FAR)
                row_max = lanes if row_max is None else jnp.maximum(row_max, lanes)
                blocks.append((block, allowed))
        return blocks, jnp.max(row_max, axis=1, keepdims=True) * EXP2_SCALE

    def blend(t, blocks, shift):
        rows, _ = window(t)
        weights = [
            jnp.exp2(block * EXP2_SCALE - jnp.where(allowed, shift, FAR)).astype(jnp.bfloat16)
            for block, allowed in blocks
        ]
        values = jnp.concatenate([v_ref[rows, :], side_a_ref[1, rows, :], side_b_ref[1, rows, :]], axis=0)
        total = jnp.dot(
            jnp.concatenate(weights, axis=1),
            jnp.concatenate([values, jnp.ones_like(values)], axis=1),
            preferred_element_type=jnp.float32,
        )
        out_ref[t * tile : (t + 1) * tile, :] = (total[:, :HD] / total[:, HD:]).astype(jnp.bfloat16)

    ready = score(0)
    for t in range(tiles_time):
        later = score(t + 1) if t + 1 < tiles_time else None
        blend(t, *ready)
        ready = later


def attention(info, queries, keys, values, side_a, side_b, head, tile):
    count = queries.shape[0]
    side = pl.BlockSpec((2, count, HD), lambda i, info: (0, 0, 0))
    whole = pl.BlockSpec((count, HD), lambda i, info: (0, head))
    pairs = count * 6 * tile
    return pl.pallas_call(
        attention_kernel,
        out_shape=jax.ShapeDtypeStruct((count, HD), jnp.bfloat16),
        grid_spec=pltpu.PrefetchScalarGridSpec(
            num_scalar_prefetch=1,
            grid=(1,),
            in_specs=[whole, whole, whole, side, side],
            out_specs=pl.BlockSpec((count, HD), lambda i, info: (0, 0)),
        ),
        compiler_params=pltpu.CompilerParams(vmem_limit_bytes=VMEM_LIMIT),
        cost_estimate=pl.CostEstimate(
            flops=4 * pairs * HD, bytes_accessed=8 * count * HD * 2, transcendentals=pairs
        ),
        name="attention",
    )(info, queries, keys, values, side_a, side_b)


def partial_kernel(first, own_cols, info_ref, *refs):
    w_refs, refs = refs[:4], refs[4:]
    *pieces, gate_ref, base_own_ref, base_other_ref, own_ref, other_ref = refs
    tile = own_ref.shape[0]
    frames = tile // FRAME
    time_tile = pl.program_id(0)
    cond_first = info_ref[0] == 0
    weights = jnp.concatenate(
        [jnp.concatenate([w[...] for w in w_refs[i : i + 2]], axis=1) for i in (0, 2)], axis=0
    )
    half = len(pieces) // 2
    parts = []
    for which in range(2):
        rows = jnp.concatenate(
            [piece[...] for piece in pieces[which * half : (which + 1) * half]], axis=1
        )
        projected = jnp.dot(rows, weights, preferred_element_type=jnp.float32)
        parts.append(gate_ref[which] * projected)
    for frame in range(frames):
        rows = slice(frame * FRAME, (frame + 1) * FRAME)
        guide = 1.0 + 0.5 * info_ref[5 + time_tile * frames + frame].astype(jnp.float32)
        scales = (jnp.where(cond_first, guide, 1.0 - guide), jnp.where(cond_first, 1.0 - guide, guide))
        total = scales[0] * parts[0][rows] + scales[1] * parts[1][rows]
        own, other = total[:, :own_cols], total[:, own_cols:]
        if first:
            own += scales[0] * base_own_ref[rows, :].astype(jnp.float32)
            own += scales[1] * base_other_ref[rows, :].astype(jnp.float32)
        else:
            own += base_own_ref[rows, :]
            other += base_other_ref[rows, :]
        own_ref[rows, :] = own
        other_ref[rows, :] = other.astype(other_ref.dtype)


def partial_projection(info, weights, pieces, gate, base, tile, group):
    count, width = base[0].shape
    first = group.start == 0
    depth = len(group) * HD
    weight_specs = [
        pl.BlockSpec((depth, width), lambda t, info, place=place: (group.start // len(group), info[place]))
        for place in range(1, 5)
    ]
    rows = pl.BlockSpec((tile, width), lambda t, info: (t, 0))
    piece = pl.BlockSpec((tile, HD), lambda t, info: (t, 0))
    return pl.pallas_call(
        functools.partial(partial_kernel, first, width),
        out_shape=[
            jax.ShapeDtypeStruct((count, width), jnp.float32),
            jax.ShapeDtypeStruct((count, width), jnp.float32 if first else jnp.bfloat16),
        ],
        grid_spec=pltpu.PrefetchScalarGridSpec(
            num_scalar_prefetch=1,
            grid=(count // tile,),
            in_specs=weight_specs
            + [piece] * len(pieces)
            + [pl.BlockSpec(gate.shape, lambda t, info: (0, 0, 0)), rows, rows],
            out_specs=[rows, rows],
        ),
        compiler_params=pltpu.CompilerParams(vmem_limit_bytes=VMEM_LIMIT),
        cost_estimate=pl.CostEstimate(
            flops=4 * count * width * len(pieces) * HD,
            bytes_accessed=2 * count * (6 * width + len(pieces) * HD),
            transcendentals=0,
        ),
        name="partial_projection",
    )(info, *[w for w in weights for _ in range(2)], *pieces, gate, *base)


def copy_kernel(plan, info_ref, *refs):
    *arrays, sems = refs
    copies = []
    for source, cols, width, target, place in plan:
        src, dst = arrays[source], arrays[target]
        first = cols if cols is not None else pl.multiple_of(info_ref[0] * width, width)
        for part in range(COPY_PARTS):
            size = src.shape[0] // COPY_PARTS
            rows = pl.ds(part * size, size)
            to = dst.at[rows, :] if place is None else dst.at[place, rows, :]
            copies.append((src.at[rows, pl.ds(first, width)], to))
    copies = [
        pltpu.make_async_copy(src, to, sems.at[index]) for index, (src, to) in enumerate(copies)
    ]
    for copy in copies:
        copy.start()
    for copy in copies:
        copy.wait()


def copy_columns(info, sources, plan, targets):
    moved = sum(2 * 2 * sources[source].shape[0] * width for source, _, width, _, _ in plan)
    return pl.pallas_call(
        functools.partial(copy_kernel, plan),
        out_shape=[jax.ShapeDtypeStruct(shape, jnp.bfloat16) for shape in targets],
        grid_spec=pltpu.PrefetchScalarGridSpec(
            num_scalar_prefetch=1,
            grid=(1,),
            in_specs=[pl.BlockSpec(memory_space=pl.ANY)] * len(sources),
            out_specs=[pl.BlockSpec(memory_space=pl.ANY)] * len(targets),
            scratch_shapes=[pltpu.SemaphoreType.DMA((COPY_PARTS * len(plan),))],
        ),
        cost_estimate=pl.CostEstimate(flops=0, bytes_accessed=moved, transcendentals=0),
        name="copy_columns",
    )(info, *sources)


def local(queries, keys, values, residual, gate, out_weight, time_offsets, guidance_index):
    tiles_time, tiles_wide = time_offsets.shape
    count, features = queries.shape[1:]
    tile = count // tiles_time
    heads = features // HD
    head_count = lax.axis_size("head")
    columns = lax.axis_size("tokens")
    branch_pos = lax.axis_index("branch")
    head_pos = lax.axis_index("head")
    width_pos = lax.axis_index("tokens")
    width = gate.shape[2] // head_count

    rounds = [
        [pair for i in range(first, columns - 1, 2) for pair in ((i, i + 1), (i + 1, i))]
        for first in range(2)
    ]
    near_pos = (width_pos ^ 1, ((width_pos + 1) ^ 1) - 1)

    def swap(value, branch_bit, head_bits):
        if not branch_bit and not head_bits:
            return value
        if not head_bits:
            return lax.ppermute(value, "branch", [(0, 1), (1, 0)])
        if not branch_bit:
            return lax.ppermute(value, "head", [(i, i ^ head_bits) for i in range(head_count)])
        flip = head_count + head_bits
        return lax.ppermute(
            value, ("branch", "head"), [(i, i ^ flip) for i in range(2 * head_count)]
        )

    branch_pair = branch_pos * (head_count // 2)
    copy_info = jnp.stack([branch_pair + ((head_pos ^ 2) >> 1)])
    key_value = (2, count, HD)
    packed = copy_columns(
        copy_info, (keys[0], values[0]), ((0, 0, HD, 2, 0), (1, 0, HD, 2, 1)), (key_value,)
    )
    (packed, late_keys, late_values, late_weight) = lax.optimization_barrier(
        (packed, keys[0], values[0], out_weight)
    )
    *late, far = copy_columns(
        copy_info,
        (late_keys, late_values, late_weight),
        [(array, head * HD, HD, 2 + head, array) for head in range(1, heads) for array in range(2)]
        + [(2, None, 2 * width, 2 + heads, None)],
        [key_value] * (heads - 1) + [(features, 2 * width)],
    )
    late, far, residual = lax.optimization_barrier((late, far, residual))
    packed = list(packed) + late

    def halo(part):
        return [lax.ppermute(part, "tokens", pairs) for pairs in rounds]

    sides = [halo(part) for part in packed[:2]]
    far = swap(far, 0, 2)

    first_half, second_half = residual[0, :, 0], residual[0, :, 1]
    mine = jnp.where(branch_pos == 0, first_half, second_half)
    other = swap(jnp.where(branch_pos == 0, second_half, first_half), 1, 0)
    gate_block = jnp.concatenate(
        [
            lax.dynamic_slice(gate, (0, branch_pos, place * width), (2, 1, width))
            for place in (head_pos, head_pos ^ 1)
        ],
        axis=2,
    ).astype(jnp.float32)
    gate_block = jnp.where(branch_pos == 0, gate_block, gate_block[::-1])

    offsets = lax.dynamic_index_in_dim(time_offsets, width_pos, 1, keepdims=False)
    edges = jnp.stack([(pos >= 0) & (pos < tiles_wide) for pos in near_pos]).astype(jnp.int32)
    attention_info = jnp.concatenate([offsets, edges])
    places = [branch_pos * head_count + head_pos, branch_pos * head_count + (head_pos ^ 1)]
    places += [head_pos & 1, (head_pos & 1) ^ 1]
    projection_info = jnp.concatenate([jnp.stack([branch_pos] + places), guidance_index])

    pieces = {}
    head_queries = queries[0]
    for head in range(heads):
        if head == 1:
            head_queries, other = lax.optimization_barrier((head_queries, other))
        if head == 2:
            head_queries, far, pieces[1, 0, 0], pieces[1, 0, 1] = lax.optimization_barrier(
                (head_queries, far, pieces[1, 0, 0], pieces[1, 0, 1])
            )
            pieces[1, 2, 0] = swap(pieces[1, 0, 0], 0, 2)
        own = attention(
            attention_info, head_queries, keys[0], values[0], *sides[head], head, tile
        )
        if head + 2 < heads:
            own, part = lax.optimization_barrier((own, packed[head + 2]))
            sides.append(halo(part))
        pieces[0, 0, head] = own
        pieces[1, 0, head] = swap(own, 1, 0)
        pieces[0, 2, head] = swap(own, 0, 2)
        if head == 1:
            pieces[1, 2, head] = swap(pieces[0, 2, head], 1, 0)
        elif head:
            pieces[1, 2, head] = swap(pieces[1, 0, head], 0, 2)

    base = (mine, other)
    for group in (range(heads - 1), range(heads - 1, heads)):
        ordered = [pieces[bit, bits, head] for bit in range(2) for bits in (0, 2) for head in group]
        base = partial_projection(
            projection_info, (out_weight, far), ordered, gate_block, base, tile, group
        )
    return (base[0] + swap(base[1], 0, 1).astype(jnp.float32)).astype(jnp.bfloat16)


def solution(mesh):
    return jax.shard_map(
        local,
        mesh=mesh,
        in_specs=(
            P("branch", "tokens", "head"),
            P("branch", "tokens", "head"),
            P("branch", "tokens", "head"),
            P("branch", "tokens", None, "head"),
            P(),
            P("head", None),
            P(),
            P(),
        ),
        out_specs=P("tokens", ("branch", "head")),
        check_vma=False,
    )
```

```python
import functools
import math

import jax
import jax.numpy as jnp
from jax import lax
from jax.experimental import pallas as pl
from jax.experimental.pallas import tpu as pltpu
from jax.sharding import PartitionSpec as P

HD = 128
FRAME = 64
FAR = 1e30
EXP2_SCALE = math.log2(math.e) / math.sqrt(HD)
VMEM_LIMIT = 16 * 1024 * 1024
COPY_LIMIT = 8 * 1024 * 1024
COPY_PARTS = 3
SMALL_COST = pl.CostEstimate(flops=0, bytes_accessed=1024, transcendentals=0)


def attention_kernel(info_ref, q_ref, k_ref, v_ref, side_a_ref, side_b_ref, out_ref):
    tiles_time = info_ref.shape[0] - 2
    tile = q_ref.shape[0] // tiles_time
    width_oks = (None, info_ref[tiles_time] == 1, info_ref[tiles_time + 1] == 1)

    def window(t):
        first = t - info_ref[t]
        base = jnp.clip(first, 0, tiles_time - 2)
        inside = [(base + step >= first) & (base + step <= first + 1) for step in range(2)]
        return pl.ds(pl.multiple_of(base * tile, tile), 2 * tile), inside

    def score(t):
        rows, inside = window(t)
        query = q_ref[t * tile : (t + 1) * tile, :]
        blocks = []
        row_max = None
        for keys, width_ok in zip(
            (k_ref[rows, :], side_a_ref[0, rows, :], side_b_ref[0, rows, :]), width_oks
        ):
            scores = lax.dot_general(
                query, keys, (((1,), (1,)), ((), ())), preferred_element_type=jnp.float32
            )
            for step in range(2):
                allowed = inside[step] if width_ok is None else inside[step] & width_ok
                block = scores[:, step * tile : (step + 1) * tile]
                lanes = block[:, :HD]
                for first in range(HD, tile, HD):
                    lanes = jnp.maximum(lanes, block[:, first : first + HD])
                lanes = jnp.where(allowed, lanes, -FAR)
                row_max = lanes if row_max is None else jnp.maximum(row_max, lanes)
                blocks.append((block, allowed))
        return blocks, jnp.max(row_max, axis=1, keepdims=True) * EXP2_SCALE

    def blend(t, blocks, shift):
        rows, _ = window(t)
        weights = [
            jnp.exp2(block * EXP2_SCALE - jnp.where(allowed, shift, FAR)).astype(jnp.bfloat16)
            for block, allowed in blocks
        ]
        values = jnp.concatenate([v_ref[rows, :], side_a_ref[1, rows, :], side_b_ref[1, rows, :]], axis=0)
        total = jnp.dot(
            jnp.concatenate(weights, axis=1),
            jnp.concatenate([values, jnp.ones_like(values)], axis=1),
            preferred_element_type=jnp.float32,
        )
        out_ref[t * tile : (t + 1) * tile, :] = (total[:, :HD] / total[:, HD:]).astype(jnp.bfloat16)

    ready = score(0)
    for t in range(tiles_time):
        later = score(t + 1) if t + 1 < tiles_time else None
        blend(t, *ready)
        ready = later


def attention(info, queries, keys, values, side_a, side_b, head, tile):
    count = queries.shape[0]
    side = pl.BlockSpec((2, count, HD), lambda i, info: (0, 0, 0))
    whole = pl.BlockSpec((count, HD), lambda i, info: (0, head))
    pairs = count * 6 * tile
    return pl.pallas_call(
        attention_kernel,
        out_shape=jax.ShapeDtypeStruct((count, HD), jnp.bfloat16),
        grid_spec=pltpu.PrefetchScalarGridSpec(
            num_scalar_prefetch=1,
            grid=(1,),
            in_specs=[whole, whole, whole, side, side],
            out_specs=pl.BlockSpec((count, HD), lambda i, info: (0, 0)),
        ),
        compiler_params=pltpu.CompilerParams(vmem_limit_bytes=VMEM_LIMIT),
        cost_estimate=SMALL_COST,
        name="attention",
    )(info, queries, keys, values, side_a, side_b)


def partial_kernel(first, kinds, info_ref, *refs):
    w_refs, refs = refs[:4], refs[4:]
    *pieces, gate_ref, base_own_ref, base_other_ref, own_ref, other_ref = refs
    tile, own_cols = own_ref.shape
    frames = tile // FRAME
    time_tile = pl.program_id(0)
    cond_first = info_ref[0] == 0
    parts = []
    for which in range(2):
        chosen = [i for i, kind in enumerate(kinds) if kind[0] == which]
        rows = jnp.concatenate([pieces[i][...] for i in chosen], axis=1)
        weights = []
        for i in chosen:
            _, far, head = kinds[i]
            depth = slice(head * HD, (head + 1) * HD)
            weights.append(jnp.concatenate([w[depth, :] for w in w_refs[2 * far : 2 * far + 2]], axis=1))
        weights = jnp.concatenate(weights, axis=0)
        projected = jnp.dot(rows, weights, preferred_element_type=jnp.float32)
        parts.append(gate_ref[which] * projected)
    for frame in range(frames):
        rows = slice(frame * FRAME, (frame + 1) * FRAME)
        guide = 1.0 + 0.5 * info_ref[5 + time_tile * frames + frame].astype(jnp.float32)
        scales = (jnp.where(cond_first, guide, 1.0 - guide), jnp.where(cond_first, 1.0 - guide, guide))
        total = scales[0] * parts[0][rows] + scales[1] * parts[1][rows]
        own, other = total[:, :own_cols], total[:, own_cols:]
        if first:
            own += scales[0] * base_own_ref[rows, :].astype(jnp.float32)
            own += scales[1] * base_other_ref[rows, :].astype(jnp.float32)
        else:
            own += base_own_ref[rows, :]
            other += base_other_ref[rows, :]
        own_ref[rows, :] = own
        other_ref[rows, :] = other.astype(other_ref.dtype)


def partial_projection(info, weights, pieces, gate, base, tile, first):
    count, width = base[0].shape
    features = weights[0].shape[0]
    kinds = tuple(pieces)
    rows = pl.BlockSpec((tile, width), lambda t, info: (t, 0))
    piece = pl.BlockSpec((tile, HD), lambda t, info: (t, 0))
    weight_specs = [
        pl.BlockSpec((features, width), lambda t, info, place=place: (0, info[place]))
        for place in range(1, 5)
    ]
    return pl.pallas_call(
        functools.partial(partial_kernel, first, kinds),
        out_shape=[
            jax.ShapeDtypeStruct((count, width), jnp.float32),
            jax.ShapeDtypeStruct((count, width), jnp.float32 if first else jnp.bfloat16),
        ],
        grid_spec=pltpu.PrefetchScalarGridSpec(
            num_scalar_prefetch=1,
            grid=(count // tile,),
            in_specs=weight_specs
            + [piece] * len(pieces)
            + [pl.BlockSpec(gate.shape, lambda t, info: (0, 0, 0)), rows, rows],
            out_specs=[rows, rows],
        ),
        compiler_params=pltpu.CompilerParams(vmem_limit_bytes=VMEM_LIMIT),
        cost_estimate=SMALL_COST,
        name="partial_projection",
    )(info, *[w for w in weights for _ in range(2)], *pieces.values(), gate, *base)


def copy_kernel(plan, info_ref, *refs):
    *arrays, sems = refs
    copies = []
    for source, cols, width, target, place in plan:
        src, dst = arrays[source], arrays[target]
        first = cols if cols is not None else pl.multiple_of(info_ref[0] * width, width)
        for part in range(COPY_PARTS):
            size = src.shape[0] // COPY_PARTS
            rows = pl.ds(part * size, size)
            to = dst.at[rows, :] if place is None else dst.at[place, rows, :]
            copies.append((src.at[rows, pl.ds(first, width)], to))
    copies = [
        pltpu.make_async_copy(src, to, sems.at[index]) for index, (src, to) in enumerate(copies)
    ]
    for copy in copies:
        copy.start()
    for copy in copies:
        copy.wait()


def copy_columns(info, sources, plan, targets):
    moved = sum(2 * 2 * sources[source].shape[0] * width for source, _, width, _, _ in plan)
    return pl.pallas_call(
        functools.partial(copy_kernel, plan),
        out_shape=[jax.ShapeDtypeStruct(shape, jnp.bfloat16) for shape in targets],
        grid_spec=pltpu.PrefetchScalarGridSpec(
            num_scalar_prefetch=1,
            grid=(1,),
            in_specs=[pl.BlockSpec(memory_space=pl.ANY)] * len(sources),
            out_specs=[pl.BlockSpec(memory_space=pltpu.VMEM)] * len(targets),
            scratch_shapes=[pltpu.SemaphoreType.DMA((COPY_PARTS * len(plan),))],
        ),
        cost_estimate=SMALL_COST,
        compiler_params=pltpu.CompilerParams(vmem_limit_bytes=COPY_LIMIT),
        name="copy_columns",
    )(info, *sources)


def local(queries, keys, values, residual, gate, out_weight, time_offsets, guidance_index):
    tiles_time, tiles_wide = time_offsets.shape
    count, features = queries.shape[1:]
    tile = count // tiles_time
    heads = features // HD
    head_count = lax.axis_size("head")
    columns = lax.axis_size("tokens")
    branch_pos = lax.axis_index("branch")
    head_pos = lax.axis_index("head")
    width_pos = lax.axis_index("tokens")
    width = gate.shape[2] // head_count

    rounds = [
        [pair for i in range(first, columns - 1, 2) for pair in ((i, i + 1), (i + 1, i))]
        for first in range(2)
    ]
    near_pos = (width_pos ^ 1, ((width_pos + 1) ^ 1) - 1)

    def swap(value, branch_bit, head_bits):
        if not branch_bit and not head_bits:
            return value
        if not head_bits:
            return lax.ppermute(value, "branch", [(0, 1), (1, 0)])
        if not branch_bit:
            return lax.ppermute(value, "head", [(i, i ^ head_bits) for i in range(head_count)])
        flip = head_count + head_bits
        return lax.ppermute(
            value, ("branch", "head"), [(i, i ^ flip) for i in range(2 * head_count)]
        )

    branch_pair = branch_pos * (head_count // 2)
    copy_info = jnp.stack([branch_pair + ((head_pos ^ 2) >> 1)])
    key_value = (2, count, HD)
    packed = copy_columns(
        copy_info, (keys[0], values[0]), ((0, 0, HD, 2, 0), (1, 0, HD, 2, 1)), (key_value,)
    )
    (packed, late_keys, late_values, late_weight) = lax.optimization_barrier(
        (packed, keys[0], values[0], out_weight)
    )
    *late, far = copy_columns(
        copy_info,
        (late_keys, late_values, late_weight),
        [(array, head * HD, HD, 2 + head, array) for head in range(1, heads) for array in range(2)]
        + [(2, None, 2 * width, 2 + heads, None)],
        [key_value] * (heads - 1) + [(features, 2 * width)],
    )
    late, far, residual = lax.optimization_barrier((late, far, residual))
    packed = list(packed) + late

    def halo(part):
        return [lax.ppermute(part, "tokens", pairs) for pairs in rounds]

    sides = [halo(part) for part in packed[:2]]
    far = swap(far, 0, 2)

    first_half, second_half = residual[0, :, 0], residual[0, :, 1]
    mine = jnp.where(branch_pos == 0, first_half, second_half)
    other = swap(jnp.where(branch_pos == 0, second_half, first_half), 1, 0)
    gate_block = jnp.concatenate(
        [
            lax.dynamic_slice(gate, (0, branch_pos, place * width), (2, 1, width))
            for place in (head_pos, head_pos ^ 1)
        ],
        axis=2,
    ).astype(jnp.float32)
    gate_block = jnp.where(branch_pos == 0, gate_block, gate_block[::-1])

    offsets = lax.dynamic_index_in_dim(time_offsets, width_pos, 1, keepdims=False)
    edges = jnp.stack([(pos >= 0) & (pos < tiles_wide) for pos in near_pos]).astype(jnp.int32)
    attention_info = jnp.concatenate([offsets, edges])
    places = [branch_pos * head_count + head_pos, branch_pos * head_count + (head_pos ^ 1)]
    places += [head_pos & 1, (head_pos & 1) ^ 1]
    projection_info = jnp.concatenate([jnp.stack([branch_pos] + places), guidance_index])

    pieces = {}
    head_queries = queries[0]
    for head in range(heads):
        if head == 2:
            early = [(1, 0, 0), (0, 1, 0), (1, 0, 1), (1, 1, 0)]
            head_queries, far, other, *here = lax.optimization_barrier(
                (head_queries, far, other, *[pieces[name] for name in early])
            )
            pieces.update(zip(early, here))
        own = attention(
            attention_info, head_queries, keys[0], values[0], *sides[head], head, tile
        )
        if head + 2 < heads:
            own, part = lax.optimization_barrier((own, packed[head + 2]))
            sides.append(halo(part))
        pieces[0, 0, head] = own
        pieces[1, 0, head] = swap(own, 1, 0)
        pieces[0, 1, head] = swap(own, 0, 2)
        if head == 1:
            pieces[1, 1, head] = swap(pieces[0, 1, head], 1, 0)
        else:
            pieces[1, 1, head] = swap(pieces[1, 0, head], 0, 2)

    late = [(1, 1, heads - 2)] + [name for name in pieces if name[2] == heads - 1]
    base = (mine, other)
    for chosen in ([name for name in pieces if name not in late], late):
        base = partial_projection(
            projection_info,
            (out_weight, far),
            {name: pieces[name] for name in chosen},
            gate_block,
            base,
            tile,
            base[0] is mine,
        )
    return (base[0] + swap(base[1], 0, 1).astype(jnp.float32)).astype(jnp.bfloat16)


def solution(mesh):
    return jax.shard_map(
        local,
        mesh=mesh,
        in_specs=(
            P("branch", "tokens", "head"),
            P("branch", "tokens", "head"),
            P("branch", "tokens", "head"),
            P("branch", "tokens", None, "head"),
            P(),
            P("head", None),
            P(),
            P(),
        ),
        out_specs=P("tokens", ("branch", "head")),
        check_vma=False,
    )
```

```python
import functools
import math

import jax
import jax.numpy as jnp
from jax import lax
from jax.experimental import pallas as pl
from jax.experimental.pallas import tpu as pltpu
from jax.sharding import PartitionSpec as P

HD = 128
FRAME = 64
FAR = 1e30
EXP2_SCALE = math.log2(math.e) / math.sqrt(HD)
VMEM_LIMIT = 16 * 1024 * 1024
COPY_LIMIT = 8 * 1024 * 1024
COPY_PARTS = 3
SCALARS = pl.BlockSpec(memory_space=pltpu.SMEM)
IN_VMEM = pl.BlockSpec(memory_space=pltpu.VMEM)
SMALL_COST = pl.CostEstimate(flops=0, bytes_accessed=1024, transcendentals=0)


def attention_kernel(info_ref, q_ref, own_ref, side_a_ref, side_b_ref, out_ref):
    tiles_time = info_ref.shape[0] - 2
    tile = q_ref.shape[0] // tiles_time
    width_oks = (None, info_ref[tiles_time] == 1, info_ref[tiles_time + 1] == 1)

    def window(t):
        first = t - info_ref[t]
        base = jnp.clip(first, 0, tiles_time - 2)
        inside = [(base + step >= first) & (base + step <= first + 1) for step in range(2)]
        return pl.ds(pl.multiple_of(base * tile, tile), 2 * tile), inside

    def score(t):
        rows, inside = window(t)
        query = q_ref[t * tile : (t + 1) * tile, :]
        blocks = []
        row_max = None
        for ref, width_ok in zip((own_ref, side_a_ref, side_b_ref), width_oks):
            scores = lax.dot_general(
                query, ref[0, rows, :], (((1,), (1,)), ((), ())), preferred_element_type=jnp.float32
            )
            for step in range(2):
                allowed = inside[step] if width_ok is None else inside[step] & width_ok
                block = scores[:, step * tile : (step + 1) * tile]
                lanes = block[:, :HD]
                for first in range(HD, tile, HD):
                    lanes = jnp.maximum(lanes, block[:, first : first + HD])
                lanes = jnp.where(allowed, lanes, -FAR)
                row_max = lanes if row_max is None else jnp.maximum(row_max, lanes)
                blocks.append((block, allowed))
        return blocks, jnp.max(row_max, axis=1, keepdims=True) * EXP2_SCALE

    def blend(t, blocks, shift):
        rows, _ = window(t)
        weights = [
            jnp.exp2(block * EXP2_SCALE - jnp.where(allowed, shift, FAR)).astype(jnp.bfloat16)
            for block, allowed in blocks
        ]
        values = jnp.concatenate(
            [ref[1, rows, :] for ref in (own_ref, side_a_ref, side_b_ref)], axis=0
        )
        total = jnp.dot(
            jnp.concatenate(weights, axis=1),
            jnp.concatenate([values, jnp.ones_like(values)], axis=1),
            preferred_element_type=jnp.float32,
        )
        out_ref[t * tile : (t + 1) * tile, :] = (total[:, :HD] / total[:, HD:]).astype(jnp.bfloat16)

    ready = score(0)
    for t in range(tiles_time):
        later = score(t + 1) if t + 1 < tiles_time else None
        blend(t, *ready)
        ready = later


def attention(info, *operands):
    return pl.pallas_call(
        attention_kernel,
        out_shape=jax.ShapeDtypeStruct(operands[0].shape, jnp.bfloat16),
        in_specs=[SCALARS] + [IN_VMEM] * len(operands),
        out_specs=IN_VMEM,
        compiler_params=pltpu.CompilerParams(vmem_limit_bytes=VMEM_LIMIT),
        cost_estimate=SMALL_COST,
        name="attention",
    )(info, *operands)


def partial_kernel(first, kinds, tile, info_ref, *refs):
    w_refs, refs = refs[:2], refs[2:]
    *pieces, gate_ref, base_own_ref, base_other_ref, own_ref, other_ref = refs
    own_cols = own_ref.shape[1]
    frames = tile // FRAME
    cond_first = info_ref[0] == 0
    places = [pl.ds(pl.multiple_of(info_ref[i] * own_cols, own_cols), own_cols) for i in (1, 2)]
    chosen = [[i for i, kind in enumerate(kinds) if kind[0] == which] for which in range(2)]
    weights = []
    for names in chosen:
        blocks = []
        for _, far, head in [kinds[i] for i in names]:
            depth = slice(head * HD, (head + 1) * HD)
            blocks.append(jnp.concatenate([w_refs[far][depth, place] for place in places], axis=1))
        weights.append(jnp.concatenate(blocks, axis=0))
    for time_tile in range(own_ref.shape[0] // tile):
        token_rows = slice(time_tile * tile, (time_tile + 1) * tile)
        parts = []
        for which in range(2):
            attended = jnp.concatenate([pieces[i][token_rows, :] for i in chosen[which]], axis=1)
            projected = jnp.dot(attended, weights[which], preferred_element_type=jnp.float32)
            parts.append(gate_ref[which] * projected)
        for frame in range(frames):
            rows = slice(frame * FRAME, (frame + 1) * FRAME)
            out_rows = slice(time_tile * tile + rows.start, time_tile * tile + rows.stop)
            guide = 1.0 + 0.5 * info_ref[3 + time_tile * frames + frame].astype(jnp.float32)
            scales = (
                jnp.where(cond_first, guide, 1.0 - guide),
                jnp.where(cond_first, 1.0 - guide, guide),
            )
            total = scales[0] * parts[0][rows] + scales[1] * parts[1][rows]
            own, other = total[:, :own_cols], total[:, own_cols:]
            if first:
                own += scales[0] * base_own_ref[out_rows, :].astype(jnp.float32)
                own += scales[1] * base_other_ref[out_rows, :].astype(jnp.float32)
            else:
                own += base_own_ref[out_rows, :]
                other += base_other_ref[out_rows, :]
            own_ref[out_rows, :] = own
            other_ref[out_rows, :] = other.astype(other_ref.dtype)


def partial_projection(info, weights, pieces, gate, base, tile, first):
    shape = base[0].shape
    return pl.pallas_call(
        functools.partial(partial_kernel, first, tuple(pieces), tile),
        out_shape=[
            jax.ShapeDtypeStruct(shape, jnp.float32),
            jax.ShapeDtypeStruct(shape, jnp.float32 if first else jnp.bfloat16),
        ],
        in_specs=[SCALARS] + [IN_VMEM] * (len(weights) + len(pieces) + 3),
        out_specs=[IN_VMEM] * 2,
        compiler_params=pltpu.CompilerParams(vmem_limit_bytes=VMEM_LIMIT),
        cost_estimate=SMALL_COST,
        name="partial_projection",
    )(info, *weights, *pieces.values(), gate, *base)


def copy_kernel(plan, info_ref, *refs):
    *arrays, sems = refs
    copies = []
    for source, block, width, target, place in plan:
        src, dst = arrays[source], arrays[target]
        first = block * width
        if block < 0:
            first = pl.multiple_of(info_ref[block + info_ref.shape[0]] * width, width)
        for part in range(COPY_PARTS):
            size = src.shape[0] // COPY_PARTS
            rows = pl.ds(part * size, size)
            to = dst.at[rows, :] if place is None else dst.at[place, rows, :]
            copies.append((src.at[rows, pl.ds(first, width)], to))
    copies = [
        pltpu.make_async_copy(src, to, sems.at[index]) for index, (src, to) in enumerate(copies)
    ]
    for copy in copies:
        copy.start()
    for copy in copies:
        copy.wait()


def copy_columns(info, sources, plan, targets):
    return pl.pallas_call(
        functools.partial(copy_kernel, plan),
        out_shape=[jax.ShapeDtypeStruct(shape, jnp.bfloat16) for shape in targets],
        in_specs=[SCALARS] + [pl.BlockSpec(memory_space=pltpu.HBM)] * len(sources),
        out_specs=[IN_VMEM] * len(targets),
        scratch_shapes=[pltpu.SemaphoreType.DMA((COPY_PARTS * len(plan),))],
        compiler_params=pltpu.CompilerParams(vmem_limit_bytes=COPY_LIMIT),
        cost_estimate=SMALL_COST,
        name="copy_columns",
    )(info, *[pltpu.with_memory_space_constraint(source, pltpu.HBM) for source in sources])


def local(queries, keys, values, residual, gate, out_weight, time_offsets, guidance_index):
    tiles_time, tiles_wide = time_offsets.shape
    count, features = queries.shape[1:]
    tile = count // tiles_time
    heads = features // HD
    head_count = lax.axis_size("head")
    columns = lax.axis_size("tokens")
    branch_pos = lax.axis_index("branch")
    head_pos = lax.axis_index("head")
    width_pos = lax.axis_index("tokens")
    width = gate.shape[2] // head_count

    rounds = [
        [pair for i in range(first, columns - 1, 2) for pair in ((i, i + 1), (i + 1, i))]
        for first in range(2)
    ]
    near_pos = (width_pos ^ 1, ((width_pos + 1) ^ 1) - 1)

    def swap(value, branch_bit, head_bits):
        if not branch_bit and not head_bits:
            return value
        if not head_bits:
            return lax.ppermute(value, "branch", [(0, 1), (1, 0)])
        if not branch_bit:
            return lax.ppermute(value, "head", [(i, i ^ head_bits) for i in range(head_count)])
        flip = head_count + head_bits
        return lax.ppermute(
            value, ("branch", "head"), [(i, i ^ flip) for i in range(2 * head_count)]
        )

    pair = head_pos >> 1
    branch_pair = branch_pos * (head_count // 2)
    copy_info = jnp.stack([branch_pair + pair, branch_pair + (pair ^ 1)])
    query, key_value, pair_weight = (count, HD), (2, count, HD), (features, 2 * width)
    packed = copy_columns(
        copy_info, (keys[0], values[0]), [(0, 0, HD, 2, 0), (1, 0, HD, 2, 1)], [key_value]
    )
    packed, late_sources = lax.optimization_barrier(
        (packed, (queries[0], keys[0], values[0], out_weight))
    )
    plan, targets = [], []

    def plan_copies(sources, block, width, places, target):
        for source, place in zip(sources, places):
            plan.append((source, block, width, len(late_sources) + len(targets), place))
        targets.append(target)

    for head in range(1, heads):
        plan_copies((1, 2), head, HD, (0, 1), key_value)
    for head in range(heads):
        plan_copies((0,), head, HD, (None,), query)
    for block in (-2, -1):
        plan_copies((3,), block, 2 * width, (None,), pair_weight)
    late = copy_columns(copy_info, late_sources, plan, targets)
    packed, head_queries, (near, far) = list(packed) + list(late)[: heads - 1], list(late[heads - 1 : -2]), late[-2:]

    def halo(part):
        return [lax.ppermute(part, "tokens", pairs) for pairs in rounds]

    sides = [halo(part) for part in packed[:2]]
    far = swap(far, 0, 2)

    sides[0], residual = lax.optimization_barrier((sides[0], residual))
    first_half, second_half = residual[0, :, 0], residual[0, :, 1]
    mine = jnp.where(branch_pos == 0, first_half, second_half)
    other = swap(jnp.where(branch_pos == 0, second_half, first_half), 1, 0)
    gate_block = jnp.concatenate(
        [
            lax.dynamic_slice(gate, (0, branch_pos, place * width), (2, 1, width))
            for place in (head_pos, head_pos ^ 1)
        ],
        axis=2,
    ).astype(jnp.float32)
    gate_block = jnp.where(branch_pos == 0, gate_block, gate_block[::-1])

    offsets = lax.dynamic_index_in_dim(time_offsets, width_pos, 1, keepdims=False)
    edges = jnp.stack([(pos >= 0) & (pos < tiles_wide) for pos in near_pos]).astype(jnp.int32)
    attention_info = jnp.concatenate([offsets, edges])
    place = head_pos & 1
    projection_info = jnp.concatenate([jnp.stack([branch_pos, place, place ^ 1]), guidance_index])

    pieces = {}

    def await_pieces(head, *names, more=()):
        head_queries[head], here, more = lax.optimization_barrier(
            (head_queries[head], [pieces[name] for name in names], more)
        )
        pieces.update(zip(names, here))
        return more

    for head in range(heads):
        if head == 0:
            head_queries[0], far, projection_info, gate_block = lax.optimization_barrier(
                (head_queries[0], far, projection_info, gate_block)
            )
        elif head == 1:
            await_pieces(head, (0, 1, 0))
        else:
            other = await_pieces(head, (1, 0, 0), (1, 0, 1), (1, 1, 0), more=other)
        own = attention(attention_info, head_queries[head], packed[head], *sides[head])
        if head + 2 < heads:
            own, part = lax.optimization_barrier((own, packed[head + 2]))
            sides.append(halo(part))
        pieces[0, 0, head] = own
        pieces[1, 0, head] = swap(own, 1, 0)
        pieces[0, 1, head] = swap(own, 0, 2)
        if head == 1:
            pieces[1, 1, head] = swap(pieces[0, 1, head], 1, 0)
        else:
            pieces[1, 1, head] = swap(pieces[1, 0, head], 0, 2)

    late = [(1, 1, heads - 2)] + [name for name in pieces if name[2] == heads - 1]
    base = (mine, other)
    for chosen in ([name for name in pieces if name not in late], late):
        base = partial_projection(
            projection_info,
            (near, far),
            {name: pieces[name] for name in chosen},
            gate_block,
            base,
            tile,
            base[0] is mine,
        )
    return (base[0] + swap(base[1], 0, 1).astype(jnp.float32)).astype(jnp.bfloat16)


def solution(mesh):
    return jax.shard_map(
        local,
        mesh=mesh,
        in_specs=(
            P("branch", "tokens", "head"),
            P("branch", "tokens", "head"),
            P("branch", "tokens", "head"),
            P("branch", "tokens", None, "head"),
            P(),
            P("head", None),
            P(),
            P(),
        ),
        out_specs=P("tokens", ("branch", "head")),
        check_vma=False,
    )
```

```python
import functools
import math

import jax
import jax.numpy as jnp
from jax import lax
from jax.experimental import pallas as pl
from jax.experimental.pallas import tpu as pltpu
from jax.sharding import PartitionSpec as P

HD = 128
FRAME = 64
FAR = 1e30
EXP2_SCALE = math.log2(math.e) / math.sqrt(HD)
VMEM_LIMIT = 16 * 1024 * 1024
COPY_LIMIT = 8 * 1024 * 1024
COPY_PARTS = 3
LATE_PACK = True
RESIDUAL_FIRST = True
SPLIT = 2
BEFORE_X = {1: (), 2: ((1, 1, 0),)}
BEFORE_Y = {1: (), 2: ()}
RESIDUAL_AFTER = 0
AWAITED = {0: (), 1: ('far', (0, 1, 0)), 2: ('far', 'other', (1, 0, 0), (0, 1, 0)), 3: ((1, 0, 1),)}
RELAY = ('y', 'x', 'y')
LATE = ((1, 1, 1),)
SCALARS = pl.BlockSpec(memory_space=pltpu.SMEM)
IN_VMEM = pl.BlockSpec(memory_space=pltpu.VMEM)
SMALL_COST = pl.CostEstimate(flops=0, bytes_accessed=1024, transcendentals=0)


def attention_kernel(first, last, info_ref, q_ref, own_ref, side_a_ref, side_b_ref, *refs):
    *earlier, out_ref = refs
    tiles_time = info_ref.shape[0] - 2
    tile = q_ref.shape[0] // tiles_time
    width_oks = (None, info_ref[tiles_time] == 1, info_ref[tiles_time + 1] == 1)

    def window(t):
        first = t - info_ref[t]
        base = jnp.clip(first, 0, tiles_time - 2)
        inside = [(base + step >= first) & (base + step <= first + 1) for step in range(2)]
        return pl.ds(pl.multiple_of(base * tile, tile), 2 * tile), inside

    def score(t):
        rows, inside = window(t)
        query = q_ref[t * tile : (t + 1) * tile, :]
        blocks = []
        row_max = None
        for ref, width_ok in zip((own_ref, side_a_ref, side_b_ref), width_oks):
            scores = lax.dot_general(
                query, ref[0, rows, :], (((1,), (1,)), ((), ())), preferred_element_type=jnp.float32
            )
            for step in range(2):
                allowed = inside[step] if width_ok is None else inside[step] & width_ok
                block = scores[:, step * tile : (step + 1) * tile]
                lanes = block[:, :HD]
                for first in range(HD, tile, HD):
                    lanes = jnp.maximum(lanes, block[:, first : first + HD])
                lanes = jnp.where(allowed, lanes, -FAR)
                row_max = lanes if row_max is None else jnp.maximum(row_max, lanes)
                blocks.append((block, allowed))
        return blocks, jnp.max(row_max, axis=1, keepdims=True) * EXP2_SCALE

    def blend(t, blocks, shift):
        rows, _ = window(t)
        weights = [
            jnp.exp2(block * EXP2_SCALE - jnp.where(allowed, shift, FAR)).astype(jnp.bfloat16)
            for block, allowed in blocks
        ]
        values = jnp.concatenate(
            [ref[1, rows, :] for ref in (own_ref, side_a_ref, side_b_ref)], axis=0
        )
        total = jnp.dot(
            jnp.concatenate(weights, axis=1),
            jnp.concatenate([values, jnp.ones_like(values)], axis=1),
            preferred_element_type=jnp.float32,
        )
        out_ref[t * tile : (t + 1) * tile, :] = (total[:, :HD] / total[:, HD:]).astype(jnp.bfloat16)

    ready = score(first)
    for ref in earlier:
        out_ref[: first * tile, :] = ref[: first * tile, :]
    for t in range(first, last):
        later = score(t + 1) if t + 1 < last else None
        blend(t, *ready)
        ready = later


def attention(info, tiles, *operands):
    return pl.pallas_call(
        functools.partial(attention_kernel, *tiles),
        out_shape=jax.ShapeDtypeStruct(operands[0].shape, jnp.bfloat16),
        in_specs=[SCALARS] + [IN_VMEM] * len(operands),
        out_specs=IN_VMEM,
        compiler_params=pltpu.CompilerParams(vmem_limit_bytes=VMEM_LIMIT),
        cost_estimate=SMALL_COST,
        name="attention",
    )(info, *operands)


def partial_kernel(first, kinds, tile, info_ref, *refs):
    w_refs, refs = refs[:2], refs[2:]
    *pieces, gate_ref, base_own_ref, base_other_ref, own_ref, other_ref = refs
    own_cols = own_ref.shape[1]
    frames = tile // FRAME
    cond_first = info_ref[0] == 0
    places = [pl.ds(pl.multiple_of(info_ref[i] * own_cols, own_cols), own_cols) for i in (1, 2)]
    chosen = [[i for i, kind in enumerate(kinds) if kind[0] == which] for which in range(2)]
    weights = []
    for names in chosen:
        blocks = []
        for _, far, head in [kinds[i] for i in names]:
            depth = slice(head * HD, (head + 1) * HD)
            blocks.append(jnp.concatenate([w_refs[far][depth, place] for place in places], axis=1))
        weights.append(jnp.concatenate(blocks, axis=0))
    for time_tile in range(own_ref.shape[0] // tile):
        token_rows = slice(time_tile * tile, (time_tile + 1) * tile)
        parts = []
        for which in range(2):
            attended = jnp.concatenate([pieces[i][token_rows, :] for i in chosen[which]], axis=1)
            projected = jnp.dot(attended, weights[which], preferred_element_type=jnp.float32)
            parts.append(gate_ref[which] * projected)
        for frame in range(frames):
            rows = slice(frame * FRAME, (frame + 1) * FRAME)
            out_rows = slice(time_tile * tile + rows.start, time_tile * tile + rows.stop)
            guide = 1.0 + 0.5 * info_ref[3 + time_tile * frames + frame].astype(jnp.float32)
            scales = (
                jnp.where(cond_first, guide, 1.0 - guide),
                jnp.where(cond_first, 1.0 - guide, guide),
            )
            total = scales[0] * parts[0][rows] + scales[1] * parts[1][rows]
            own, other = total[:, :own_cols], total[:, own_cols:]
            if first:
                own += scales[0] * base_own_ref[out_rows, :].astype(jnp.float32)
                own += scales[1] * base_other_ref[out_rows, :].astype(jnp.float32)
            else:
                own += base_own_ref[out_rows, :]
                other += base_other_ref[out_rows, :]
            own_ref[out_rows, :] = own
            other_ref[out_rows, :] = other.astype(other_ref.dtype)


def partial_projection(info, weights, pieces, gate, base, tile, first):
    shape = base[0].shape
    return pl.pallas_call(
        functools.partial(partial_kernel, first, tuple(pieces), tile),
        out_shape=[
            jax.ShapeDtypeStruct(shape, jnp.float32),
            jax.ShapeDtypeStruct(shape, jnp.float32 if first else jnp.bfloat16),
        ],
        in_specs=[SCALARS] + [IN_VMEM] * (len(weights) + len(pieces) + 3),
        out_specs=[IN_VMEM] * 2,
        compiler_params=pltpu.CompilerParams(vmem_limit_bytes=VMEM_LIMIT),
        cost_estimate=SMALL_COST,
        name="partial_projection",
    )(info, *weights, *pieces.values(), gate, *base)


def copy_kernel(plan, info_ref, *refs):
    *arrays, sems = refs
    copies = []
    for source, block, width, target, place in plan:
        src, dst = arrays[source], arrays[target]
        first = block * width
        if block < 0:
            first = pl.multiple_of(info_ref[block + info_ref.shape[0]] * width, width)
        for part in range(COPY_PARTS):
            size = src.shape[0] // COPY_PARTS
            rows = pl.ds(part * size, size)
            to = dst.at[rows, :] if place is None else dst.at[place, rows, :]
            copies.append((src.at[rows, pl.ds(first, width)], to))
    copies = [
        pltpu.make_async_copy(src, to, sems.at[index]) for index, (src, to) in enumerate(copies)
    ]
    for copy in copies:
        copy.start()
    for copy in copies:
        copy.wait()


def copy_columns(info, sources, plan, targets):
    return pl.pallas_call(
        functools.partial(copy_kernel, plan),
        out_shape=[jax.ShapeDtypeStruct(shape, jnp.bfloat16) for shape in targets],
        in_specs=[SCALARS] + [pl.BlockSpec(memory_space=pltpu.HBM)] * len(sources),
        out_specs=[IN_VMEM] * len(targets),
        scratch_shapes=[pltpu.SemaphoreType.DMA((COPY_PARTS * len(plan),))],
        compiler_params=pltpu.CompilerParams(vmem_limit_bytes=COPY_LIMIT),
        cost_estimate=SMALL_COST,
        name="copy_columns",
    )(info, *[pltpu.with_memory_space_constraint(source, pltpu.HBM) for source in sources])


def local(queries, keys, values, residual, gate, out_weight, time_offsets, guidance_index):
    tiles_time, tiles_wide = time_offsets.shape
    count, features = queries.shape[1:]
    tile = count // tiles_time
    heads = features // HD
    head_count = lax.axis_size("head")
    columns = lax.axis_size("tokens")
    branch_pos = lax.axis_index("branch")
    head_pos = lax.axis_index("head")
    width_pos = lax.axis_index("tokens")
    width = gate.shape[2] // head_count

    rounds = [
        [pair for i in range(first, columns - 1, 2) for pair in ((i, i + 1), (i + 1, i))]
        for first in range(2)
    ]
    near_pos = (width_pos ^ 1, ((width_pos + 1) ^ 1) - 1)

    def swap(value, branch_bit, head_bits):
        if not branch_bit and not head_bits:
            return value
        if not head_bits:
            return lax.ppermute(value, "branch", [(0, 1), (1, 0)])
        if not branch_bit:
            return lax.ppermute(value, "head", [(i, i ^ head_bits) for i in range(head_count)])
        flip = head_count + head_bits
        return lax.ppermute(
            value, ("branch", "head"), [(i, i ^ flip) for i in range(2 * head_count)]
        )

    pair = head_pos >> 1
    branch_pair = branch_pos * (head_count // 2)
    copy_info = jnp.stack([branch_pair + pair, branch_pair + (pair ^ 1)])
    sources = (queries[0], keys[0], values[0], out_weight)
    key_value = [((1, 2), head, HD, (0, 1), (2, count, HD)) for head in range(heads)]
    query = [((0,), head, HD, (None,), (count, HD)) for head in range(heads)]
    pair_weight = [((3,), block, 2 * width, (None,), (features, 2 * width)) for block in (-2, -1)]

    def pack(parts, after=None):
        here = sources
        if after is not None:
            _, here = lax.optimization_barrier((after, sources))
        used = sorted({index for part in parts for index in part[0]})
        plan = [
            (used.index(source), block, cols, len(used) + target, place)
            for target, (froms, block, cols, places, _) in enumerate(parts)
            for source, place in zip(froms, places)
        ]
        return copy_columns(
            copy_info, [here[index] for index in used], plan, [part[-1] for part in parts]
        )

    def split_residual(residual):
        first_half, second_half = residual[0, :, 0], residual[0, :, 1]
        mine = jnp.where(branch_pos == 0, first_half, second_half)
        return mine, jnp.where(branch_pos == 0, second_half, first_half)

    packed = pack(key_value[:1])
    after = packed
    if RESIDUAL_AFTER == 0:
        _, residual = lax.optimization_barrier((packed, residual))
        mine, other = split_residual(residual)
        after = (packed, other) if RESIDUAL_FIRST else packed
    late_key_value, far = pack([key_value[1], pair_weight[1]], after)
    packed = list(packed) + [late_key_value]

    def halo(part):
        return [lax.ppermute(part, "tokens", pairs) for pairs in rounds]

    sides = [halo(part) for part in packed]
    near, *late = pack(pair_weight[:1] + query + key_value[2:], sides[0] if LATE_PACK else packed)
    head_queries, packed = late[:heads], packed + late[heads:]
    store = {"far": swap(far, 0, 2)}

    if RESIDUAL_AFTER:
        _, residual = lax.optimization_barrier(((packed[1], sides[0])[RESIDUAL_AFTER - 1], residual))
        mine, other = split_residual(residual)
    store["other"] = swap(other, 1, 0)
    gate_block = jnp.concatenate(
        [
            lax.dynamic_slice(gate, (0, branch_pos, place * width), (2, 1, width))
            for place in (head_pos, head_pos ^ 1)
        ],
        axis=2,
    ).astype(jnp.float32)
    gate_block = jnp.where(branch_pos == 0, gate_block, gate_block[::-1])

    offsets = lax.dynamic_index_in_dim(time_offsets, width_pos, 1, keepdims=False)
    edges = jnp.stack([(pos >= 0) & (pos < tiles_wide) for pos in near_pos]).astype(jnp.int32)
    attention_info = jnp.concatenate([offsets, edges])
    place = head_pos & 1
    projection_info = jnp.concatenate([jnp.stack([branch_pos, place, place ^ 1]), guidance_index])

    def await_names(names, value):
        value, awaited = lax.optimization_barrier((value, [store[name] for name in names]))
        store.update(zip(names, awaited))
        return value

    for head in range(heads):
        head_queries[head] = await_names(AWAITED.get(head, ()), head_queries[head])
        operands = [head_queries[head], packed[head], *sides[head]]
        if head == heads - 1 and SPLIT:
            own = attention(attention_info, (0, SPLIT), *operands)
            own = await_names(AWAITED.get(heads, ()), own)
            own = attention(attention_info, (SPLIT, tiles_time), *operands, own)
        else:
            own = attention(attention_info, (0, tiles_time), *operands)
        if head + 2 < heads:
            own, part = lax.optimization_barrier((own, packed[head + 2]))
            sides.append(halo(part))
        store[0, 0, head] = own
        store[1, 0, head] = swap(await_names(BEFORE_X.get(head, ()), own), 1, 0)
        store[0, 1, head] = swap(await_names(BEFORE_Y.get(head, ()), own), 0, 2)
        if RELAY[head] == "x":
            store[1, 1, head] = swap(store[0, 1, head], 1, 0)
        elif RELAY[head] == "y":
            store[1, 1, head] = swap(store[1, 0, head], 0, 2)
        else:
            store[1, 1, head] = swap(own, 1, 2)

    names = [name for name in store if isinstance(name, tuple)]
    late = [name for name in names if name[2] == heads - 1 or name in LATE]
    base = (mine, store["other"])
    for chosen in ([name for name in names if name not in late], late):
        base = partial_projection(
            projection_info,
            (near, store["far"]),
            {name: store[name] for name in chosen},
            gate_block,
            base,
            tile,
            base[0] is mine,
        )
    return (base[0] + swap(base[1], 0, 1).astype(jnp.float32)).astype(jnp.bfloat16)


def solution(mesh):
    return jax.shard_map(
        local,
        mesh=mesh,
        in_specs=(
            P("branch", "tokens", "head"),
            P("branch", "tokens", "head"),
            P("branch", "tokens", "head"),
            P("branch", "tokens", None, "head"),
            P(),
            P("head", None),
            P(),
            P(),
        ),
        out_specs=P("tokens", ("branch", "head")),
        check_vma=False,
    )
```

```python
import functools
import math

import jax
import jax.numpy as jnp
from jax import lax
from jax.experimental import pallas as pl
from jax.experimental.pallas import tpu as pltpu
from jax.sharding import PartitionSpec as P

HD = 128
FRAME = 64
FAR = 1e30
EXP2_SCALE = math.log2(math.e) / math.sqrt(HD)
VMEM_LIMIT = 14 * 1024 * 1024
COPY_LIMIT = 8 * 1024 * 1024
COPY_PARTS = 3
LATE_PACK = True
RESIDUAL_FIRST = True
SPLIT = 0
TIE_PARTIAL = True
BEFORE_X = {1: (), 2: ()}
BEFORE_Y = {1: (), 2: ()}
RESIDUAL_AFTER = 0
AWAITED = {0: (), 1: ('far', 'other'), 2: ('far', 'other', (1, 0, 0), (0, 1, 0)), 3: ((1, 0, 1),)}
RELAY = ('y', 'x', 'y')
LATE = ((1, 1, 1),)
SCALARS = pl.BlockSpec(memory_space=pltpu.SMEM)
IN_VMEM = pl.BlockSpec(memory_space=pltpu.VMEM)
SMALL_COST = pl.CostEstimate(flops=0, bytes_accessed=1024, transcendentals=0)


def attention_kernel(first, last, info_ref, q_ref, own_ref, side_a_ref, side_b_ref, *refs):
    *earlier, out_ref = refs
    tiles_time = info_ref.shape[0] - 2
    tile = q_ref.shape[0] // tiles_time
    width_oks = (None, info_ref[tiles_time] == 1, info_ref[tiles_time + 1] == 1)

    def window(t):
        first = t - info_ref[t]
        base = jnp.clip(first, 0, tiles_time - 2)
        inside = [(base + step >= first) & (base + step <= first + 1) for step in range(2)]
        return pl.ds(pl.multiple_of(base * tile, tile), 2 * tile), inside

    refs = (own_ref, side_a_ref, side_b_ref)

    def score(t, side):
        rows, inside = window(t)
        scores = lax.dot_general(
            q_ref[t * tile : (t + 1) * tile, :],
            refs[side][0, rows, :],
            (((1,), (1,)), ((), ())),
            preferred_element_type=jnp.float32,
        )
        blocks, largest = [], None
        for step in range(2):
            allowed = inside[step] if side == 0 else inside[step] & width_oks[side]
            block = scores[:, step * tile : (step + 1) * tile]
            lanes = block[:, :HD]
            for start in range(HD, tile, HD):
                lanes = jnp.maximum(lanes, block[:, start : start + HD])
            lanes = jnp.where(allowed, lanes, -FAR)
            largest = lanes if largest is None else jnp.maximum(largest, lanes)
            blocks.append((block, allowed))
        return blocks, largest

    def blend(t, side, blocks, shift):
        rows, _ = window(t)
        weights = [
            jnp.exp2(block * EXP2_SCALE - jnp.where(allowed, shift, FAR)).astype(jnp.bfloat16)
            for block, allowed in blocks
        ]
        values = refs[side][1, rows, :]
        return jnp.dot(
            jnp.concatenate(weights, axis=1),
            jnp.concatenate([values, jnp.ones_like(values)], axis=1),
            preferred_element_type=jnp.float32,
        )

    ready = [score(first, side) for side in range(3)]
    for ref in earlier:
        out_ref[: first * tile, :] = ref[: first * tile, :]
    for t in range(first, last):
        row_max = jnp.maximum(jnp.maximum(ready[0][1], ready[1][1]), ready[2][1])
        shift = jnp.max(row_max, axis=1, keepdims=True) * EXP2_SCALE
        later, total = [], None
        for side in range(3):
            if t + 1 < last:
                later.append(score(t + 1, side))
            part = blend(t, side, ready[side][0], shift)
            total = part if total is None else total + part
        out_ref[t * tile : (t + 1) * tile, :] = (total[:, :HD] / total[:, HD:]).astype(jnp.bfloat16)
        ready = later


def pinned(operands):
    return [pltpu.with_memory_space_constraint(operand, pltpu.VMEM) for operand in operands]


def attention(info, tiles, *operands):
    return pl.pallas_call(
        functools.partial(attention_kernel, *tiles),
        out_shape=jax.ShapeDtypeStruct(operands[0].shape, jnp.bfloat16),
        in_specs=[SCALARS] + [IN_VMEM] * len(operands),
        out_specs=IN_VMEM,
        compiler_params=pltpu.CompilerParams(vmem_limit_bytes=VMEM_LIMIT),
        cost_estimate=SMALL_COST,
        name="attention",
    )(info, *pinned(operands))


def partial_kernel(first, kinds, tile, info_ref, *refs):
    w_refs, refs = refs[:2], refs[2:]
    *pieces, gate_ref, base_own_ref, base_other_ref, own_ref, other_ref = refs
    own_cols = own_ref.shape[1]
    frames = tile // FRAME
    cond_first = info_ref[0] == 0
    places = [pl.ds(pl.multiple_of(info_ref[i] * own_cols, own_cols), own_cols) for i in (1, 2)]
    chosen = [[i for i, kind in enumerate(kinds) if kind[0] == which] for which in range(2)]
    weights = []
    for names in chosen:
        blocks = []
        for _, far, head in [kinds[i] for i in names]:
            depth = slice(head * HD, (head + 1) * HD)
            blocks.append(jnp.concatenate([w_refs[far][depth, place] for place in places], axis=1))
        weights.append(jnp.concatenate(blocks, axis=0))
    for time_tile in range(own_ref.shape[0] // tile):
        token_rows = slice(time_tile * tile, (time_tile + 1) * tile)
        parts = []
        for which in range(2):
            attended = jnp.concatenate([pieces[i][token_rows, :] for i in chosen[which]], axis=1)
            projected = jnp.dot(attended, weights[which], preferred_element_type=jnp.float32)
            parts.append(gate_ref[which] * projected)
        for frame in range(frames):
            rows = slice(frame * FRAME, (frame + 1) * FRAME)
            out_rows = slice(time_tile * tile + rows.start, time_tile * tile + rows.stop)
            guide = 1.0 + 0.5 * info_ref[3 + time_tile * frames + frame].astype(jnp.float32)
            scales = (
                jnp.where(cond_first, guide, 1.0 - guide),
                jnp.where(cond_first, 1.0 - guide, guide),
            )
            total = scales[0] * parts[0][rows] + scales[1] * parts[1][rows]
            own, other = total[:, :own_cols], total[:, own_cols:]
            if first:
                own += scales[0] * base_own_ref[out_rows, :].astype(jnp.float32)
                own += scales[1] * base_other_ref[out_rows, :].astype(jnp.float32)
            else:
                own += base_own_ref[out_rows, :]
                other += base_other_ref[out_rows, :]
            own_ref[out_rows, :] = own
            other_ref[out_rows, :] = other.astype(other_ref.dtype)


def partial_projection(info, weights, pieces, gate, base, tile, first):
    shape = base[0].shape
    return pl.pallas_call(
        functools.partial(partial_kernel, first, tuple(pieces), tile),
        out_shape=[
            jax.ShapeDtypeStruct(shape, jnp.float32),
            jax.ShapeDtypeStruct(shape, jnp.float32 if first else jnp.bfloat16),
        ],
        in_specs=[SCALARS] + [IN_VMEM] * (len(weights) + len(pieces) + 3),
        out_specs=[IN_VMEM] * 2,
        compiler_params=pltpu.CompilerParams(vmem_limit_bytes=VMEM_LIMIT),
        cost_estimate=SMALL_COST,
        name="partial_projection",
    )(info, *pinned([*weights, *pieces.values()]), gate, *pinned(base))


def copy_kernel(plan, info_ref, *refs):
    *arrays, sems = refs
    copies = []
    for source, block, width, target, place in plan:
        src, dst = arrays[source], arrays[target]
        first = block * width
        if block < 0:
            first = pl.multiple_of(info_ref[block + info_ref.shape[0]] * width, width)
        for part in range(COPY_PARTS):
            size = src.shape[0] // COPY_PARTS
            rows = pl.ds(part * size, size)
            to = dst.at[rows, :] if place is None else dst.at[place, rows, :]
            copies.append((src.at[rows, pl.ds(first, width)], to))
    copies = [
        pltpu.make_async_copy(src, to, sems.at[index]) for index, (src, to) in enumerate(copies)
    ]
    for copy in copies:
        copy.start()
    for copy in copies:
        copy.wait()


def copy_columns(info, sources, plan, targets):
    return pl.pallas_call(
        functools.partial(copy_kernel, plan),
        out_shape=[jax.ShapeDtypeStruct(shape, jnp.bfloat16) for shape in targets],
        in_specs=[SCALARS] + [pl.BlockSpec(memory_space=pltpu.HBM)] * len(sources),
        out_specs=[IN_VMEM] * len(targets),
        scratch_shapes=[pltpu.SemaphoreType.DMA((COPY_PARTS * len(plan),))],
        compiler_params=pltpu.CompilerParams(vmem_limit_bytes=COPY_LIMIT),
        cost_estimate=SMALL_COST,
        name="copy_columns",
    )(info, *[pltpu.with_memory_space_constraint(source, pltpu.HBM) for source in sources])


def halves_kernel(info_ref, both_ref, mine_ref, other_ref, sems):
    copies = [
        pltpu.make_async_copy(both_ref.at[half], to, sems.at[index])
        for index, (half, to) in enumerate(((info_ref[0], mine_ref), (1 - info_ref[0], other_ref)))
    ]
    for copy in copies:
        copy.start()
    for copy in copies:
        copy.wait()


def split_halves(info, both):
    return pl.pallas_call(
        halves_kernel,
        out_shape=[jax.ShapeDtypeStruct(both.shape[1:], both.dtype)] * 2,
        in_specs=[SCALARS, pl.BlockSpec(memory_space=pl.ANY)],
        out_specs=[IN_VMEM] * 2,
        scratch_shapes=[pltpu.SemaphoreType.DMA((2,))],
        compiler_params=pltpu.CompilerParams(vmem_limit_bytes=COPY_LIMIT),
        cost_estimate=SMALL_COST,
        name="split_halves",
    )(info, both)


def local(queries, keys, values, residual, gate, out_weight, time_offsets, guidance_index):
    tiles_time, tiles_wide = time_offsets.shape
    count, features = queries.shape[1:]
    tile = count // tiles_time
    heads = features // HD
    head_count = lax.axis_size("head")
    columns = lax.axis_size("tokens")
    branch_pos = lax.axis_index("branch")
    head_pos = lax.axis_index("head")
    width_pos = lax.axis_index("tokens")
    width = gate.shape[2] // head_count

    rounds = [
        [pair for i in range(first, columns - 1, 2) for pair in ((i, i + 1), (i + 1, i))]
        for first in range(2)
    ]
    near_pos = (width_pos ^ 1, ((width_pos + 1) ^ 1) - 1)

    def swap(value, branch_bit, head_bits):
        if not branch_bit and not head_bits:
            return value
        if not head_bits:
            return lax.ppermute(value, "branch", [(0, 1), (1, 0)])
        if not branch_bit:
            return lax.ppermute(value, "head", [(i, i ^ head_bits) for i in range(head_count)])
        flip = head_count + head_bits
        return lax.ppermute(
            value, ("branch", "head"), [(i, i ^ flip) for i in range(2 * head_count)]
        )

    pair = head_pos >> 1
    branch_pair = branch_pos * (head_count // 2)
    copy_info = jnp.stack([branch_pair + pair, branch_pair + (pair ^ 1)])
    sources = (queries[0], keys[0], values[0], out_weight)
    key_value = [((1, 2), head, HD, (0, 1), (2, count, HD)) for head in range(heads)]
    query = [((0,), head, HD, (None,), (count, HD)) for head in range(heads)]
    pair_weight = [((3,), block, 2 * width, (None,), (features, 2 * width)) for block in (-2, -1)]

    def pack(parts, after=None):
        here = sources
        if after is not None:
            _, here = lax.optimization_barrier((after, sources))
        used = sorted({index for part in parts for index in part[0]})
        plan = [
            (used.index(source), block, cols, len(used) + target, place)
            for target, (froms, block, cols, places, _) in enumerate(parts)
            for source, place in zip(froms, places)
        ]
        return copy_columns(
            copy_info, [here[index] for index in used], plan, [part[-1] for part in parts]
        )

    def split_residual(residual):
        return split_halves(branch_pos[None], jnp.transpose(residual[0], (1, 0, 2)))

    packed = pack(key_value[:1])
    after = packed
    if RESIDUAL_AFTER == 0:
        _, residual = lax.optimization_barrier((packed, residual))
        mine, other = split_residual(residual)
        after = (packed, other) if RESIDUAL_FIRST else packed
    late_key_value, far = pack([key_value[1], pair_weight[1]], after)
    packed = list(packed) + [late_key_value]

    def halo(part):
        return [lax.ppermute(part, "tokens", pairs) for pairs in rounds]

    sides = [halo(part) for part in packed]
    near, *late = pack(pair_weight[:1] + query + key_value[2:], sides[0] if LATE_PACK else packed)
    head_queries, packed = late[:heads], packed + late[heads:]
    store = {"far": swap(far, 0, 2)}

    if RESIDUAL_AFTER:
        _, residual = lax.optimization_barrier(((packed[1], sides[0])[RESIDUAL_AFTER - 1], residual))
        mine, other = split_residual(residual)
    store["other"] = swap(other, 1, 0)
    gate_block = jnp.concatenate(
        [
            lax.dynamic_slice(gate, (0, branch_pos, place * width), (2, 1, width))
            for place in (head_pos, head_pos ^ 1)
        ],
        axis=2,
    ).astype(jnp.float32)
    gate_block = jnp.where(branch_pos == 0, gate_block, gate_block[::-1])

    offsets = lax.dynamic_index_in_dim(time_offsets, width_pos, 1, keepdims=False)
    edges = jnp.stack([(pos >= 0) & (pos < tiles_wide) for pos in near_pos]).astype(jnp.int32)
    attention_info = jnp.concatenate([offsets, edges])
    place = head_pos & 1
    projection_info = jnp.concatenate([jnp.stack([branch_pos, place, place ^ 1]), guidance_index])

    def relay(head):
        if RELAY[head] == "x":
            store[1, 1, head] = swap(store[0, 1, head], 1, 0)
        elif RELAY[head] == "y":
            store[1, 1, head] = swap(store[1, 0, head], 0, 2)
        else:
            store[1, 1, head] = swap(store[0, 0, head], 1, 2)

    def await_names(names, value):
        value, awaited = lax.optimization_barrier((value, [store[name] for name in names]))
        store.update(zip(names, awaited))
        return value

    for head in range(heads):
        head_queries[head] = await_names(AWAITED.get(head, ()), head_queries[head])
        operands = [head_queries[head], packed[head], *sides[head]]
        if head == heads - 1 and SPLIT:
            own = attention(attention_info, (0, SPLIT), *operands)
            own = await_names(AWAITED.get(heads, ()), own)
            own = attention(attention_info, (SPLIT, tiles_time), *operands, own)
        else:
            own = attention(attention_info, (0, tiles_time), *operands)
        if head + 2 < heads:
            own, part = lax.optimization_barrier((own, packed[head + 2]))
            sides.append(halo(part))
        store[0, 0, head] = own
        store[1, 0, head] = swap(await_names(BEFORE_X.get(head, ()), own), 1, 0)
        store[0, 1, head] = swap(await_names(BEFORE_Y.get(head, ()), own), 0, 2)
        if head < heads - 1:
            relay(head)

    names = [name for name in store if isinstance(name, tuple)]
    late = [name for name in names if name[2] == heads - 1 or name in LATE]
    base = (mine, store["other"])

    def partial(names, base):
        return partial_projection(
            projection_info,
            (near, store["far"]),
            {name: store[name] for name in names},
            gate_block,
            base,
            tile,
            base[0] is mine,
        )

    base = partial([name for name in names if name not in late], base)
    if TIE_PARTIAL:
        name = (1, 0, heads - 1) if RELAY[-1] == "y" else (0, 1, heads - 1)
        base, store[name] = lax.optimization_barrier((base, store[name]))
    relay(heads - 1)
    base = partial(late + [(1, 1, heads - 1)], base)
    return (base[0] + swap(base[1], 0, 1).astype(jnp.float32)).astype(jnp.bfloat16)


def solution(mesh):
    return jax.shard_map(
        local,
        mesh=mesh,
        in_specs=(
            P("branch", "tokens", "head"),
            P("branch", "tokens", "head"),
            P("branch", "tokens", "head"),
            P("branch", "tokens", None, "head"),
            P(),
            P("head", None),
            P(),
            P(),
        ),
        out_specs=P("tokens", ("branch", "head")),
        check_vma=False,
    )
```

```python
import functools
import math

import jax
import jax.numpy as jnp
from jax import lax
from jax.experimental import pallas as pl
from jax.experimental.pallas import tpu as pltpu
from jax.sharding import PartitionSpec as P

HD = 128
FRAME = 64
FAR = 1e30
EXP2_SCALE = math.log2(math.e) / math.sqrt(HD)
VMEM_LIMIT = 14 * 1024 * 1024
COPY_LIMIT = 2 * 1024 * 1024
COPY_PARTS = 3
RESIDUAL_FIRST = True
SPLIT = 0
TIE_PARTIAL = True
BEFORE_X = {1: (), 2: ()}
BEFORE_Y = {1: (), 2: ((1, 1, 0),)}
RESIDUAL_AFTER = 0
AWAITED = {0: (), 1: ('far', 'other', (0, 1, 0)), 2: ('far', 'other', (1, 0, 0), (0, 1, 0)), 3: ((1, 0, 1),)}
RELAY = ('x', 'y', 'x')
LATE = ((1, 1, 1),)
SCALARS = pl.BlockSpec(memory_space=pltpu.SMEM)
IN_VMEM = pl.BlockSpec(memory_space=pltpu.VMEM)
SMALL_COST = pl.CostEstimate(flops=0, bytes_accessed=1024, transcendentals=0)


def attention_kernel(first, last, info_ref, q_ref, own_ref, side_a_ref, side_b_ref, *refs):
    *earlier, out_ref = refs
    tiles_time = info_ref.shape[0] - 2
    tile = q_ref.shape[0] // tiles_time
    width_oks = (None, info_ref[tiles_time] == 1, info_ref[tiles_time + 1] == 1)

    def window(t):
        first = t - info_ref[t]
        base = jnp.clip(first, 0, tiles_time - 2)
        inside = [(base + step >= first) & (base + step <= first + 1) for step in range(2)]
        return pl.ds(pl.multiple_of(base * tile, tile), 2 * tile), inside

    refs = (own_ref, side_a_ref, side_b_ref)

    def score(t, side):
        rows, inside = window(t)
        scores = lax.dot_general(
            q_ref[t * tile : (t + 1) * tile, :],
            refs[side][0, rows, :],
            (((1,), (1,)), ((), ())),
            preferred_element_type=jnp.float32,
        )
        blocks, largest = [], None
        for step in range(2):
            allowed = inside[step] if side == 0 else inside[step] & width_oks[side]
            block = scores[:, step * tile : (step + 1) * tile]
            lanes = block[:, :HD]
            for start in range(HD, tile, HD):
                lanes = jnp.maximum(lanes, block[:, start : start + HD])
            lanes = jnp.where(allowed, lanes, -FAR)
            largest = lanes if largest is None else jnp.maximum(largest, lanes)
            blocks.append((block, allowed))
        return blocks, largest

    def blend(t, side, blocks, shift):
        rows, _ = window(t)
        weights = [
            jnp.exp2(block * EXP2_SCALE - jnp.where(allowed, shift, FAR)).astype(jnp.bfloat16)
            for block, allowed in blocks
        ]
        values = refs[side][1, rows, :]
        return jnp.dot(
            jnp.concatenate(weights, axis=1),
            jnp.concatenate([values, jnp.ones_like(values)], axis=1),
            preferred_element_type=jnp.float32,
        )

    ready = [score(first, side) for side in range(3)]
    for ref in earlier:
        out_ref[: first * tile, :] = ref[: first * tile, :]
    for t in range(first, last):
        row_max = jnp.maximum(jnp.maximum(ready[0][1], ready[1][1]), ready[2][1])
        shift = jnp.max(row_max, axis=1, keepdims=True) * EXP2_SCALE
        later, total = [], None
        for side in range(3):
            if t + 1 < last:
                later.append(score(t + 1, side))
            part = blend(t, side, ready[side][0], shift)
            total = part if total is None else total + part
        out_ref[t * tile : (t + 1) * tile, :] = (total[:, :HD] / total[:, HD:]).astype(jnp.bfloat16)
        ready = later


def in_hbm(operands):
    return [pltpu.with_memory_space_constraint(operand, pltpu.HBM) for operand in operands]


def pinned(operands):
    return [pltpu.with_memory_space_constraint(operand, pltpu.VMEM) for operand in operands]


def attention(info, tiles, *operands):
    return pl.pallas_call(
        functools.partial(attention_kernel, *tiles),
        out_shape=jax.ShapeDtypeStruct(operands[0].shape, jnp.bfloat16),
        in_specs=[SCALARS] + [IN_VMEM] * len(operands),
        out_specs=IN_VMEM,
        compiler_params=pltpu.CompilerParams(vmem_limit_bytes=VMEM_LIMIT),
        cost_estimate=SMALL_COST,
        name="attention",
    )(info, *pinned(operands))


def attention_copies_kernel(last, plan, source_count, info_ref, copy_info_ref, *refs):
    operands, sources = refs[:4], refs[4 : 4 + source_count]
    out_ref, targets, sems = refs[4 + source_count], refs[5 + source_count : -1], refs[-1]
    copies = planned_copies(plan, copy_info_ref, sources + targets, sems)
    for copy in copies:
        copy.start()
    attention_kernel(0, last, info_ref, *operands, out_ref)
    for copy in copies:
        copy.wait()


def attention_copies(info, last, operands, copy_info, sources, plan, targets):
    return pl.pallas_call(
        functools.partial(attention_copies_kernel, last, plan, len(sources)),
        out_shape=[
            jax.ShapeDtypeStruct(shape, jnp.bfloat16) for shape in [operands[0].shape] + targets
        ],
        in_specs=[SCALARS] * 2
        + [IN_VMEM] * len(operands)
        + [pl.BlockSpec(memory_space=pltpu.HBM)] * len(sources),
        out_specs=[IN_VMEM] * (1 + len(targets)),
        scratch_shapes=[pltpu.SemaphoreType.DMA((COPY_PARTS * len(plan),))],
        compiler_params=pltpu.CompilerParams(vmem_limit_bytes=VMEM_LIMIT),
        cost_estimate=SMALL_COST,
        name="attention_copies",
    )(info, copy_info, *pinned(operands), *in_hbm(sources))


def partial_kernel(first, kinds, tile, info_ref, *refs):
    w_refs, refs = refs[:2], refs[2:]
    *pieces, gate_ref, base_own_ref, base_other_ref, own_ref, other_ref = refs
    own_cols = own_ref.shape[1]
    frames = tile // FRAME
    cond_first = info_ref[0] == 0
    places = [pl.ds(pl.multiple_of(info_ref[i] * own_cols, own_cols), own_cols) for i in (1, 2)]
    gates = []
    for which in range(2):
        branch = info_ref[0] if which == 0 else 1 - info_ref[0]
        cols = []
        for place in (info_ref[3], info_ref[3] ^ 1):
            here = pl.ds(pl.multiple_of(place * own_cols, own_cols), own_cols)
            both = gate_ref[branch, :, here].astype(jnp.float32)
            cols.append(jnp.where(cond_first, both[0:1], both[1:2]))
        gates.append(jnp.concatenate(cols, axis=1))
    chosen = [[i for i, kind in enumerate(kinds) if kind[0] == which] for which in range(2)]
    weights = []
    for names in chosen:
        blocks = []
        for _, far, head in [kinds[i] for i in names]:
            depth = slice(head * HD, (head + 1) * HD)
            blocks.append(jnp.concatenate([w_refs[far][depth, place] for place in places], axis=1))
        weights.append(jnp.concatenate(blocks, axis=0))
    for time_tile in range(own_ref.shape[0] // tile):
        token_rows = slice(time_tile * tile, (time_tile + 1) * tile)
        parts = []
        for which in range(2):
            attended = jnp.concatenate([pieces[i][token_rows, :] for i in chosen[which]], axis=1)
            projected = jnp.dot(attended, weights[which], preferred_element_type=jnp.float32)
            parts.append(gates[which] * projected)
        for frame in range(frames):
            rows = slice(frame * FRAME, (frame + 1) * FRAME)
            out_rows = slice(time_tile * tile + rows.start, time_tile * tile + rows.stop)
            guide = 1.0 + 0.5 * info_ref[4 + time_tile * frames + frame].astype(jnp.float32)
            scales = (
                jnp.where(cond_first, guide, 1.0 - guide),
                jnp.where(cond_first, 1.0 - guide, guide),
            )
            total = scales[0] * parts[0][rows] + scales[1] * parts[1][rows]
            own, other = total[:, :own_cols], total[:, own_cols:]
            if first:
                own += scales[0] * base_own_ref[out_rows, :].astype(jnp.float32)
                own += scales[1] * base_other_ref[out_rows, :].astype(jnp.float32)
            else:
                own += base_own_ref[out_rows, :]
                other += base_other_ref[out_rows, :]
            own_ref[out_rows, :] = own
            other_ref[out_rows, :] = other.astype(other_ref.dtype)


def partial_projection(info, weights, pieces, gate, base, tile, first):
    shape = base[0].shape
    return pl.pallas_call(
        functools.partial(partial_kernel, first, tuple(pieces), tile),
        out_shape=[
            jax.ShapeDtypeStruct(shape, jnp.float32),
            jax.ShapeDtypeStruct(shape, jnp.float32 if first else jnp.bfloat16),
        ],
        in_specs=[SCALARS] + [IN_VMEM] * (len(weights) + len(pieces) + 3),
        out_specs=[IN_VMEM] * 2,
        compiler_params=pltpu.CompilerParams(vmem_limit_bytes=VMEM_LIMIT),
        cost_estimate=SMALL_COST,
        name="partial_projection",
    )(info, *pinned([*weights, *pieces.values()]), gate, *pinned(base))


def planned_copies(plan, info_ref, arrays, sems):
    copies = []
    for source, block, width, target, place in plan:
        src, dst = arrays[source], arrays[target]
        first = block * width
        if block < 0:
            first = pl.multiple_of(info_ref[block + info_ref.shape[0]] * width, width)
        for part in range(COPY_PARTS):
            size = src.shape[0] // COPY_PARTS
            rows = pl.ds(part * size, size)
            to = dst.at[rows, :] if place is None else dst.at[place, rows, :]
            copies.append((src.at[rows, pl.ds(first, width)], to))
    return [pltpu.make_async_copy(src, to, sems.at[i]) for i, (src, to) in enumerate(copies)]


def copy_kernel(plan, info_ref, *refs):
    copies = planned_copies(plan, info_ref, refs[:-1], refs[-1])
    for copy in copies:
        copy.start()
    for copy in copies:
        copy.wait()


def copy_columns(info, sources, plan, targets):
    return pl.pallas_call(
        functools.partial(copy_kernel, plan),
        out_shape=[jax.ShapeDtypeStruct(shape, jnp.bfloat16) for shape in targets],
        in_specs=[SCALARS] + [pl.BlockSpec(memory_space=pltpu.HBM)] * len(sources),
        out_specs=[IN_VMEM] * len(targets),
        scratch_shapes=[pltpu.SemaphoreType.DMA((COPY_PARTS * len(plan),))],
        compiler_params=pltpu.CompilerParams(vmem_limit_bytes=COPY_LIMIT),
        cost_estimate=SMALL_COST,
        name="copy_columns",
    )(info, *in_hbm(sources))


def halves_kernel(info_ref, both_ref, mine_ref, other_ref, sems):
    copies = [
        pltpu.make_async_copy(both_ref.at[half], to, sems.at[index])
        for index, (half, to) in enumerate(((info_ref[0], mine_ref), (1 - info_ref[0], other_ref)))
    ]
    for copy in copies:
        copy.start()
    for copy in copies:
        copy.wait()


def split_halves(info, both):
    return pl.pallas_call(
        halves_kernel,
        out_shape=[jax.ShapeDtypeStruct(both.shape[1:], both.dtype)] * 2,
        in_specs=[SCALARS, pl.BlockSpec(memory_space=pl.ANY)],
        out_specs=[IN_VMEM] * 2,
        scratch_shapes=[pltpu.SemaphoreType.DMA((2,))],
        compiler_params=pltpu.CompilerParams(vmem_limit_bytes=COPY_LIMIT),
        cost_estimate=SMALL_COST,
        name="split_halves",
    )(info, both)


def local(queries, keys, values, residual, gate, out_weight, time_offsets, guidance_index):
    tiles_time, tiles_wide = time_offsets.shape
    count, features = queries.shape[1:]
    tile = count // tiles_time
    heads = features // HD
    head_count = lax.axis_size("head")
    columns = lax.axis_size("tokens")
    branch_pos = lax.axis_index("branch")
    head_pos = lax.axis_index("head")
    width_pos = lax.axis_index("tokens")
    width = gate.shape[2] // head_count

    rounds = [
        [pair for i in range(first, columns - 1, 2) for pair in ((i, i + 1), (i + 1, i))]
        for first in range(2)
    ]
    near_pos = (width_pos ^ 1, ((width_pos + 1) ^ 1) - 1)

    def swap(value, branch_bit, head_bits):
        if not branch_bit and not head_bits:
            return value
        if not head_bits:
            return lax.ppermute(value, "branch", [(0, 1), (1, 0)])
        if not branch_bit:
            return lax.ppermute(value, "head", [(i, i ^ head_bits) for i in range(head_count)])
        flip = head_count + head_bits
        return lax.ppermute(
            value, ("branch", "head"), [(i, i ^ flip) for i in range(2 * head_count)]
        )

    pair = head_pos >> 1
    branch_pair = branch_pos * (head_count // 2)
    copy_info = jnp.stack([branch_pair + pair, branch_pair + (pair ^ 1)])
    sources = (queries[0], keys[0], values[0], out_weight)
    key_value = [((1, 2), head, HD, (0, 1), (2, count, HD)) for head in range(heads)]
    query = [((0,), head, HD, (None,), (count, HD)) for head in range(heads)]
    pair_weight = [((3,), block, 2 * width, (None,), (features, 2 * width)) for block in (-2, -1)]

    def plan_of(parts):
        used = sorted({index for part in parts for index in part[0]})
        plan = [
            (used.index(source), block, cols, len(used) + target, place)
            for target, (froms, block, cols, places, _) in enumerate(parts)
            for source, place in zip(froms, places)
        ]
        return used, plan, [part[-1] for part in parts]

    def pack(parts, after=None):
        here = sources
        if after is not None:
            _, here = lax.optimization_barrier((after, sources))
        used, plan, targets = plan_of(parts)
        return copy_columns(copy_info, [here[index] for index in used], plan, targets)

    def split_residual(residual):
        return split_halves(branch_pos[None], jnp.transpose(residual[0], (1, 0, 2)))

    packed = pack(key_value[:1])
    after = packed
    if RESIDUAL_AFTER == 0:
        _, residual = lax.optimization_barrier((packed, residual))
        mine, other = split_residual(residual)
        after = (packed, other) if RESIDUAL_FIRST else packed
    late_key_value, far, first_query = pack([key_value[1], pair_weight[1], query[0]], after)
    packed = list(packed) + [late_key_value]
    head_queries = [first_query]

    def halo(part):
        return [lax.ppermute(part, "tokens", pairs) for pairs in rounds]

    sides = [halo(part) for part in packed]
    store = {"far": swap(far, 0, 2)}

    if RESIDUAL_AFTER:
        _, residual = lax.optimization_barrier(((packed[1], sides[0])[RESIDUAL_AFTER - 1], residual))
        mine, other = split_residual(residual)
    store["other"] = swap(other, 1, 0)
    offsets = lax.dynamic_index_in_dim(time_offsets, width_pos, 1, keepdims=False)
    edges = jnp.stack([(pos >= 0) & (pos < tiles_wide) for pos in near_pos]).astype(jnp.int32)
    attention_info = jnp.concatenate([offsets, edges])
    place = head_pos & 1
    projection_info = jnp.concatenate([jnp.stack([branch_pos, place, place ^ 1, head_pos]), guidance_index])

    def relay(head):
        if RELAY[head] == "x":
            store[1, 1, head] = swap(store[0, 1, head], 1, 0)
        elif RELAY[head] == "y":
            store[1, 1, head] = swap(store[1, 0, head], 0, 2)
        else:
            store[1, 1, head] = swap(store[0, 0, head], 1, 2)

    def await_names(names, value):
        value, awaited = lax.optimization_barrier((value, [store[name] for name in names]))
        store.update(zip(names, awaited))
        return value

    for head in range(heads):
        head_queries[head] = await_names(AWAITED.get(head, ()), head_queries[head])
        operands = [head_queries[head], packed[head], *sides[head]]
        if head == 0:
            used, plan, targets = plan_of(pair_weight[:1] + query[1:] + key_value[2:])
            own, near, *late = attention_copies(
                attention_info,
                tiles_time,
                operands,
                copy_info,
                [sources[index] for index in used],
                plan,
                targets,
            )
            head_queries, packed = head_queries + late[: heads - 1], packed + late[heads - 1 :]
        elif head == heads - 1 and SPLIT:
            own = attention(attention_info, (0, SPLIT), *operands)
            own = await_names(AWAITED.get(heads, ()), own)
            own = attention(attention_info, (SPLIT, tiles_time), *operands, own)
        else:
            own = attention(attention_info, (0, tiles_time), *operands)
        if head + 2 < heads:
            sides.append(halo(packed[head + 2]))
        store[0, 0, head] = own
        store[1, 0, head] = swap(await_names(BEFORE_X.get(head, ()), own), 1, 0)
        store[0, 1, head] = swap(await_names(BEFORE_Y.get(head, ()), own), 0, 2)
        if head < heads - 1:
            relay(head)

    names = [name for name in store if isinstance(name, tuple)]
    late = [name for name in names if name[2] == heads - 1 or name in LATE]
    base = (mine, store["other"])

    def partial(names, base):
        return partial_projection(
            projection_info,
            (near, store["far"]),
            {name: store[name] for name in names},
            gate,
            base,
            tile,
            base[0] is mine,
        )

    base = partial([name for name in names if name not in late], base)
    if TIE_PARTIAL:
        name = (1, 0, heads - 1) if RELAY[-1] == "y" else (0, 1, heads - 1)
        base, store[name] = lax.optimization_barrier((base, store[name]))
    relay(heads - 1)
    base = partial(late + [(1, 1, heads - 1)], base)
    return (base[0] + swap(base[1], 0, 1).astype(jnp.float32)).astype(jnp.bfloat16)


def solution(mesh):
    return jax.shard_map(
        local,
        mesh=mesh,
        in_specs=(
            P("branch", "tokens", "head"),
            P("branch", "tokens", "head"),
            P("branch", "tokens", "head"),
            P("branch", "tokens", None, "head"),
            P(),
            P("head", None),
            P(),
            P(),
        ),
        out_specs=P("tokens", ("branch", "head")),
        check_vma=False,
    )
```

```python
import functools
import math

import jax
import jax.numpy as jnp
from jax import lax
from jax.experimental import pallas as pl
from jax.experimental.pallas import tpu as pltpu
from jax.sharding import PartitionSpec as P

HD = 128
FRAME = 64
FAR = 1e30
EXP2_SCALE = math.log2(math.e) / math.sqrt(HD)
VMEM_LIMIT = 10 * 1024 * 1024
COPY_LIMIT = 2 * 1024 * 1024
COPY_PARTS = 3
RESIDUAL_FIRST = True
SPLIT = 0
INFO_HEAD = 6
TIE_PARTIAL = True
BEFORE_X = {1: (), 2: ()}
BEFORE_Y = {1: (), 2: ((1, 1, 0),)}
RESIDUAL_AFTER = 0
AWAITED = {0: (), 1: ('far', 'other', (0, 1, 0)), 2: ('far', 'other', (1, 0, 0), (0, 1, 0)), 3: ((1, 0, 1),)}
RELAY = ('x', 'y', 'x')
LATE = ((1, 1, 1),)
SCALARS = pl.BlockSpec(memory_space=pltpu.SMEM)
IN_VMEM = pl.BlockSpec(memory_space=pltpu.VMEM)
SMALL_COST = pl.CostEstimate(flops=0, bytes_accessed=1024, transcendentals=0)


def attention_kernel(first, last, info_ref, q_ref, own_ref, side_a_ref, side_b_ref, *refs):
    *earlier, out_ref = refs
    tiles_time = info_ref.shape[0] - 2
    tile = q_ref.shape[0] // tiles_time
    width_oks = (None, info_ref[tiles_time] == 1, info_ref[tiles_time + 1] == 1)

    def window(t):
        first = t - info_ref[t]
        base = jnp.clip(first, 0, tiles_time - 2)
        inside = [(base + step >= first) & (base + step <= first + 1) for step in range(2)]
        return pl.ds(pl.multiple_of(base * tile, tile), 2 * tile), inside

    refs = (own_ref, side_a_ref, side_b_ref)

    def score(t, side):
        rows, inside = window(t)
        scores = lax.dot_general(
            q_ref[t * tile : (t + 1) * tile, :],
            refs[side][0, rows, :],
            (((1,), (1,)), ((), ())),
            preferred_element_type=jnp.float32,
        )
        blocks, largest = [], None
        for step in range(2):
            allowed = inside[step] if side == 0 else inside[step] & width_oks[side]
            block = scores[:, step * tile : (step + 1) * tile]
            lanes = block[:, :HD]
            for start in range(HD, tile, HD):
                lanes = jnp.maximum(lanes, block[:, start : start + HD])
            lanes = jnp.where(allowed, lanes, -FAR)
            largest = lanes if largest is None else jnp.maximum(largest, lanes)
            blocks.append((block, allowed))
        return blocks, largest

    def blend(t, side, blocks, shift):
        rows, _ = window(t)
        weights = [
            jnp.exp2(block * EXP2_SCALE - jnp.where(allowed, shift, FAR)).astype(jnp.bfloat16)
            for block, allowed in blocks
        ]
        values = refs[side][1, rows, :]
        return jnp.dot(
            jnp.concatenate(weights, axis=1),
            jnp.concatenate([values, jnp.ones_like(values)], axis=1),
            preferred_element_type=jnp.float32,
        )

    ready = [score(first, side) for side in range(3)]
    for ref in earlier:
        out_ref[: first * tile, :] = ref[: first * tile, :]
    for t in range(first, last):
        row_max = jnp.maximum(jnp.maximum(ready[0][1], ready[1][1]), ready[2][1])
        shift = jnp.max(row_max, axis=1, keepdims=True) * EXP2_SCALE
        later, total = [], None
        for side in range(3):
            if t + 1 < last:
                later.append(score(t + 1, side))
            part = blend(t, side, ready[side][0], shift)
            total = part if total is None else total + part
        out_ref[t * tile : (t + 1) * tile, :] = (total[:, :HD] / total[:, HD:]).astype(jnp.bfloat16)
        ready = later


def in_hbm(operands):
    return [pltpu.with_memory_space_constraint(operand, pltpu.HBM) for operand in operands]


def pinned(operands):
    return [pltpu.with_memory_space_constraint(operand, pltpu.VMEM) for operand in operands]


def attention(info, tiles, *operands):
    return pl.pallas_call(
        functools.partial(attention_kernel, *tiles),
        out_shape=jax.ShapeDtypeStruct(operands[0].shape, jnp.bfloat16),
        in_specs=[SCALARS] + [IN_VMEM] * len(operands),
        out_specs=IN_VMEM,
        compiler_params=pltpu.CompilerParams(vmem_limit_bytes=VMEM_LIMIT),
        cost_estimate=SMALL_COST,
        name="attention",
    )(info, *pinned(operands))


def attention_copies_kernel(last, plan, source_count, info_ref, copy_info_ref, *refs):
    operands, sources = refs[:4], refs[4 : 4 + source_count]
    out_ref, targets, sems = refs[4 + source_count], refs[5 + source_count : -1], refs[-1]
    copies = planned_copies(plan, copy_info_ref, sources + targets, sems)
    for copy in copies:
        copy.start()
    attention_kernel(0, last, info_ref, *operands, out_ref)
    for copy in copies:
        copy.wait()


def attention_copies(info, last, operands, copy_info, sources, plan, targets):
    return pl.pallas_call(
        functools.partial(attention_copies_kernel, last, plan, len(sources)),
        out_shape=[
            jax.ShapeDtypeStruct(shape, jnp.bfloat16) for shape in [operands[0].shape] + targets
        ],
        in_specs=[SCALARS] * 2
        + [IN_VMEM] * len(operands)
        + [pl.BlockSpec(memory_space=pltpu.HBM)] * len(sources),
        out_specs=[IN_VMEM] * (1 + len(targets)),
        scratch_shapes=[pltpu.SemaphoreType.DMA((COPY_PARTS * len(plan),))],
        compiler_params=pltpu.CompilerParams(vmem_limit_bytes=VMEM_LIMIT),
        cost_estimate=SMALL_COST,
        name="attention_copies",
    )(info, copy_info, *pinned(operands), *in_hbm(sources))


def guided_share(info_ref, gate_ref, cols, frames, time_tile, attended, weights):
    cond_first = info_ref[0] == 0
    parts = []
    for which in range(2):
        branch = info_ref[0] if which == 0 else 1 - info_ref[0]
        gates = []
        for place in (info_ref[3], info_ref[3] ^ 1):
            both = gate_ref[branch, :, pl.ds(pl.multiple_of(place * cols, cols), cols)]
            both = both.astype(jnp.float32)
            gates.append(jnp.where(cond_first, both[0:1], both[1:2]))
        projected = jnp.dot(attended[which], weights[which], preferred_element_type=jnp.float32)
        parts.append(jnp.concatenate(gates, axis=1) * projected)
    for frame in range(frames):
        rows = slice(frame * FRAME, (frame + 1) * FRAME)
        guide = 1.0 + 0.5 * info_ref[INFO_HEAD + time_tile * frames + frame].astype(jnp.float32)
        scales = (jnp.where(cond_first, guide, 1.0 - guide), jnp.where(cond_first, 1.0 - guide, guide))
        yield rows, scales, scales[0] * parts[0][rows] + scales[1] * parts[1][rows]


def weight_rows(blocks, kinds):
    return [blocks[far][head * HD : (head + 1) * HD] for _, far, head in kinds]


def first_kernel(kinds, late, info_ref, near_own_ref, near_other_ref, far_ref, *refs):
    *pieces, gate_ref, mine_ref, other_ref, own_ref, partner_ref, late_ref = refs
    tile, cols = own_ref.shape
    places = [pl.ds(pl.multiple_of(info_ref[i] * cols, cols), cols) for i in (1, 2)]
    blocks = [
        jnp.concatenate([near_own_ref[...], near_other_ref[...]], axis=1),
        jnp.concatenate([far_ref[:, place] for place in places], axis=1),
    ]

    @pl.when(pl.program_id(0) == 0)
    def _():
        late_ref[...] = jnp.concatenate(weight_rows(blocks, late), axis=0)

    attended, weights = [], []
    for which in range(2):
        chosen = [i for i, kind in enumerate(kinds) if kind[0] == which]
        attended.append(jnp.concatenate([pieces[i][...] for i in chosen], axis=1))
        weights.append(jnp.concatenate(weight_rows(blocks, [kinds[i] for i in chosen]), axis=0))
    for rows, scales, total in guided_share(
        info_ref, gate_ref, cols, tile // FRAME, pl.program_id(0), attended, weights
    ):
        own = total[:, :cols]
        own += scales[0] * mine_ref[rows, :].astype(jnp.float32)
        own += scales[1] * other_ref[rows, :].astype(jnp.float32)
        own_ref[rows, :] = own
        partner_ref[rows, :] = total[:, cols:]


def first_share(info, weight, far, pieces, gate, halves, other, late, tile):
    count, cols = other.shape
    features = weight.shape[0]
    piece = pl.BlockSpec((tile, HD), lambda t, info: (t, 0))
    rows = pl.BlockSpec((tile, cols), lambda t, info: (t, 0))
    near = [
        pl.BlockSpec((features, cols), lambda t, info, place=place: (0, info[place]))
        for place in (4, 5)
    ]
    late_shape = (len(late) * HD, 2 * cols)
    operands = in_hbm([weight, weight]) + pinned([far, *pieces.values()])
    operands += [gate, *in_hbm([halves]), *pinned([other])]
    return pl.pallas_call(
        functools.partial(first_kernel, tuple(pieces), late),
        out_shape=[
            pltpu.VMEM((count, cols), jnp.float32),
            pltpu.VMEM((count, cols), jnp.float32),
            pltpu.VMEM(late_shape, jnp.bfloat16),
        ],
        grid_spec=pltpu.PrefetchScalarGridSpec(
            num_scalar_prefetch=1,
            grid=(count // tile,),
            in_specs=near
            + [pl.BlockSpec(far.shape, lambda t, info: (0, 0))]
            + [piece] * len(pieces)
            + [
                pl.BlockSpec(gate.shape, lambda t, info: (0, 0, 0)),
                pl.BlockSpec((None, tile, cols), lambda t, info: (info[0], t, 0)),
                rows,
            ],
            out_specs=[rows, rows, pl.BlockSpec(late_shape, lambda t, info: (0, 0))],
        ),
        compiler_params=pltpu.CompilerParams(vmem_limit_bytes=VMEM_LIMIT),
        cost_estimate=SMALL_COST,
        name="first_share",
    )(info, *operands)


def last_kernel(chosen, tile, info_ref, w_ref, *refs):
    *pieces, gate_ref, base_own_ref, base_partner_ref, own_ref, partner_ref = refs
    cols = own_ref.shape[1]
    weights = [
        jnp.concatenate([w_ref[at * HD : (at + 1) * HD, :] for _, at in names], axis=0)
        for names in chosen
    ]
    for time_tile in range(own_ref.shape[0] // tile):
        first = time_tile * tile
        attended = [
            jnp.concatenate([pieces[i][first : first + tile, :] for i, _ in names], axis=1)
            for names in chosen
        ]
        for rows, _, total in guided_share(
            info_ref, gate_ref, cols, tile // FRAME, time_tile, attended, weights
        ):
            to = slice(first + rows.start, first + rows.stop)
            own_ref[to, :] = base_own_ref[to, :] + total[:, :cols]
            partner_ref[to, :] = (base_partner_ref[to, :] + total[:, cols:]).astype(jnp.bfloat16)


def last_share(info, weights, pieces, gate, base, late, tile):
    shape = base[0].shape
    chosen = [
        [
            (i, [kind[1:] for kind in late].index(kind[1:]))
            for i, kind in enumerate(pieces)
            if kind[0] == which
        ]
        for which in range(2)
    ]
    return pl.pallas_call(
        functools.partial(last_kernel, chosen, tile),
        out_shape=[
            jax.ShapeDtypeStruct(shape, jnp.float32),
            jax.ShapeDtypeStruct(shape, jnp.bfloat16),
        ],
        in_specs=[SCALARS] + [IN_VMEM] * (len(pieces) + 4),
        out_specs=[IN_VMEM] * 2,
        compiler_params=pltpu.CompilerParams(vmem_limit_bytes=VMEM_LIMIT),
        cost_estimate=SMALL_COST,
        name="last_share",
    )(info, *pinned([weights, *pieces.values()]), gate, *pinned(base))


def planned_copies(plan, info_ref, arrays, sems):
    copies = []
    for source, block, width, target, place in plan:
        src, dst = arrays[source], arrays[target]
        first = block * width
        if block < 0:
            first = pl.multiple_of(info_ref[block + info_ref.shape[0]] * width, width)
        for part in range(COPY_PARTS):
            size = src.shape[0] // COPY_PARTS
            rows = pl.ds(part * size, size)
            to = dst.at[rows, :] if place is None else dst.at[place, rows, :]
            copies.append((src.at[rows, pl.ds(first, width)], to))
    return [pltpu.make_async_copy(src, to, sems.at[i]) for i, (src, to) in enumerate(copies)]


def copy_kernel(plan, info_ref, *refs):
    copies = planned_copies(plan, info_ref, refs[:-1], refs[-1])
    for copy in copies:
        copy.start()
    for copy in copies:
        copy.wait()


def copy_columns(info, sources, plan, targets):
    return pl.pallas_call(
        functools.partial(copy_kernel, plan),
        out_shape=[jax.ShapeDtypeStruct(shape, jnp.bfloat16) for shape in targets],
        in_specs=[SCALARS] + [pl.BlockSpec(memory_space=pltpu.HBM)] * len(sources),
        out_specs=[IN_VMEM] * len(targets),
        scratch_shapes=[pltpu.SemaphoreType.DMA((COPY_PARTS * len(plan),))],
        compiler_params=pltpu.CompilerParams(vmem_limit_bytes=COPY_LIMIT),
        cost_estimate=SMALL_COST,
        name="copy_columns",
    )(info, *in_hbm(sources))


def half_kernel(info_ref, both_ref, out_ref, sem):
    copy = pltpu.make_async_copy(both_ref.at[1 - info_ref[0]], out_ref, sem.at[0])
    copy.start()
    copy.wait()


def other_half(info, both):
    return pl.pallas_call(
        half_kernel,
        out_shape=jax.ShapeDtypeStruct(both.shape[1:], both.dtype),
        in_specs=[SCALARS, pl.BlockSpec(memory_space=pltpu.HBM)],
        out_specs=IN_VMEM,
        scratch_shapes=[pltpu.SemaphoreType.DMA((1,))],
        compiler_params=pltpu.CompilerParams(vmem_limit_bytes=COPY_LIMIT),
        cost_estimate=SMALL_COST,
        name="other_half",
    )(info, *in_hbm([both]))


def local(queries, keys, values, residual, gate, out_weight, time_offsets, guidance_index):
    tiles_time, tiles_wide = time_offsets.shape
    count, features = queries.shape[1:]
    tile = count // tiles_time
    heads = features // HD
    head_count = lax.axis_size("head")
    columns = lax.axis_size("tokens")
    branch_pos = lax.axis_index("branch")
    head_pos = lax.axis_index("head")
    width_pos = lax.axis_index("tokens")
    width = gate.shape[2] // head_count

    rounds = [
        [pair for i in range(first, columns - 1, 2) for pair in ((i, i + 1), (i + 1, i))]
        for first in range(2)
    ]
    near_pos = (width_pos ^ 1, ((width_pos + 1) ^ 1) - 1)

    def swap(value, branch_bit, head_bits):
        if not branch_bit and not head_bits:
            return value
        if not head_bits:
            return lax.ppermute(value, "branch", [(0, 1), (1, 0)])
        if not branch_bit:
            return lax.ppermute(value, "head", [(i, i ^ head_bits) for i in range(head_count)])
        flip = head_count + head_bits
        return lax.ppermute(
            value, ("branch", "head"), [(i, i ^ flip) for i in range(2 * head_count)]
        )

    pair = head_pos >> 1
    branch_pair = branch_pos * (head_count // 2)
    copy_info = jnp.stack([branch_pair + pair, branch_pair + (pair ^ 1)])
    sources = (queries[0], keys[0], values[0], out_weight)
    key_value = [((1, 2), head, HD, (0, 1), (2, count, HD)) for head in range(heads)]
    query = [((0,), head, HD, (None,), (count, HD)) for head in range(heads)]
    pair_weight = [((3,), block, 2 * width, (None,), (features, 2 * width)) for block in (-2, -1)]

    def plan_of(parts):
        used = sorted({index for part in parts for index in part[0]})
        plan = [
            (used.index(source), block, cols, len(used) + target, place)
            for target, (froms, block, cols, places, _) in enumerate(parts)
            for source, place in zip(froms, places)
        ]
        return used, plan, [part[-1] for part in parts]

    def pack(parts, after=None):
        here = sources
        if after is not None:
            _, here = lax.optimization_barrier((after, sources))
        used, plan, targets = plan_of(parts)
        return copy_columns(copy_info, [here[index] for index in used], plan, targets)

    def split_residual(residual):
        both = jnp.transpose(residual[0], (1, 0, 2))
        return both, other_half(branch_pos[None], both)

    packed = pack(key_value[:1])
    after = packed
    if RESIDUAL_AFTER == 0:
        _, residual = lax.optimization_barrier((packed, residual))
        halves, other = split_residual(residual)
        after = (packed, other) if RESIDUAL_FIRST else packed
    late_key_value, far, first_query = pack([key_value[1], pair_weight[1], query[0]], after)
    packed = list(packed) + [late_key_value]
    head_queries = [first_query]

    def halo(part):
        return [lax.ppermute(part, "tokens", pairs) for pairs in rounds]

    sides = [halo(part) for part in packed]
    store = {"far": swap(far, 0, 2)}

    if RESIDUAL_AFTER:
        _, residual = lax.optimization_barrier(((packed[1], sides[0])[RESIDUAL_AFTER - 1], residual))
        halves, other = split_residual(residual)
    store["other"] = swap(other, 1, 0)
    offsets = lax.dynamic_index_in_dim(time_offsets, width_pos, 1, keepdims=False)
    edges = jnp.stack([(pos >= 0) & (pos < tiles_wide) for pos in near_pos]).astype(jnp.int32)
    attention_info = jnp.concatenate([offsets, edges])
    place = head_pos & 1
    block = branch_pos * head_count + head_pos
    places = [branch_pos, place, place ^ 1, head_pos, block, block ^ 1]
    projection_info = jnp.concatenate([jnp.stack(places), guidance_index])

    def relay(head):
        if RELAY[head] == "x":
            store[1, 1, head] = swap(store[0, 1, head], 1, 0)
        elif RELAY[head] == "y":
            store[1, 1, head] = swap(store[1, 0, head], 0, 2)
        else:
            store[1, 1, head] = swap(store[0, 0, head], 1, 2)

    def await_names(names, value):
        value, awaited = lax.optimization_barrier((value, [store[name] for name in names]))
        store.update(zip(names, awaited))
        return value

    for head in range(heads):
        head_queries[head] = await_names(AWAITED.get(head, ()), head_queries[head])
        operands = [head_queries[head], packed[head], *sides[head]]
        if head == 0:
            used, plan, targets = plan_of(query[1:] + key_value[2:])
            own, *late = attention_copies(
                attention_info,
                tiles_time,
                operands,
                copy_info,
                [sources[index] for index in used],
                plan,
                targets,
            )
            head_queries, packed = head_queries + late[: heads - 1], packed + late[heads - 1 :]
        elif head == heads - 1 and SPLIT:
            own = attention(attention_info, (0, SPLIT), *operands)
            own = await_names(AWAITED.get(heads, ()), own)
            own = attention(attention_info, (SPLIT, tiles_time), *operands, own)
        else:
            own = attention(attention_info, (0, tiles_time), *operands)
        if head + 2 < heads:
            sides.append(halo(packed[head + 2]))
        store[0, 0, head] = own
        store[1, 0, head] = swap(await_names(BEFORE_X.get(head, ()), own), 1, 0)
        store[0, 1, head] = swap(await_names(BEFORE_Y.get(head, ()), own), 0, 2)
        if head < heads - 1:
            relay(head)

    names = [name for name in store if isinstance(name, tuple)]
    late = [name for name in names if name[2] == heads - 1 or name in LATE]
    late_rows = [(0, 0, heads - 1), (0, 1, heads - 1)]
    late_rows += [(0,) + name[1:] for name in LATE]
    *base, late_weights = first_share(
        projection_info,
        out_weight,
        store["far"],
        {name: store[name] for name in names if name not in late},
        gate,
        halves,
        store["other"],
        tuple(late_rows),
        tile,
    )
    if TIE_PARTIAL:
        name = (1, 0, heads - 1) if RELAY[-1] == "y" else (0, 1, heads - 1)
        base, store[name] = lax.optimization_barrier((base, store[name]))
    relay(heads - 1)
    pieces = {name: store[name] for name in late + [(1, 1, heads - 1)]}
    base = last_share(projection_info, late_weights, pieces, gate, base, late_rows, tile)
    return (base[0] + swap(base[1], 0, 1).astype(jnp.float32)).astype(jnp.bfloat16)


def solution(mesh):
    return jax.shard_map(
        local,
        mesh=mesh,
        in_specs=(
            P("branch", "tokens", "head"),
            P("branch", "tokens", "head"),
            P("branch", "tokens", "head"),
            P("branch", "tokens", None, "head"),
            P(),
            P("head", None),
            P(),
            P(),
        ),
        out_specs=P("tokens", ("branch", "head")),
        check_vma=False,
    )
```

```python
import functools
import math

import jax
import jax.numpy as jnp
from jax import lax
from jax.experimental import pallas as pl
from jax.experimental.pallas import tpu as pltpu
from jax.sharding import PartitionSpec as P

HD = 128
FRAME = 64
FAR = 1e30
EXP2_SCALE = math.log2(math.e) / math.sqrt(HD)
VMEM_LIMIT = 14 * 1024 * 1024
COPY_LIMIT = 8 * 1024 * 1024
COPY_PARTS = 3
LATE_PACK = True
RESIDUAL_FIRST = True
SPLIT = 0
TIE_PARTIAL = True
BEFORE_X = {1: (), 2: ()}
BEFORE_Y = {1: (), 2: ()}
RESIDUAL_AFTER = 0
AWAITED = {0: (), 1: ('far', 'other'), 2: ('far', 'other', (1, 0, 0), (0, 1, 0)), 3: ((1, 0, 1),)}
RELAY = ('y', 'x', 'y')
LATE = ((1, 1, 1),)
SCALARS = pl.BlockSpec(memory_space=pltpu.SMEM)
IN_VMEM = pl.BlockSpec(memory_space=pltpu.VMEM)
SMALL_COST = pl.CostEstimate(flops=0, bytes_accessed=1024, transcendentals=0)


def attention_kernel(first, last, info_ref, q_ref, own_ref, side_a_ref, side_b_ref, *refs):
    *earlier, out_ref, turned_ref = refs
    tiles_time = info_ref.shape[0] - 2
    tile = q_ref.shape[0] // tiles_time
    width_oks = (None, info_ref[tiles_time] == 1, info_ref[tiles_time + 1] == 1)

    def window(t):
        first = t - info_ref[t]
        base = jnp.clip(first, 0, tiles_time - 2)
        inside = [(base + step >= first) & (base + step <= first + 1) for step in range(2)]
        return pl.ds(pl.multiple_of(base * tile, tile), 2 * tile), inside

    refs = (own_ref, side_a_ref, side_b_ref)
    for side, ref in enumerate(refs):
        turned_ref[side] = ref[0].T

    def score(t, side):
        rows, inside = window(t)
        scores = jnp.dot(
            q_ref[t * tile : (t + 1) * tile, :],
            turned_ref[side, :, rows],
            preferred_element_type=jnp.float32,
        )
        blocks, largest = [], None
        for step in range(2):
            allowed = inside[step] if side == 0 else inside[step] & width_oks[side]
            block = scores[:, step * tile : (step + 1) * tile]
            lanes = block[:, :HD]
            for start in range(HD, tile, HD):
                lanes = jnp.maximum(lanes, block[:, start : start + HD])
            lanes = jnp.where(allowed, lanes, -FAR)
            largest = lanes if largest is None else jnp.maximum(largest, lanes)
            blocks.append((block, allowed))
        return blocks, largest

    def blend(t, side, blocks, shift):
        rows, _ = window(t)
        weights = [
            jnp.exp2(block * EXP2_SCALE - jnp.where(allowed, shift, FAR)).astype(jnp.bfloat16)
            for block, allowed in blocks
        ]
        values = refs[side][1, rows, :]
        return jnp.dot(
            jnp.concatenate(weights, axis=1),
            jnp.concatenate([values, jnp.ones_like(values)], axis=1),
            preferred_element_type=jnp.float32,
        )

    ready = [score(first, side) for side in range(3)]
    for ref in earlier:
        out_ref[: first * tile, :] = ref[: first * tile, :]
    for t in range(first, last):
        row_max = jnp.maximum(jnp.maximum(ready[0][1], ready[1][1]), ready[2][1])
        shift = jnp.max(row_max, axis=1, keepdims=True) * EXP2_SCALE
        later, total = [], None
        for side in range(3):
            if t + 1 < last:
                later.append(score(t + 1, side))
            part = blend(t, side, ready[side][0], shift)
            total = part if total is None else total + part
        out_ref[t * tile : (t + 1) * tile, :] = (total[:, :HD] / total[:, HD:]).astype(jnp.bfloat16)
        ready = later


def pinned(operands):
    return [pltpu.with_memory_space_constraint(operand, pltpu.VMEM) for operand in operands]


def attention(info, tiles, *operands):
    return pl.pallas_call(
        functools.partial(attention_kernel, *tiles),
        out_shape=jax.ShapeDtypeStruct(operands[0].shape, jnp.bfloat16),
        in_specs=[SCALARS] + [IN_VMEM] * len(operands),
        out_specs=IN_VMEM,
        scratch_shapes=[pltpu.VMEM((3,) + operands[0].shape[::-1], jnp.bfloat16)],
        compiler_params=pltpu.CompilerParams(vmem_limit_bytes=VMEM_LIMIT),
        cost_estimate=SMALL_COST,
        name="attention",
    )(info, *pinned(operands))


def partial_kernel(first, kinds, tile, info_ref, *refs):
    w_refs, refs = refs[:2], refs[2:]
    *pieces, gate_ref, base_own_ref, base_other_ref, own_ref, other_ref = refs
    own_cols = own_ref.shape[1]
    frames = tile // FRAME
    cond_first = info_ref[0] == 0
    places = [pl.ds(pl.multiple_of(info_ref[i] * own_cols, own_cols), own_cols) for i in (1, 2)]
    gates = []
    for which in range(2):
        branch = info_ref[0] if which == 0 else 1 - info_ref[0]
        cols = []
        for place in (info_ref[3], info_ref[3] ^ 1):
            here = pl.ds(pl.multiple_of(place * own_cols, own_cols), own_cols)
            both = gate_ref[branch, :, here].astype(jnp.float32)
            cols.append(jnp.where(cond_first, both[0:1], both[1:2]))
        gates.append(jnp.concatenate(cols, axis=1))
    chosen = [[i for i, kind in enumerate(kinds) if kind[0] == which] for which in range(2)]
    weights = []
    for names in chosen:
        blocks = []
        for _, far, head in [kinds[i] for i in names]:
            depth = slice(head * HD, (head + 1) * HD)
            blocks.append(jnp.concatenate([w_refs[far][depth, place] for place in places], axis=1))
        weights.append(jnp.concatenate(blocks, axis=0))
    for time_tile in range(own_ref.shape[0] // tile):
        token_rows = slice(time_tile * tile, (time_tile + 1) * tile)
        parts = []
        for which in range(2):
            attended = jnp.concatenate([pieces[i][token_rows, :] for i in chosen[which]], axis=1)
            projected = jnp.dot(attended, weights[which], preferred_element_type=jnp.float32)
            parts.append(gates[which] * projected)
        for frame in range(frames):
            rows = slice(frame * FRAME, (frame + 1) * FRAME)
            out_rows = slice(time_tile * tile + rows.start, time_tile * tile + rows.stop)
            guide = 1.0 + 0.5 * info_ref[4 + time_tile * frames + frame].astype(jnp.float32)
            scales = (
                jnp.where(cond_first, guide, 1.0 - guide),
                jnp.where(cond_first, 1.0 - guide, guide),
            )
            total = scales[0] * parts[0][rows] + scales[1] * parts[1][rows]
            own, other = total[:, :own_cols], total[:, own_cols:]
            if first:
                own += scales[0] * base_own_ref[out_rows, :].astype(jnp.float32)
                own += scales[1] * base_other_ref[out_rows, :].astype(jnp.float32)
            else:
                own += base_own_ref[out_rows, :]
                other += base_other_ref[out_rows, :]
            own_ref[out_rows, :] = own
            other_ref[out_rows, :] = other.astype(other_ref.dtype)


def partial_projection(info, weights, pieces, gate, base, tile, first):
    shape = base[0].shape
    return pl.pallas_call(
        functools.partial(partial_kernel, first, tuple(pieces), tile),
        out_shape=[
            jax.ShapeDtypeStruct(shape, jnp.float32),
            jax.ShapeDtypeStruct(shape, jnp.float32 if first else jnp.bfloat16),
        ],
        in_specs=[SCALARS] + [IN_VMEM] * (len(weights) + len(pieces) + 3),
        out_specs=[IN_VMEM] * 2,
        compiler_params=pltpu.CompilerParams(vmem_limit_bytes=VMEM_LIMIT),
        cost_estimate=SMALL_COST,
        name="partial_projection",
    )(info, *pinned([*weights, *pieces.values()]), gate, *pinned(base))


def copy_kernel(plan, info_ref, *refs):
    *arrays, sems = refs
    copies = []
    for source, block, width, target, place in plan:
        src, dst = arrays[source], arrays[target]
        first = block * width
        if block < 0:
            first = pl.multiple_of(info_ref[block + info_ref.shape[0]] * width, width)
        for part in range(COPY_PARTS):
            size = src.shape[0] // COPY_PARTS
            rows = pl.ds(part * size, size)
            to = dst.at[rows, :] if place is None else dst.at[place, rows, :]
            copies.append((src.at[rows, pl.ds(first, width)], to))
    copies = [
        pltpu.make_async_copy(src, to, sems.at[index]) for index, (src, to) in enumerate(copies)
    ]
    for copy in copies:
        copy.start()
    for copy in copies:
        copy.wait()


def copy_columns(info, sources, plan, targets):
    return pl.pallas_call(
        functools.partial(copy_kernel, plan),
        out_shape=[jax.ShapeDtypeStruct(shape, jnp.bfloat16) for shape in targets],
        in_specs=[SCALARS] + [pl.BlockSpec(memory_space=pltpu.HBM)] * len(sources),
        out_specs=[IN_VMEM] * len(targets),
        scratch_shapes=[pltpu.SemaphoreType.DMA((COPY_PARTS * len(plan),))],
        compiler_params=pltpu.CompilerParams(vmem_limit_bytes=COPY_LIMIT),
        cost_estimate=SMALL_COST,
        name="copy_columns",
    )(info, *[pltpu.with_memory_space_constraint(source, pltpu.HBM) for source in sources])


def halves_kernel(info_ref, both_ref, mine_ref, other_ref, sems):
    copies = [
        pltpu.make_async_copy(both_ref.at[half], to, sems.at[index])
        for index, (half, to) in enumerate(((info_ref[0], mine_ref), (1 - info_ref[0], other_ref)))
    ]
    for copy in copies:
        copy.start()
    for copy in copies:
        copy.wait()


def split_halves(info, both):
    return pl.pallas_call(
        halves_kernel,
        out_shape=[jax.ShapeDtypeStruct(both.shape[1:], both.dtype)] * 2,
        in_specs=[SCALARS, pl.BlockSpec(memory_space=pl.ANY)],
        out_specs=[IN_VMEM] * 2,
        scratch_shapes=[pltpu.SemaphoreType.DMA((2,))],
        compiler_params=pltpu.CompilerParams(vmem_limit_bytes=COPY_LIMIT),
        cost_estimate=SMALL_COST,
        name="split_halves",
    )(info, both)


def local(queries, keys, values, residual, gate, out_weight, time_offsets, guidance_index):
    tiles_time, tiles_wide = time_offsets.shape
    count, features = queries.shape[1:]
    tile = count // tiles_time
    heads = features // HD
    head_count = lax.axis_size("head")
    columns = lax.axis_size("tokens")
    branch_pos = lax.axis_index("branch")
    head_pos = lax.axis_index("head")
    width_pos = lax.axis_index("tokens")
    width = gate.shape[2] // head_count

    rounds = [
        [pair for i in range(first, columns - 1, 2) for pair in ((i, i + 1), (i + 1, i))]
        for first in range(2)
    ]
    near_pos = (width_pos ^ 1, ((width_pos + 1) ^ 1) - 1)

    def swap(value, branch_bit, head_bits):
        if not branch_bit and not head_bits:
            return value
        if not head_bits:
            return lax.ppermute(value, "branch", [(0, 1), (1, 0)])
        if not branch_bit:
            return lax.ppermute(value, "head", [(i, i ^ head_bits) for i in range(head_count)])
        flip = head_count + head_bits
        return lax.ppermute(
            value, ("branch", "head"), [(i, i ^ flip) for i in range(2 * head_count)]
        )

    pair = head_pos >> 1
    branch_pair = branch_pos * (head_count // 2)
    copy_info = jnp.stack([branch_pair + pair, branch_pair + (pair ^ 1)])
    sources = (queries[0], keys[0], values[0], out_weight)
    key_value = [((1, 2), head, HD, (0, 1), (2, count, HD)) for head in range(heads)]
    query = [((0,), head, HD, (None,), (count, HD)) for head in range(heads)]
    pair_weight = [((3,), block, 2 * width, (None,), (features, 2 * width)) for block in (-2, -1)]

    def pack(parts, after=None):
        here = sources
        if after is not None:
            _, here = lax.optimization_barrier((after, sources))
        used = sorted({index for part in parts for index in part[0]})
        plan = [
            (used.index(source), block, cols, len(used) + target, place)
            for target, (froms, block, cols, places, _) in enumerate(parts)
            for source, place in zip(froms, places)
        ]
        return copy_columns(
            copy_info, [here[index] for index in used], plan, [part[-1] for part in parts]
        )

    def split_residual(residual):
        return split_halves(branch_pos[None], jnp.transpose(residual[0], (1, 0, 2)))

    packed = pack(key_value[:1])
    after = packed
    if RESIDUAL_AFTER == 0:
        _, residual = lax.optimization_barrier((packed, residual))
        mine, other = split_residual(residual)
        after = (packed, other) if RESIDUAL_FIRST else packed
    late_key_value, far = pack([key_value[1], pair_weight[1]], after)
    packed = list(packed) + [late_key_value]

    def halo(part):
        return [lax.ppermute(part, "tokens", pairs) for pairs in rounds]

    sides = [halo(part) for part in packed]
    near, *late = pack(pair_weight[:1] + query + key_value[2:], sides[0] if LATE_PACK else packed)
    head_queries, packed = late[:heads], packed + late[heads:]
    store = {"far": swap(far, 0, 2)}

    if RESIDUAL_AFTER:
        _, residual = lax.optimization_barrier(((packed[1], sides[0])[RESIDUAL_AFTER - 1], residual))
        mine, other = split_residual(residual)
    store["other"] = swap(other, 1, 0)
    offsets = lax.dynamic_index_in_dim(time_offsets, width_pos, 1, keepdims=False)
    edges = jnp.stack([(pos >= 0) & (pos < tiles_wide) for pos in near_pos]).astype(jnp.int32)
    attention_info = jnp.concatenate([offsets, edges])
    place = head_pos & 1
    projection_info = jnp.concatenate([jnp.stack([branch_pos, place, place ^ 1, head_pos]), guidance_index])

    def relay(head):
        if RELAY[head] == "x":
            store[1, 1, head] = swap(store[0, 1, head], 1, 0)
        elif RELAY[head] == "y":
            store[1, 1, head] = swap(store[1, 0, head], 0, 2)
        else:
            store[1, 1, head] = swap(store[0, 0, head], 1, 2)

    def await_names(names, value):
        value, awaited = lax.optimization_barrier((value, [store[name] for name in names]))
        store.update(zip(names, awaited))
        return value

    for head in range(heads):
        head_queries[head] = await_names(AWAITED.get(head, ()), head_queries[head])
        operands = [head_queries[head], packed[head], *sides[head]]
        if head == heads - 1 and SPLIT:
            own = attention(attention_info, (0, SPLIT), *operands)
            own = await_names(AWAITED.get(heads, ()), own)
            own = attention(attention_info, (SPLIT, tiles_time), *operands, own)
        else:
            own = attention(attention_info, (0, tiles_time), *operands)
        if head + 2 < heads:
            own, part = lax.optimization_barrier((own, packed[head + 2]))
            sides.append(halo(part))
        store[0, 0, head] = own
        store[1, 0, head] = swap(await_names(BEFORE_X.get(head, ()), own), 1, 0)
        store[0, 1, head] = swap(await_names(BEFORE_Y.get(head, ()), own), 0, 2)
        if head < heads - 1:
            relay(head)

    names = [name for name in store if isinstance(name, tuple)]
    late = [name for name in names if name[2] == heads - 1 or name in LATE]
    base = (mine, store["other"])

    def partial(names, base):
        return partial_projection(
            projection_info,
            (near, store["far"]),
            {name: store[name] for name in names},
            gate,
            base,
            tile,
            base[0] is mine,
        )

    base = partial([name for name in names if name not in late], base)
    if TIE_PARTIAL:
        name = (1, 0, heads - 1) if RELAY[-1] == "y" else (0, 1, heads - 1)
        base, store[name] = lax.optimization_barrier((base, store[name]))
    relay(heads - 1)
    base = partial(late + [(1, 1, heads - 1)], base)
    return (base[0] + swap(base[1], 0, 1).astype(jnp.float32)).astype(jnp.bfloat16)


def solution(mesh):
    return jax.shard_map(
        local,
        mesh=mesh,
        in_specs=(
            P("branch", "tokens", "head"),
            P("branch", "tokens", "head"),
            P("branch", "tokens", "head"),
            P("branch", "tokens", None, "head"),
            P(),
            P("head", None),
            P(),
            P(),
        ),
        out_specs=P("tokens", ("branch", "head")),
        check_vma=False,
    )
```

```python
import functools
import math

import jax
import jax.numpy as jnp
from jax import lax
from jax.experimental import pallas as pl
from jax.experimental.pallas import tpu as pltpu
from jax.sharding import PartitionSpec as P

HD = 128
FRAME = 64
FAR = 1e30
EXP2_SCALE = math.log2(math.e) / math.sqrt(HD)
VMEM_LIMIT = 14 * 1024 * 1024
COPY_LIMIT = 8 * 1024 * 1024
COPY_PARTS = 3
LATE_PACK = True
RESIDUAL_FIRST = True
SPLIT = 0
TIE_PARTIAL = False
BEFORE_LAST = ((1, 1, 0), (1, 0, 1), (0, 1, 1))
BEFORE_X = {1: (), 2: ()}
BEFORE_Y = {1: (), 2: ()}
RESIDUAL_AFTER = 0
AWAITED = {0: (), 1: ('far', 'other'), 2: ('far', 'other', (1, 0, 0), (0, 1, 0)), 3: ((1, 0, 1),)}
RELAY = ('y', 'x', 'y')
LATE = ((1, 1, 1),)
SCALARS = pl.BlockSpec(memory_space=pltpu.SMEM)
IN_VMEM = pl.BlockSpec(memory_space=pltpu.VMEM)
SMALL_COST = pl.CostEstimate(flops=0, bytes_accessed=1024, transcendentals=0)


def attention_kernel(first, last, info_ref, q_ref, own_ref, side_a_ref, side_b_ref, *refs):
    *earlier, out_ref = refs
    tiles_time = info_ref.shape[0] - 2
    tile = q_ref.shape[0] // tiles_time
    width_oks = (None, info_ref[tiles_time] == 1, info_ref[tiles_time + 1] == 1)

    def window(t):
        first = t - info_ref[t]
        base = jnp.clip(first, 0, tiles_time - 2)
        inside = [(base + step >= first) & (base + step <= first + 1) for step in range(2)]
        return pl.ds(pl.multiple_of(base * tile, tile), 2 * tile), inside

    refs = (own_ref, side_a_ref, side_b_ref)

    def score(t, side):
        rows, inside = window(t)
        scores = lax.dot_general(
            q_ref[t * tile : (t + 1) * tile, :],
            refs[side][0, rows, :],
            (((1,), (1,)), ((), ())),
            preferred_element_type=jnp.float32,
        )
        blocks, largest = [], None
        for step in range(2):
            allowed = inside[step] if side == 0 else inside[step] & width_oks[side]
            block = scores[:, step * tile : (step + 1) * tile]
            lanes = block[:, :HD]
            for start in range(HD, tile, HD):
                lanes = jnp.maximum(lanes, block[:, start : start + HD])
            lanes = jnp.where(allowed, lanes, -FAR)
            largest = lanes if largest is None else jnp.maximum(largest, lanes)
            blocks.append((block, allowed))
        return blocks, largest

    def blend(t, side, blocks, shift):
        rows, _ = window(t)
        weights = [
            jnp.exp2(block * EXP2_SCALE - jnp.where(allowed, shift, FAR)).astype(jnp.bfloat16)
            for block, allowed in blocks
        ]
        values = refs[side][1, rows, :]
        return jnp.dot(
            jnp.concatenate(weights, axis=1),
            jnp.concatenate([values, jnp.ones_like(values)], axis=1),
            preferred_element_type=jnp.float32,
        )

    ready = [score(first, side) for side in range(3)]
    for ref in earlier:
        out_ref[: first * tile, :] = ref[: first * tile, :]
    for t in range(first, last):
        row_max = jnp.maximum(jnp.maximum(ready[0][1], ready[1][1]), ready[2][1])
        shift = jnp.max(row_max, axis=1, keepdims=True) * EXP2_SCALE
        later, total = [], None
        for side in range(3):
            if t + 1 < last:
                later.append(score(t + 1, side))
            part = blend(t, side, ready[side][0], shift)
            total = part if total is None else total + part
        out_ref[t * tile : (t + 1) * tile, :] = (total[:, :HD] / total[:, HD:]).astype(jnp.bfloat16)
        ready = later


def pinned(operands):
    return [pltpu.with_memory_space_constraint(operand, pltpu.VMEM) for operand in operands]


def attention(info, tiles, *operands):
    return pl.pallas_call(
        functools.partial(attention_kernel, *tiles),
        out_shape=jax.ShapeDtypeStruct(operands[0].shape, jnp.bfloat16),
        in_specs=[SCALARS] + [IN_VMEM] * len(operands),
        out_specs=IN_VMEM,
        compiler_params=pltpu.CompilerParams(vmem_limit_bytes=VMEM_LIMIT),
        cost_estimate=SMALL_COST,
        name="attention",
    )(info, *pinned(operands))


def partial_kernel(first, kinds, tile, info_ref, *refs):
    w_refs, refs = refs[:2], refs[2:]
    *pieces, gate_ref, base_own_ref, base_other_ref, own_ref, other_ref = refs
    own_cols = own_ref.shape[1]
    frames = tile // FRAME
    cond_first = info_ref[0] == 0
    places = [pl.ds(pl.multiple_of(info_ref[i] * own_cols, own_cols), own_cols) for i in (1, 2)]
    gates = []
    for which in range(2):
        branch = info_ref[0] if which == 0 else 1 - info_ref[0]
        cols = []
        for place in (info_ref[3], info_ref[3] ^ 1):
            here = pl.ds(pl.multiple_of(place * own_cols, own_cols), own_cols)
            both = gate_ref[branch, :, here].astype(jnp.float32)
            cols.append(jnp.where(cond_first, both[0:1], both[1:2]))
        gates.append(jnp.concatenate(cols, axis=1))
    chosen = [[i for i, kind in enumerate(kinds) if kind[0] == which] for which in range(2)]
    weights = []
    for names in chosen:
        blocks = []
        for _, far, head in [kinds[i] for i in names]:
            depth = slice(head * HD, (head + 1) * HD)
            blocks.append(jnp.concatenate([w_refs[far][depth, place] for place in places], axis=1))
        weights.append(jnp.concatenate(blocks, axis=0))
    for time_tile in range(own_ref.shape[0] // tile):
        token_rows = slice(time_tile * tile, (time_tile + 1) * tile)
        parts = []
        for which in range(2):
            attended = jnp.concatenate([pieces[i][token_rows, :] for i in chosen[which]], axis=1)
            projected = jnp.dot(attended, weights[which], preferred_element_type=jnp.float32)
            parts.append(gates[which] * projected)
        for frame in range(frames):
            rows = slice(frame * FRAME, (frame + 1) * FRAME)
            out_rows = slice(time_tile * tile + rows.start, time_tile * tile + rows.stop)
            guide = 1.0 + 0.5 * info_ref[4 + time_tile * frames + frame].astype(jnp.float32)
            scales = (
                jnp.where(cond_first, guide, 1.0 - guide),
                jnp.where(cond_first, 1.0 - guide, guide),
            )
            total = scales[0] * parts[0][rows] + scales[1] * parts[1][rows]
            own, other = total[:, :own_cols], total[:, own_cols:]
            if first:
                own += scales[0] * base_own_ref[out_rows, :].astype(jnp.float32)
                own += scales[1] * base_other_ref[out_rows, :].astype(jnp.float32)
            else:
                own += base_own_ref[out_rows, :]
                other += base_other_ref[out_rows, :]
            own_ref[out_rows, :] = own
            other_ref[out_rows, :] = other.astype(other_ref.dtype)


def partial_projection(info, weights, pieces, gate, base, tile, first):
    shape = base[0].shape
    return pl.pallas_call(
        functools.partial(partial_kernel, first, tuple(pieces), tile),
        out_shape=[
            jax.ShapeDtypeStruct(shape, jnp.float32),
            jax.ShapeDtypeStruct(shape, jnp.float32 if first else jnp.bfloat16),
        ],
        in_specs=[SCALARS] + [IN_VMEM] * (len(weights) + len(pieces) + 3),
        out_specs=[IN_VMEM] * 2,
        compiler_params=pltpu.CompilerParams(vmem_limit_bytes=VMEM_LIMIT),
        cost_estimate=SMALL_COST,
        name="partial_projection",
    )(info, *pinned([*weights, *pieces.values()]), gate, *pinned(base))


def copy_kernel(plan, info_ref, *refs):
    *arrays, sems = refs
    copies = []
    for source, block, width, target, place in plan:
        src, dst = arrays[source], arrays[target]
        first = block * width
        if block < 0:
            first = pl.multiple_of(info_ref[block + info_ref.shape[0]] * width, width)
        for part in range(COPY_PARTS):
            size = src.shape[0] // COPY_PARTS
            rows = pl.ds(part * size, size)
            to = dst.at[rows, :] if place is None else dst.at[place, rows, :]
            copies.append((src.at[rows, pl.ds(first, width)], to))
    copies = [
        pltpu.make_async_copy(src, to, sems.at[index]) for index, (src, to) in enumerate(copies)
    ]
    for copy in copies:
        copy.start()
    for copy in copies:
        copy.wait()


def copy_columns(info, sources, plan, targets):
    return pl.pallas_call(
        functools.partial(copy_kernel, plan),
        out_shape=[jax.ShapeDtypeStruct(shape, jnp.bfloat16) for shape in targets],
        in_specs=[SCALARS] + [pl.BlockSpec(memory_space=pltpu.HBM)] * len(sources),
        out_specs=[IN_VMEM] * len(targets),
        scratch_shapes=[pltpu.SemaphoreType.DMA((COPY_PARTS * len(plan),))],
        compiler_params=pltpu.CompilerParams(vmem_limit_bytes=COPY_LIMIT),
        cost_estimate=SMALL_COST,
        name="copy_columns",
    )(info, *[pltpu.with_memory_space_constraint(source, pltpu.HBM) for source in sources])


def halves_kernel(info_ref, both_ref, mine_ref, other_ref, sems):
    copies = [
        pltpu.make_async_copy(both_ref.at[half], to, sems.at[index])
        for index, (half, to) in enumerate(((info_ref[0], mine_ref), (1 - info_ref[0], other_ref)))
    ]
    for copy in copies:
        copy.start()
    for copy in copies:
        copy.wait()


def split_halves(info, both):
    return pl.pallas_call(
        halves_kernel,
        out_shape=[jax.ShapeDtypeStruct(both.shape[1:], both.dtype)] * 2,
        in_specs=[SCALARS, pl.BlockSpec(memory_space=pl.ANY)],
        out_specs=[IN_VMEM] * 2,
        scratch_shapes=[pltpu.SemaphoreType.DMA((2,))],
        compiler_params=pltpu.CompilerParams(vmem_limit_bytes=COPY_LIMIT),
        cost_estimate=SMALL_COST,
        name="split_halves",
    )(info, both)


def local(queries, keys, values, residual, gate, out_weight, time_offsets, guidance_index):
    tiles_time, tiles_wide = time_offsets.shape
    count, features = queries.shape[1:]
    tile = count // tiles_time
    heads = features // HD
    head_count = lax.axis_size("head")
    columns = lax.axis_size("tokens")
    branch_pos = lax.axis_index("branch")
    head_pos = lax.axis_index("head")
    width_pos = lax.axis_index("tokens")
    width = gate.shape[2] // head_count

    rounds = [
        [pair for i in range(first, columns - 1, 2) for pair in ((i, i + 1), (i + 1, i))]
        for first in range(2)
    ]
    near_pos = (width_pos ^ 1, ((width_pos + 1) ^ 1) - 1)

    def swap(value, branch_bit, head_bits):
        if not branch_bit and not head_bits:
            return value
        if not head_bits:
            return lax.ppermute(value, "branch", [(0, 1), (1, 0)])
        if not branch_bit:
            return lax.ppermute(value, "head", [(i, i ^ head_bits) for i in range(head_count)])
        flip = head_count + head_bits
        return lax.ppermute(
            value, ("branch", "head"), [(i, i ^ flip) for i in range(2 * head_count)]
        )

    pair = head_pos >> 1
    branch_pair = branch_pos * (head_count // 2)
    copy_info = jnp.stack([branch_pair + pair, branch_pair + (pair ^ 1)])
    sources = (queries[0], keys[0], values[0], out_weight)
    key_value = [((1, 2), head, HD, (0, 1), (2, count, HD)) for head in range(heads)]
    query = [((0,), head, HD, (None,), (count, HD)) for head in range(heads)]
    pair_weight = [((3,), block, 2 * width, (None,), (features, 2 * width)) for block in (-2, -1)]

    def pack(parts, after=None):
        here = sources
        if after is not None:
            _, here = lax.optimization_barrier((after, sources))
        used = sorted({index for part in parts for index in part[0]})
        plan = [
            (used.index(source), block, cols, len(used) + target, place)
            for target, (froms, block, cols, places, _) in enumerate(parts)
            for source, place in zip(froms, places)
        ]
        return copy_columns(
            copy_info, [here[index] for index in used], plan, [part[-1] for part in parts]
        )

    def split_residual(residual):
        return split_halves(branch_pos[None], jnp.transpose(residual[0], (1, 0, 2)))

    packed = pack(key_value[:1])
    after = packed
    if RESIDUAL_AFTER == 0:
        _, residual = lax.optimization_barrier((packed, residual))
        mine, other = split_residual(residual)
        after = (packed, other) if RESIDUAL_FIRST else packed
    late_key_value, far = pack([key_value[1], pair_weight[1]], after)
    packed = list(packed) + [late_key_value]

    def halo(part):
        return [lax.ppermute(part, "tokens", pairs) for pairs in rounds]

    sides = [halo(part) for part in packed]
    near, *late = pack(pair_weight[:1] + query + key_value[2:], sides[0] if LATE_PACK else packed)
    head_queries, packed = late[:heads], packed + late[heads:]
    store = {"far": swap(far, 0, 2)}

    if RESIDUAL_AFTER:
        _, residual = lax.optimization_barrier(((packed[1], sides[0])[RESIDUAL_AFTER - 1], residual))
        mine, other = split_residual(residual)
    store["other"] = swap(other, 1, 0)
    offsets = lax.dynamic_index_in_dim(time_offsets, width_pos, 1, keepdims=False)
    edges = jnp.stack([(pos >= 0) & (pos < tiles_wide) for pos in near_pos]).astype(jnp.int32)
    attention_info = jnp.concatenate([offsets, edges])
    place = head_pos & 1
    projection_info = jnp.concatenate([jnp.stack([branch_pos, place, place ^ 1, head_pos]), guidance_index])

    head_queries[0], projection_info = lax.optimization_barrier((head_queries[0], projection_info))
    def relay(head):
        if RELAY[head] == "x":
            store[1, 1, head] = swap(store[0, 1, head], 1, 0)
        elif RELAY[head] == "y":
            store[1, 1, head] = swap(store[1, 0, head], 0, 2)
        else:
            store[1, 1, head] = swap(store[0, 0, head], 1, 2)

    def await_names(names, value):
        value, awaited = lax.optimization_barrier((value, [store[name] for name in names]))
        store.update(zip(names, awaited))
        return value

    for head in range(heads):
        head_queries[head] = await_names(AWAITED.get(head, ()), head_queries[head])
        operands = [head_queries[head], packed[head], *sides[head]]
        if head == heads - 1 and SPLIT:
            own = attention(attention_info, (0, SPLIT), *operands)
            own = await_names(AWAITED.get(heads, ()), own)
            own = attention(attention_info, (SPLIT, tiles_time), *operands, own)
        else:
            own = attention(attention_info, (0, tiles_time), *operands)
        if head + 2 < heads:
            own, part = lax.optimization_barrier((own, packed[head + 2]))
            sides.append(halo(part))
        store[0, 0, head] = own
        store[1, 0, head] = swap(await_names(BEFORE_X.get(head, ()), own), 1, 0)
        store[0, 1, head] = swap(await_names(BEFORE_Y.get(head, ()), own), 0, 2)
        if head < heads - 1:
            relay(head)

    names = [name for name in store if isinstance(name, tuple)]
    late = [name for name in names if name[2] == heads - 1 or name in LATE]
    base = (mine, store["other"])

    def partial(names, base):
        return partial_projection(
            projection_info,
            (near, store["far"]),
            {name: store[name] for name in names},
            gate,
            base,
            tile,
            base[0] is mine,
        )

    base = partial([name for name in names if name not in late], base)
    if TIE_PARTIAL:
        name = (1, 0, heads - 1) if RELAY[-1] == "y" else (0, 1, heads - 1)
        base, store[name] = lax.optimization_barrier((base, store[name]))
    if BEFORE_LAST:
        name = (1, 0, heads - 1) if RELAY[-1] == "y" else (0, 1, heads - 1)
        store[name] = await_names(BEFORE_LAST, store[name])
    relay(heads - 1)
    base = partial(late + [(1, 1, heads - 1)], base)
    return (base[0] + swap(base[1], 0, 1).astype(jnp.float32)).astype(jnp.bfloat16)


def solution(mesh):
    return jax.shard_map(
        local,
        mesh=mesh,
        in_specs=(
            P("branch", "tokens", "head"),
            P("branch", "tokens", "head"),
            P("branch", "tokens", "head"),
            P("branch", "tokens", None, "head"),
            P(),
            P("head", None),
            P(),
            P(),
        ),
        out_specs=P("tokens", ("branch", "head")),
        check_vma=False,
    )
```

```python
import functools
import math

import jax
import jax.numpy as jnp
from jax import lax
from jax.experimental import pallas as pl
from jax.experimental.pallas import tpu as pltpu
from jax.sharding import PartitionSpec as P

HD = 128
FRAME = 64
FAR = 1e30
EXP2_SCALE = math.log2(math.e) / math.sqrt(HD)
VMEM_LIMIT = 14 * 1024 * 1024
COPY_LIMIT = 8 * 1024 * 1024
COPY_PARTS = 8
LATE_PACK = True
RESIDUAL_FIRST = True
SPLIT = 0
TIE_PARTIAL = False
BEFORE_LAST = ((1, 1, 0), (1, 0, 1), (0, 1, 1))
BEFORE_X = {1: (), 2: ()}
BEFORE_Y = {1: (), 2: ()}
RESIDUAL_AFTER = 0
AWAITED = {0: (), 1: ('far', 'other'), 2: ('far', 'other', (1, 0, 0), (0, 1, 0)), 3: ((1, 0, 1),)}
RELAY = ('y', 'x', 'y')
LATE = ((1, 1, 1),)
SCALARS = pl.BlockSpec(memory_space=pltpu.SMEM)
IN_VMEM = pl.BlockSpec(memory_space=pltpu.VMEM)
SMALL_COST = pl.CostEstimate(flops=0, bytes_accessed=1024, transcendentals=0)


def attention_kernel(first, last, info_ref, q_ref, own_ref, side_a_ref, side_b_ref, *refs):
    *earlier, out_ref = refs
    tiles_time = info_ref.shape[0] - 2
    tile = q_ref.shape[0] // tiles_time
    width_oks = (None, info_ref[tiles_time] == 1, info_ref[tiles_time + 1] == 1)

    def window(t):
        first = t - info_ref[t]
        base = jnp.clip(first, 0, tiles_time - 2)
        inside = [(base + step >= first) & (base + step <= first + 1) for step in range(2)]
        return pl.ds(pl.multiple_of(base * tile, tile), 2 * tile), inside

    refs = (own_ref, side_a_ref, side_b_ref)

    def score(t, side):
        rows, inside = window(t)
        scores = lax.dot_general(
            q_ref[t * tile : (t + 1) * tile, :],
            refs[side][0, rows, :],
            (((1,), (1,)), ((), ())),
            preferred_element_type=jnp.float32,
        )
        blocks, largest = [], None
        for step in range(2):
            allowed = inside[step] if side == 0 else inside[step] & width_oks[side]
            block = scores[:, step * tile : (step + 1) * tile]
            lanes = block[:, :HD]
            for start in range(HD, tile, HD):
                lanes = jnp.maximum(lanes, block[:, start : start + HD])
            lanes = jnp.where(allowed, lanes, -FAR)
            largest = lanes if largest is None else jnp.maximum(largest, lanes)
            blocks.append((block, allowed))
        return blocks, largest

    def blend(t, side, blocks, shift):
        rows, _ = window(t)
        weights = [
            jnp.exp2(block * EXP2_SCALE - jnp.where(allowed, shift, FAR)).astype(jnp.bfloat16)
            for block, allowed in blocks
        ]
        values = refs[side][1, rows, :]
        return jnp.dot(
            jnp.concatenate(weights, axis=1),
            jnp.concatenate([values, jnp.ones_like(values)], axis=1),
            preferred_element_type=jnp.float32,
        )

    ready = [score(first, side) for side in range(3)]
    for ref in earlier:
        out_ref[: first * tile, :] = ref[: first * tile, :]
    for t in range(first, last):
        row_max = jnp.maximum(jnp.maximum(ready[0][1], ready[1][1]), ready[2][1])
        shift = jnp.max(row_max, axis=1, keepdims=True) * EXP2_SCALE
        later, total = [], None
        for side in range(3):
            if t + 1 < last:
                later.append(score(t + 1, side))
            part = blend(t, side, ready[side][0], shift)
            total = part if total is None else total + part
        out_ref[t * tile : (t + 1) * tile, :] = (total[:, :HD] / total[:, HD:]).astype(jnp.bfloat16)
        ready = later


def pinned(operands):
    return [pltpu.with_memory_space_constraint(operand, pltpu.VMEM) for operand in operands]


def attention(info, tiles, *operands):
    return pl.pallas_call(
        functools.partial(attention_kernel, *tiles),
        out_shape=jax.ShapeDtypeStruct(operands[0].shape, jnp.bfloat16),
        in_specs=[SCALARS] + [IN_VMEM] * len(operands),
        out_specs=IN_VMEM,
        compiler_params=pltpu.CompilerParams(vmem_limit_bytes=VMEM_LIMIT),
        cost_estimate=SMALL_COST,
        name="attention",
    )(info, *pinned(operands))


def partial_kernel(first, kinds, tile, info_ref, *refs):
    w_refs, refs = refs[:2], refs[2:]
    *pieces, gate_ref, base_own_ref, base_other_ref, own_ref, other_ref = refs
    own_cols = own_ref.shape[1]
    frames = tile // FRAME
    cond_first = info_ref[0] == 0
    places = [pl.ds(pl.multiple_of(info_ref[i] * own_cols, own_cols), own_cols) for i in (1, 2)]
    gates = []
    for which in range(2):
        branch = info_ref[0] if which == 0 else 1 - info_ref[0]
        cols = []
        for place in (info_ref[3], info_ref[3] ^ 1):
            here = pl.ds(pl.multiple_of(place * own_cols, own_cols), own_cols)
            both = gate_ref[branch, :, here].astype(jnp.float32)
            cols.append(jnp.where(cond_first, both[0:1], both[1:2]))
        gates.append(jnp.concatenate(cols, axis=1))
    chosen = [[i for i, kind in enumerate(kinds) if kind[0] == which] for which in range(2)]
    weights = []
    for names in chosen:
        blocks = []
        for _, far, head in [kinds[i] for i in names]:
            depth = slice(head * HD, (head + 1) * HD)
            blocks.append(jnp.concatenate([w_refs[far][depth, place] for place in places], axis=1))
        weights.append(jnp.concatenate(blocks, axis=0))
    for time_tile in range(own_ref.shape[0] // tile):
        token_rows = slice(time_tile * tile, (time_tile + 1) * tile)
        parts = []
        for which in range(2):
            attended = jnp.concatenate([pieces[i][token_rows, :] for i in chosen[which]], axis=1)
            projected = jnp.dot(attended, weights[which], preferred_element_type=jnp.float32)
            parts.append(gates[which] * projected)
        for frame in range(frames):
            rows = slice(frame * FRAME, (frame + 1) * FRAME)
            out_rows = slice(time_tile * tile + rows.start, time_tile * tile + rows.stop)
            guide = 1.0 + 0.5 * info_ref[4 + time_tile * frames + frame].astype(jnp.float32)
            scales = (
                jnp.where(cond_first, guide, 1.0 - guide),
                jnp.where(cond_first, 1.0 - guide, guide),
            )
            total = scales[0] * parts[0][rows] + scales[1] * parts[1][rows]
            own, other = total[:, :own_cols], total[:, own_cols:]
            if first:
                own += scales[0] * base_own_ref[out_rows, :].astype(jnp.float32)
                own += scales[1] * base_other_ref[out_rows, :].astype(jnp.float32)
            else:
                own += base_own_ref[out_rows, :]
                other += base_other_ref[out_rows, :]
            own_ref[out_rows, :] = own
            other_ref[out_rows, :] = other.astype(other_ref.dtype)


def partial_projection(info, weights, pieces, gate, base, tile, first):
    shape = base[0].shape
    return pl.pallas_call(
        functools.partial(partial_kernel, first, tuple(pieces), tile),
        out_shape=[
            jax.ShapeDtypeStruct(shape, jnp.float32),
            jax.ShapeDtypeStruct(shape, jnp.float32 if first else jnp.bfloat16),
        ],
        in_specs=[SCALARS] + [IN_VMEM] * (len(weights) + len(pieces) + 3),
        out_specs=[IN_VMEM] * 2,
        compiler_params=pltpu.CompilerParams(vmem_limit_bytes=VMEM_LIMIT),
        cost_estimate=SMALL_COST,
        name="partial_projection",
    )(info, *pinned([*weights, *pieces.values()]), gate, *pinned(base))


def copy_kernel(plan, info_ref, *refs):
    *arrays, sems = refs
    copies = []
    for source, block, width, target, place in plan:
        src, dst = arrays[source], arrays[target]
        first = block * width
        if block < 0:
            first = pl.multiple_of(info_ref[block + info_ref.shape[0]] * width, width)
        for part in range(COPY_PARTS):
            size = src.shape[0] // COPY_PARTS
            rows = pl.ds(part * size, size)
            to = dst.at[rows, :] if place is None else dst.at[place, rows, :]
            copies.append((src.at[rows, pl.ds(first, width)], to))
    copies = [
        pltpu.make_async_copy(src, to, sems.at[index]) for index, (src, to) in enumerate(copies)
    ]
    for copy in copies:
        copy.start()
    for copy in copies:
        copy.wait()


def copy_columns(info, sources, plan, targets):
    return pl.pallas_call(
        functools.partial(copy_kernel, plan),
        out_shape=[jax.ShapeDtypeStruct(shape, jnp.bfloat16) for shape in targets],
        in_specs=[SCALARS] + [pl.BlockSpec(memory_space=pltpu.HBM)] * len(sources),
        out_specs=[IN_VMEM] * len(targets),
        scratch_shapes=[pltpu.SemaphoreType.DMA((COPY_PARTS * len(plan),))],
        compiler_params=pltpu.CompilerParams(vmem_limit_bytes=COPY_LIMIT),
        cost_estimate=SMALL_COST,
        name="copy_columns",
    )(info, *[pltpu.with_memory_space_constraint(source, pltpu.HBM) for source in sources])


def halves_kernel(info_ref, both_ref, mine_ref, other_ref, sems):
    copies = [
        pltpu.make_async_copy(both_ref.at[half], to, sems.at[index])
        for index, (half, to) in enumerate(((info_ref[0], mine_ref), (1 - info_ref[0], other_ref)))
    ]
    for copy in copies:
        copy.start()
    for copy in copies:
        copy.wait()


def split_halves(info, both):
    return pl.pallas_call(
        halves_kernel,
        out_shape=[jax.ShapeDtypeStruct(both.shape[1:], both.dtype)] * 2,
        in_specs=[SCALARS, pl.BlockSpec(memory_space=pl.ANY)],
        out_specs=[IN_VMEM] * 2,
        scratch_shapes=[pltpu.SemaphoreType.DMA((2,))],
        compiler_params=pltpu.CompilerParams(vmem_limit_bytes=COPY_LIMIT),
        cost_estimate=SMALL_COST,
        name="split_halves",
    )(info, both)


def local(queries, keys, values, residual, gate, out_weight, time_offsets, guidance_index):
    tiles_time, tiles_wide = time_offsets.shape
    count, features = queries.shape[1:]
    tile = count // tiles_time
    heads = features // HD
    head_count = lax.axis_size("head")
    columns = lax.axis_size("tokens")
    branch_pos = lax.axis_index("branch")
    head_pos = lax.axis_index("head")
    width_pos = lax.axis_index("tokens")
    width = gate.shape[2] // head_count

    rounds = [
        [pair for i in range(first, columns - 1, 2) for pair in ((i, i + 1), (i + 1, i))]
        for first in range(2)
    ]
    near_pos = (width_pos ^ 1, ((width_pos + 1) ^ 1) - 1)

    def swap(value, branch_bit, head_bits):
        if not branch_bit and not head_bits:
            return value
        if not head_bits:
            return lax.ppermute(value, "branch", [(0, 1), (1, 0)])
        if not branch_bit:
            return lax.ppermute(value, "head", [(i, i ^ head_bits) for i in range(head_count)])
        flip = head_count + head_bits
        return lax.ppermute(
            value, ("branch", "head"), [(i, i ^ flip) for i in range(2 * head_count)]
        )

    pair = head_pos >> 1
    branch_pair = branch_pos * (head_count // 2)
    copy_info = jnp.stack([branch_pair + pair, branch_pair + (pair ^ 1)])
    sources = (queries[0], keys[0], values[0], out_weight)
    key_value = [((1, 2), head, HD, (0, 1), (2, count, HD)) for head in range(heads)]
    query = [((0,), head, HD, (None,), (count, HD)) for head in range(heads)]
    pair_weight = [((3,), block, 2 * width, (None,), (features, 2 * width)) for block in (-2, -1)]

    def pack(parts, after=None):
        here = sources
        if after is not None:
            _, here = lax.optimization_barrier((after, sources))
        used = sorted({index for part in parts for index in part[0]})
        plan = [
            (used.index(source), block, cols, len(used) + target, place)
            for target, (froms, block, cols, places, _) in enumerate(parts)
            for source, place in zip(froms, places)
        ]
        return copy_columns(
            copy_info, [here[index] for index in used], plan, [part[-1] for part in parts]
        )

    def split_residual(residual):
        return split_halves(branch_pos[None], jnp.transpose(residual[0], (1, 0, 2)))

    packed = pack(key_value[:1])
    after = packed
    if RESIDUAL_AFTER == 0:
        _, residual = lax.optimization_barrier((packed, residual))
        mine, other = split_residual(residual)
        after = (packed, other) if RESIDUAL_FIRST else packed
    late_key_value, far = pack([key_value[1], pair_weight[1]], after)
    packed = list(packed) + [late_key_value]

    def halo(part):
        return [lax.ppermute(part, "tokens", pairs) for pairs in rounds]

    sides = [halo(part) for part in packed]
    near, *late = pack(pair_weight[:1] + query + key_value[2:], sides[0] if LATE_PACK else packed)
    head_queries, packed = late[:heads], packed + late[heads:]
    store = {"far": swap(far, 0, 2)}

    if RESIDUAL_AFTER:
        _, residual = lax.optimization_barrier(((packed[1], sides[0])[RESIDUAL_AFTER - 1], residual))
        mine, other = split_residual(residual)
    store["other"] = swap(other, 1, 0)
    offsets = lax.dynamic_index_in_dim(time_offsets, width_pos, 1, keepdims=False)
    edges = jnp.stack([(pos >= 0) & (pos < tiles_wide) for pos in near_pos]).astype(jnp.int32)
    attention_info = jnp.concatenate([offsets, edges])
    place = head_pos & 1
    projection_info = jnp.concatenate([jnp.stack([branch_pos, place, place ^ 1, head_pos]), guidance_index])

    head_queries[0], projection_info = lax.optimization_barrier((head_queries[0], projection_info))
    def relay(head):
        if RELAY[head] == "x":
            store[1, 1, head] = swap(store[0, 1, head], 1, 0)
        elif RELAY[head] == "y":
            store[1, 1, head] = swap(store[1, 0, head], 0, 2)
        else:
            store[1, 1, head] = swap(store[0, 0, head], 1, 2)

    def await_names(names, value):
        value, awaited = lax.optimization_barrier((value, [store[name] for name in names]))
        store.update(zip(names, awaited))
        return value

    for head in range(heads):
        head_queries[head] = await_names(AWAITED.get(head, ()), head_queries[head])
        operands = [head_queries[head], packed[head], *sides[head]]
        if head == heads - 1 and SPLIT:
            own = attention(attention_info, (0, SPLIT), *operands)
            own = await_names(AWAITED.get(heads, ()), own)
            own = attention(attention_info, (SPLIT, tiles_time), *operands, own)
        else:
            own = attention(attention_info, (0, tiles_time), *operands)
        if head + 2 < heads:
            own, part = lax.optimization_barrier((own, packed[head + 2]))
            sides.append(halo(part))
        store[0, 0, head] = own
        store[1, 0, head] = swap(await_names(BEFORE_X.get(head, ()), own), 1, 0)
        store[0, 1, head] = swap(await_names(BEFORE_Y.get(head, ()), own), 0, 2)
        if head < heads - 1:
            relay(head)

    names = [name for name in store if isinstance(name, tuple)]
    late = [name for name in names if name[2] == heads - 1 or name in LATE]
    base = (mine, store["other"])

    def partial(names, base):
        return partial_projection(
            projection_info,
            (near, store["far"]),
            {name: store[name] for name in names},
            gate,
            base,
            tile,
            base[0] is mine,
        )

    base = partial([name for name in names if name not in late], base)
    if TIE_PARTIAL:
        name = (1, 0, heads - 1) if RELAY[-1] == "y" else (0, 1, heads - 1)
        base, store[name] = lax.optimization_barrier((base, store[name]))
    if BEFORE_LAST:
        name = (1, 0, heads - 1) if RELAY[-1] == "y" else (0, 1, heads - 1)
        store[name] = await_names(BEFORE_LAST, store[name])
    relay(heads - 1)
    base = partial(late + [(1, 1, heads - 1)], base)
    return (base[0] + swap(base[1], 0, 1).astype(jnp.float32)).astype(jnp.bfloat16)


def solution(mesh):
    return jax.shard_map(
        local,
        mesh=mesh,
        in_specs=(
            P("branch", "tokens", "head"),
            P("branch", "tokens", "head"),
            P("branch", "tokens", "head"),
            P("branch", "tokens", None, "head"),
            P(),
            P("head", None),
            P(),
            P(),
        ),
        out_specs=P("tokens", ("branch", "head")),
        check_vma=False,
    )
```

```python
import functools
import math

import jax
import jax.numpy as jnp
from jax import lax
from jax.experimental import pallas as pl
from jax.experimental.pallas import tpu as pltpu
from jax.sharding import PartitionSpec as P

HD = 128
FRAME = 64
FAR = 1e30
EXP2_SCALE = math.log2(math.e) / math.sqrt(HD)
VMEM_LIMIT = 14 * 1024 * 1024
COPY_LIMIT = 8 * 1024 * 1024
COPY_PARTS = 3
LATE_PACK = True
RESIDUAL_FIRST = True
SPLIT = 0
TIE_PARTIAL = False
BEFORE_LAST = ((1, 1, 0), (1, 0, 1), (0, 1, 1))
BEFORE_X = {1: (), 2: ()}
BEFORE_Y = {1: (), 2: ()}
RESIDUAL_AFTER = 0
AWAITED = {0: (), 1: ('far', 'other'), 2: ('far', 'other', (1, 0, 0), (0, 1, 0)), 3: ((1, 0, 1),)}
RELAY = ('y', 'x', 'y')
LATE = ((1, 1, 1),)
SCALARS = pl.BlockSpec(memory_space=pltpu.SMEM)
IN_VMEM = pl.BlockSpec(memory_space=pltpu.VMEM)
SMALL_COST = pl.CostEstimate(flops=0, bytes_accessed=1024, transcendentals=0)


def attention_kernel(first, last, info_ref, q_ref, own_ref, side_a_ref, side_b_ref, *refs):
    *earlier, out_ref = refs
    tiles_time = info_ref.shape[0] - 2
    tile = q_ref.shape[0] // tiles_time
    width_oks = (None, info_ref[tiles_time] == 1, info_ref[tiles_time + 1] == 1)

    def window(t):
        first = t - info_ref[t]
        base = jnp.clip(first, 0, tiles_time - 2)
        inside = [(base + step >= first) & (base + step <= first + 1) for step in range(2)]
        return pl.ds(pl.multiple_of(base * tile, tile), 2 * tile), inside

    refs = (own_ref, side_a_ref, side_b_ref)

    def score(t, side):
        rows, inside = window(t)
        scores = lax.dot_general(
            q_ref[t * tile : (t + 1) * tile, :],
            refs[side][0, rows, :],
            (((1,), (1,)), ((), ())),
            preferred_element_type=jnp.float32,
        )
        blocks, largest = [], None
        for step in range(2):
            allowed = inside[step] if side == 0 else inside[step] & width_oks[side]
            block = scores[:, step * tile : (step + 1) * tile]
            lanes = block[:, :HD]
            for start in range(HD, tile, HD):
                lanes = jnp.maximum(lanes, block[:, start : start + HD])
            lanes = jnp.where(allowed, lanes, -FAR)
            largest = lanes if largest is None else jnp.maximum(largest, lanes)
            blocks.append((block, allowed))
        return blocks, largest

    def blend(t, side, blocks, shift):
        rows, _ = window(t)
        weights = [
            jnp.exp2(block * EXP2_SCALE - jnp.where(allowed, shift, FAR)).astype(jnp.bfloat16)
            for block, allowed in blocks
        ]
        values = refs[side][1, rows, :]
        return jnp.dot(
            jnp.concatenate(weights, axis=1),
            jnp.concatenate([values, jnp.ones_like(values)], axis=1),
            preferred_element_type=jnp.float32,
        )

    ready = [score(first, side) for side in range(3)]
    for ref in earlier:
        out_ref[: first * tile, :] = ref[: first * tile, :]
    for t in range(first, last):
        row_max = jnp.maximum(jnp.maximum(ready[0][1], ready[1][1]), ready[2][1])
        shift = jnp.max(row_max, axis=1, keepdims=True) * EXP2_SCALE
        later, total = [], None
        for side in range(3):
            if t + 1 < last:
                later.append(score(t + 1, side))
            part = blend(t, side, ready[side][0], shift)
            total = part if total is None else total + part
        out_ref[t * tile : (t + 1) * tile, :] = (total[:, :HD] / total[:, HD:]).astype(jnp.bfloat16)
        ready = later


def pinned(operands):
    return [pltpu.with_memory_space_constraint(operand, pltpu.VMEM) for operand in operands]


def attention(info, tiles, *operands):
    return pl.pallas_call(
        functools.partial(attention_kernel, *tiles),
        out_shape=jax.ShapeDtypeStruct(operands[0].shape, jnp.bfloat16),
        in_specs=[SCALARS] + [IN_VMEM] * len(operands),
        out_specs=IN_VMEM,
        compiler_params=pltpu.CompilerParams(vmem_limit_bytes=VMEM_LIMIT),
        cost_estimate=SMALL_COST,
        name="attention",
    )(info, *pinned(operands))


def partial_kernel(first, kinds, tile, info_ref, *refs):
    w_refs, refs = refs[:2], refs[2:]
    *pieces, gate_ref, base_own_ref, base_other_ref, own_ref, other_ref = refs
    own_cols = own_ref.shape[1]
    frames = tile // FRAME
    cond_first = info_ref[0] == 0
    places = [pl.ds(pl.multiple_of(info_ref[i] * own_cols, own_cols), own_cols) for i in (1, 2)]
    gates = []
    for which in range(2):
        branch = info_ref[0] if which == 0 else 1 - info_ref[0]
        cols = []
        for place in (info_ref[3], info_ref[3] ^ 1):
            here = pl.ds(pl.multiple_of(place * own_cols, own_cols), own_cols)
            both = gate_ref[branch, :, here].astype(jnp.float32)
            cols.append(jnp.where(cond_first, both[0:1], both[1:2]))
        gates.append(jnp.concatenate(cols, axis=1))
    chosen = [[i for i, kind in enumerate(kinds) if kind[0] == which] for which in range(2)]
    weights = []
    for names in chosen:
        blocks = []
        for _, far, head in [kinds[i] for i in names]:
            depth = slice(head * HD, (head + 1) * HD)
            blocks.append(jnp.concatenate([w_refs[far][depth, place] for place in places], axis=1))
        weights.append(jnp.concatenate(blocks, axis=0))
    for time_tile in range(own_ref.shape[0] // tile):
        token_rows = slice(time_tile * tile, (time_tile + 1) * tile)
        parts = []
        for which in range(2):
            attended = jnp.concatenate([pieces[i][token_rows, :] for i in chosen[which]], axis=1)
            projected = jnp.dot(attended, weights[which], preferred_element_type=jnp.float32)
            parts.append(gates[which] * projected)
        for frame in range(frames):
            rows = slice(frame * FRAME, (frame + 1) * FRAME)
            out_rows = slice(time_tile * tile + rows.start, time_tile * tile + rows.stop)
            guide = 1.0 + 0.5 * info_ref[4 + time_tile * frames + frame].astype(jnp.float32)
            scales = (
                jnp.where(cond_first, guide, 1.0 - guide),
                jnp.where(cond_first, 1.0 - guide, guide),
            )
            total = scales[0] * parts[0][rows] + scales[1] * parts[1][rows]
            own, other = total[:, :own_cols], total[:, own_cols:]
            if first:
                own += scales[0] * base_own_ref[out_rows, :].astype(jnp.float32)
                own += scales[1] * base_other_ref[out_rows, :].astype(jnp.float32)
            else:
                own += base_own_ref[out_rows, :]
                other += base_other_ref[out_rows, :]
            own_ref[out_rows, :] = own
            other_ref[out_rows, :] = other.astype(other_ref.dtype)


def partial_projection(info, weights, pieces, gate, base, tile, first):
    shape = base[0].shape
    return pl.pallas_call(
        functools.partial(partial_kernel, first, tuple(pieces), tile),
        out_shape=[
            jax.ShapeDtypeStruct(shape, jnp.float32),
            jax.ShapeDtypeStruct(shape, jnp.float32 if first else jnp.bfloat16),
        ],
        in_specs=[SCALARS] + [IN_VMEM] * (len(weights) + len(pieces) + 3),
        out_specs=[IN_VMEM] * 2,
        compiler_params=pltpu.CompilerParams(vmem_limit_bytes=VMEM_LIMIT),
        cost_estimate=SMALL_COST,
        name="partial_projection",
    )(info, *pinned([*weights, *pieces.values()]), gate, *pinned(base))


def copy_kernel(plan, info_ref, *refs):
    *arrays, sems = refs
    copies = []
    for source, block, width, target, place in plan:
        src, dst = arrays[source], arrays[target]
        first = block * width
        if block < 0:
            first = pl.multiple_of(info_ref[block + info_ref.shape[0]] * width, width)
        for part in range(COPY_PARTS):
            size = src.shape[0] // COPY_PARTS
            rows = pl.ds(part * size, size)
            to = dst.at[rows, :] if place is None else dst.at[place, rows, :]
            copies.append((src.at[rows, pl.ds(first, width)], to))
    copies = [
        pltpu.make_async_copy(src, to, sems.at[index]) for index, (src, to) in enumerate(copies)
    ]
    for copy in copies:
        copy.start()
    for copy in copies:
        copy.wait()


def copy_columns(info, sources, plan, targets):
    return pl.pallas_call(
        functools.partial(copy_kernel, plan),
        out_shape=[jax.ShapeDtypeStruct(shape, jnp.bfloat16) for shape in targets],
        in_specs=[SCALARS] + [pl.BlockSpec(memory_space=pltpu.HBM)] * len(sources),
        out_specs=[IN_VMEM] * len(targets),
        scratch_shapes=[pltpu.SemaphoreType.DMA((COPY_PARTS * len(plan),))],
        compiler_params=pltpu.CompilerParams(vmem_limit_bytes=COPY_LIMIT),
        cost_estimate=SMALL_COST,
        name="copy_columns",
    )(info, *[pltpu.with_memory_space_constraint(source, pltpu.HBM) for source in sources])


def halves_kernel(info_ref, both_ref, mine_ref, other_ref, sems):
    copies = [
        pltpu.make_async_copy(both_ref.at[half], to, sems.at[index])
        for index, (half, to) in enumerate(((info_ref[0], mine_ref), (1 - info_ref[0], other_ref)))
    ]
    for copy in copies:
        copy.start()
    for copy in copies:
        copy.wait()


def split_halves(info, both):
    return pl.pallas_call(
        halves_kernel,
        out_shape=[jax.ShapeDtypeStruct(both.shape[1:], both.dtype)] * 2,
        in_specs=[SCALARS, pl.BlockSpec(memory_space=pl.ANY)],
        out_specs=[IN_VMEM] * 2,
        scratch_shapes=[pltpu.SemaphoreType.DMA((2,))],
        compiler_params=pltpu.CompilerParams(vmem_limit_bytes=COPY_LIMIT),
        cost_estimate=SMALL_COST,
        name="split_halves",
    )(info, both)


def local(queries, keys, values, residual, gate, out_weight, time_offsets, guidance_index):
    tiles_time, tiles_wide = time_offsets.shape
    count, features = queries.shape[1:]
    tile = count // tiles_time
    heads = features // HD
    head_count = lax.axis_size("head")
    columns = lax.axis_size("tokens")
    branch_pos = lax.axis_index("branch")
    head_pos = lax.axis_index("head")
    width_pos = lax.axis_index("tokens")
    width = gate.shape[2] // head_count

    rounds = [
        [pair for i in range(first, columns - 1, 2) for pair in ((i, i + 1), (i + 1, i))]
        for first in range(2)
    ]
    near_pos = (width_pos ^ 1, ((width_pos + 1) ^ 1) - 1)

    def swap(value, branch_bit, head_bits):
        if not branch_bit and not head_bits:
            return value
        if not head_bits:
            return lax.ppermute(value, "branch", [(0, 1), (1, 0)])
        if not branch_bit:
            return lax.ppermute(value, "head", [(i, i ^ head_bits) for i in range(head_count)])
        flip = head_count + head_bits
        return lax.ppermute(
            value, ("branch", "head"), [(i, i ^ flip) for i in range(2 * head_count)]
        )

    pair = head_pos >> 1
    branch_pair = branch_pos * (head_count // 2)
    copy_info = jnp.stack([branch_pair + pair, branch_pair + (pair ^ 1)])
    sources = (queries[0], keys[0], values[0], out_weight)
    key_value = [((1, 2), head, HD, (0, 1), (2, count, HD)) for head in range(heads)]
    query = [((0,), head, HD, (None,), (count, HD)) for head in range(heads)]
    pair_weight = [((3,), block, 2 * width, (None,), (features, 2 * width)) for block in (-2, -1)]

    def pack(parts, after=None):
        here = sources
        if after is not None:
            _, here = lax.optimization_barrier((after, sources))
        used = sorted({index for part in parts for index in part[0]})
        plan = [
            (used.index(source), block, cols, len(used) + target, place)
            for target, (froms, block, cols, places, _) in enumerate(parts)
            for source, place in zip(froms, places)
        ]
        return copy_columns(
            copy_info, [here[index] for index in used], plan, [part[-1] for part in parts]
        )

    def split_residual(residual):
        return split_halves(branch_pos[None], jnp.transpose(residual[0], (1, 0, 2)))

    packed = pack(key_value[:1])
    after = packed
    if RESIDUAL_AFTER == 0:
        _, residual = lax.optimization_barrier((packed, residual))
        mine, other = split_residual(residual)
        after = (packed, other) if RESIDUAL_FIRST else packed
    late_key_value, far = pack([key_value[1], pair_weight[1]], after)
    packed = list(packed) + [late_key_value]

    def halo(part):
        return [lax.ppermute(part, "tokens", pairs) for pairs in rounds]

    sides = [halo(part) for part in packed]
    late = pack(query + key_value[2:], sides[0] if LATE_PACK else packed)
    head_queries, packed = list(late[:heads]), packed + list(late[heads:])
    store = {"far": swap(far, 0, 2)}

    if RESIDUAL_AFTER:
        _, residual = lax.optimization_barrier(((packed[1], sides[0])[RESIDUAL_AFTER - 1], residual))
        mine, other = split_residual(residual)
    store["other"] = swap(other, 1, 0)
    offsets = lax.dynamic_index_in_dim(time_offsets, width_pos, 1, keepdims=False)
    edges = jnp.stack([(pos >= 0) & (pos < tiles_wide) for pos in near_pos]).astype(jnp.int32)
    attention_info = jnp.concatenate([offsets, edges])
    place = head_pos & 1
    projection_info = jnp.concatenate([jnp.stack([branch_pos, place, place ^ 1, head_pos]), guidance_index])

    head_queries[0], projection_info = lax.optimization_barrier((head_queries[0], projection_info))
    def relay(head):
        if RELAY[head] == "x":
            store[1, 1, head] = swap(store[0, 1, head], 1, 0)
        elif RELAY[head] == "y":
            store[1, 1, head] = swap(store[1, 0, head], 0, 2)
        else:
            store[1, 1, head] = swap(store[0, 0, head], 1, 2)

    def await_names(names, value):
        value, awaited = lax.optimization_barrier((value, [store[name] for name in names]))
        store.update(zip(names, awaited))
        return value

    for head in range(heads):
        head_queries[head] = await_names(AWAITED.get(head, ()), head_queries[head])
        operands = [head_queries[head], packed[head], *sides[head]]
        if head == heads - 1 and SPLIT:
            own = attention(attention_info, (0, SPLIT), *operands)
            own = await_names(AWAITED.get(heads, ()), own)
            own = attention(attention_info, (SPLIT, tiles_time), *operands, own)
        else:
            own = attention(attention_info, (0, tiles_time), *operands)
        if head + 2 < heads:
            own, part = lax.optimization_barrier((own, packed[head + 2]))
            sides.append(halo(part))
        store[0, 0, head] = own
        store[1, 0, head] = swap(await_names(BEFORE_X.get(head, ()), own), 1, 0)
        store[0, 1, head] = swap(await_names(BEFORE_Y.get(head, ()), own), 0, 2)
        if head < heads - 1:
            relay(head)

    (near,) = pack(pair_weight[:1], store[0, 0, heads - 1])
    names = [name for name in store if isinstance(name, tuple)]
    late = [name for name in names if name[2] == heads - 1 or name in LATE]
    base = (mine, store["other"])

    def partial(names, base):
        return partial_projection(
            projection_info,
            (near, store["far"]),
            {name: store[name] for name in names},
            gate,
            base,
            tile,
            base[0] is mine,
        )

    base = partial([name for name in names if name not in late], base)
    if TIE_PARTIAL:
        name = (1, 0, heads - 1) if RELAY[-1] == "y" else (0, 1, heads - 1)
        base, store[name] = lax.optimization_barrier((base, store[name]))
    if BEFORE_LAST:
        name = (1, 0, heads - 1) if RELAY[-1] == "y" else (0, 1, heads - 1)
        store[name] = await_names(BEFORE_LAST, store[name])
    relay(heads - 1)
    base = partial(late + [(1, 1, heads - 1)], base)
    return (base[0] + swap(base[1], 0, 1).astype(jnp.float32)).astype(jnp.bfloat16)


def solution(mesh):
    return jax.shard_map(
        local,
        mesh=mesh,
        in_specs=(
            P("branch", "tokens", "head"),
            P("branch", "tokens", "head"),
            P("branch", "tokens", "head"),
            P("branch", "tokens", None, "head"),
            P(),
            P("head", None),
            P(),
            P(),
        ),
        out_specs=P("tokens", ("branch", "head")),
        check_vma=False,
    )
```
